512 devices in a mesh: seq: 32 (over z_hi, x, core), dp: 16 (over y, z_lo).
Axes of the slice: x: 4, y: 4, z: 16 (z_hi: 4, z_lo: 4; z = z_hi * 4 + z_lo), core: 2. Of those that a mesh axis runs over, the one named last changes fastest.
Arguments:
- queries: bfloat16 [16384, 2048], P('seq', 'dp'), may hold values from -6 to 6
- keys: bfloat16 [16384, 2048], P('seq', 'dp'), may hold values from -6 to 6
- values: bfloat16 [16384, 2048], P('seq', 'dp'), may hold values from -6 to 6
- out_weight: bfloat16 [2048, 2048], P('seq', 'dp'), may hold values from -2 to 2
- grad_out: bfloat16 [16384, 2048], P('seq', 'dp'), may hold values from -1.5 to 1.5
- pattern: int32 [16, 256, 5], replicated, may hold values from 0 to 255, as said below
Outputs:
- output: bfloat16 [16384, 2048], P('seq', 'dp')
- grad_queries: bfloat16 [16384, 2048], P('seq', 'dp')
- grad_keys: bfloat16 [16384, 2048], P('seq', 'dp')
- grad_values: bfloat16 [16384, 2048], P('seq', 'dp')
The draws below stay inside these ranges and needn't reach their ends.
Inputs may be any that keep to these rules, and one draw needn't show every extreme that they name: pattern[h, b, 0] and pattern[h, b, 1] are the two global key blocks of head h, equal for every b. For each head h and each s, the random entries pattern[h, b, 2:] over the query blocks b = s * 8 to (s + 1) * 8 - 1 name at most 2 blocks in any aligned range of 8 blocks (counting repeats), and exactly 2 in one such range. Entries may repeat one another or a local block.
All inputs are finite; a program needn't handle non-finite values.
Results may differ from the reference program's by a relative error of at most 0.039.
Values may be sent and summed in bfloat16 or wider, within the bound.
A program may use at most 64 MiB of HBM per device.

```python
import jax
import jax.numpy as jnp
from jax import lax

HEADS = 16
HEAD_DIM = 128
D = 2048
BLOCK = 64
NSEL = 5
SEQ_LEN = 16384
NBLK = 256
QBLK = 8
CAP = 2


def joint_fields(key):
    base = jax.random.fold_in(key, 1234)
    query_key, key_key = jax.random.split(base, 2)
    field_shape = (SEQ_LEN, D)
    query_field = jnp.clip(1.22 * jax.random.normal(query_key, field_shape, jnp.float32), -6.0, 6.0)
    key_field = jnp.clip(1.22 * jax.random.normal(key_key, field_shape, jnp.float32), -6.0, 6.0)
    return (query_field, key_field)


def draw_queries(key, part):
    return joint_fields(key)[0].astype(jnp.bfloat16)


def draw_keys(key, part):
    return joint_fields(key)[1].astype(jnp.bfloat16)


def draw_pattern(key, part):
    base = jax.random.fold_in(key, 77)
    global_key, random_key = jax.random.split(base, 2)
    owner_count = NBLK // QBLK
    entry_count = QBLK * (NSEL - 2)
    slot_total = owner_count * CAP
    global_blocks = jax.random.randint(global_key, (HEADS, 1, 2), 0, NBLK, dtype=jnp.int32)

    def group_draw(head, shard):
        group_key = jax.random.fold_in(jax.random.fold_in(random_key, head), shard)
        first_key, order_key, offset_key, shuffle_key = jax.random.split(group_key, 4)
        first_top = (head == 0) & (shard == 0)
        first_low = (head == 0) & (shard == 1)
        forced = jax.random.randint(first_key, (), 0, owner_count, dtype=jnp.int32)
        forced = jnp.where(first_top, owner_count - 1, jnp.where(first_low, 0, forced))
        slot_owner = jnp.arange(slot_total, dtype=jnp.int32) // CAP
        order = jax.random.permutation(order_key, slot_total).astype(jnp.int32)
        ranked = jnp.where(slot_owner == forced, slot_total + jnp.arange(slot_total, dtype=jnp.int32), order)
        sorted_slots = jnp.argsort(ranked, stable=True)
        others = slot_owner[sorted_slots][:entry_count - CAP]
        owners = jnp.concatenate([jnp.full((CAP,), forced, jnp.int32), others])
        is_forced = jnp.arange(entry_count, dtype=jnp.int32) < CAP
        offsets = jax.random.randint(offset_key, (entry_count,), 0, QBLK, dtype=jnp.int32)
        offsets = jnp.where(is_forced & first_top, QBLK - 1, offsets)
        offsets = jnp.where(is_forced & first_low, 0, offsets)
        blocks = owners * QBLK + offsets
        shuffle = jax.random.permutation(shuffle_key, entry_count)
        return blocks[shuffle].reshape(QBLK, NSEL - 2)
    head_ids = jnp.arange(HEADS, dtype=jnp.int32)
    shard_ids = jnp.arange(owner_count, dtype=jnp.int32)
    random_blocks = jax.vmap(jax.vmap(group_draw, (None, 0)), (0, None))(head_ids, shard_ids)
    random_blocks = random_blocks.reshape(HEADS, NBLK, NSEL - 2)
    global_rows = jnp.broadcast_to(global_blocks, (HEADS, NBLK, 2))
    return jnp.concatenate([global_rows, random_blocks], axis=2).astype(jnp.int32)


def level_of(rng, extent, cuts, smallest, high):
    factor_of, own = 1.0, jax.random.fold_in(rng, 6)
    for axis_at, shards_of in cuts:
        heights = jnp.exp(jax.random.uniform(jax.random.fold_in(own, axis_at), (shards_of,), jnp.float32, smallest / len(cuts), high / len(cuts)))
        factor_of = factor_of * jnp.repeat(heights, extent[axis_at] // shards_of).reshape([-1 if axis == axis_at else 1 for axis in range(len(extent))])
    return factor_of


def centred(stream_key, extent, width, reach, pieces=(), kind=jnp.bfloat16):
    drawn = width * jax.random.normal(stream_key, extent, jnp.float32)
    if pieces:
        drawn = drawn * level_of(stream_key, extent, pieces, -0.22, 0.18)
    return jnp.clip(drawn, -reach, reach).astype(kind)


def setup_inputs(seed: int = 0) -> dict:
    arg_keys = jax.random.split(jax.random.key(seed), 7)
    return {
        "queries": draw_queries(jax.random.fold_in(arg_keys[6], 71), 0),
        "keys": draw_keys(jax.random.fold_in(arg_keys[6], 71), 0),
        "values": centred(arg_keys[2], (SEQ_LEN, D), 1.0, 6.0, ((0, 32), (1, 16))),
        "out_weight": centred(arg_keys[3], (D, D), (D // 256) ** -0.5, 2.0, ((0, 32), (1, 16))),
        "grad_out": centred(arg_keys[4], (SEQ_LEN, D), 0.25, 1.5, ((0, 32), (1, 16))),
        "pattern": draw_pattern(jax.random.fold_in(arg_keys[6], 71), 0),
    }


def head_pass(query_rows, key_rows, value_rows, grad_rows, index_rows):
    block_count = query_rows.shape[0] // BLOCK
    attention_scaling = HEAD_DIM ** -0.5
    query_block_list = query_rows.reshape(block_count, BLOCK, HEAD_DIM).astype(jnp.float32)
    key_block_tiles = key_rows.reshape(block_count, BLOCK, HEAD_DIM)[index_rows]
    key_block_tiles = key_block_tiles.reshape(block_count, -1, HEAD_DIM).astype(jnp.float32)
    value_block_tiles = value_rows.reshape(block_count, BLOCK, HEAD_DIM)[index_rows]
    value_block_tiles = value_block_tiles.reshape(block_count, -1, HEAD_DIM).astype(jnp.float32)
    logit_scores = jnp.einsum("rjy,rly->rjl", query_block_list, key_block_tiles) * attention_scaling
    maxima = jnp.max(logit_scores, axis=-1, keepdims=True)
    exp_scores = jnp.exp(logit_scores - maxima)
    probs_full = exp_scores / jnp.sum(exp_scores, axis=-1, keepdims=True)
    probabilities_reduced = lax.optimization_barrier(probs_full.astype(jnp.bfloat16)).astype(jnp.float32)
    context_output = jnp.einsum("xvy,xyj->xvj", probabilities_reduced, value_block_tiles).astype(jnp.bfloat16)
    gradient_blockwise = grad_rows.reshape(block_count, BLOCK, HEAD_DIM).astype(jnp.float32)
    gradient_probabilities = jnp.einsum("rjy,rly->rjl", gradient_blockwise, value_block_tiles)
    delta_sum = jnp.sum(gradient_blockwise * context_output.astype(jnp.float32), axis=-1, keepdims=True)
    score_gradient = probs_full * (gradient_probabilities - delta_sum)
    score_gradient = lax.optimization_barrier(score_gradient.astype(jnp.bfloat16)).astype(jnp.float32)
    query_gradient = (jnp.einsum("xvy,xyj->xvj", score_gradient, key_block_tiles) * attention_scaling).astype(jnp.bfloat16)
    key_contributions = jnp.einsum("vxu,vxs->vus", score_gradient, query_block_list) * attention_scaling
    value_contributions = jnp.einsum("vxu,vxs->vus", probabilities_reduced, gradient_blockwise)
    flat_index = index_rows.reshape(-1)
    empty = jnp.zeros((block_count, BLOCK, HEAD_DIM), jnp.float32)
    grad_key = empty.at[flat_index].add(key_contributions.reshape(-1, BLOCK, HEAD_DIM))
    grad_value = empty.at[flat_index].add(value_contributions.reshape(-1, BLOCK, HEAD_DIM))
    seq_total = block_count * BLOCK
    return (context_output.reshape(seq_total, HEAD_DIM), query_gradient.reshape(seq_total, HEAD_DIM),
            grad_key.astype(jnp.bfloat16).reshape(seq_total, HEAD_DIM),
            grad_value.astype(jnp.bfloat16).reshape(seq_total, HEAD_DIM))


def reference(queries, keys, values, out_weight, grad_out, pattern):
    block_count = SEQ_LEN // BLOCK
    starts = jnp.arange(block_count, dtype=jnp.int32)
    offsets = jnp.array([-1, 0, 1], dtype=jnp.int32)
    local = (starts[:, None] + offsets[None, :]) % block_count
    local = jnp.broadcast_to(local[None], (HEADS, block_count, 3)).astype(jnp.int32)
    index_all = jnp.concatenate([local, pattern.astype(jnp.int32)], axis=2)

    def split_heads(rows):
        return rows.reshape(SEQ_LEN, HEADS, HEAD_DIM).transpose(1, 0, 2)

    def merge_heads(rows):
        return rows.transpose(1, 0, 2).reshape(SEQ_LEN, D)

    grad_context = jnp.dot(grad_out, out_weight.T, preferred_element_type=jnp.float32).astype(jnp.bfloat16)
    results = lax.map(lambda group: head_pass(*group),
                      (split_heads(queries), split_heads(keys), split_heads(values),
                       split_heads(grad_context), index_all))
    context_output = merge_heads(results[0])
    output = jnp.dot(context_output, out_weight, preferred_element_type=jnp.float32).astype(jnp.bfloat16)
    return (output, merge_heads(results[1]), merge_heads(results[2]), merge_heads(results[3]))
```

```python
import functools

import jax
import jax.numpy as jnp
from jax import lax
from jax.experimental import pallas as pl
from jax.experimental.pallas import tpu as pltpu
from jax.sharding import PartitionSpec as P

HEAD_DIM = 128
BLOCK = 64
SCALE = HEAD_DIM**-0.5
CAP = 2
VMEM_LIMIT = 48 * 1024 * 1024
MESH = pl.DeviceIdType.MESH
f32 = jnp.float32
bf16 = jnp.bfloat16


class Place:
    def __init__(self, dims):
        self.Z, self.P, self.Y, self.L = dims
        seq, dp = lax.axis_index("seq"), lax.axis_index("dp")
        self.seq, self.dp = seq, dp
        self.z, self.p = seq // self.P, seq % self.P
        self.y, self.l = dp // self.L, dp % self.L

    def at_z(self, j):
        return {"seq": (self.z + j) % self.Z * self.P + self.p, "dp": self.dp}

    def at_p(self, j):
        return {"seq": self.z * self.P + (self.p + j) % self.P, "dp": self.dp}

    def at_y(self, j):
        return {"seq": self.seq, "dp": (self.y + j) % self.Y * self.L + self.l}

    def at_l(self, j):
        return {"seq": self.seq, "dp": self.y * self.L + (self.l + j) % self.L}

    def at_s(self, j):
        return {"seq": (self.seq + j) % (self.Z * self.P), "dp": self.dp}

    def enter(self):
        partners = (
            [self.at_p(j) for j in range(1, self.P)]
            + [self.at_z(j) for j in range(1, self.Z)]
            + [self.at_y(j) for j in range(1, self.Y)]
            + [self.at_l(j) for j in range(1, self.L)]
            + [self.at_s(1), self.at_s(-1)]
        )
        barrier = pltpu.get_barrier_semaphore()
        for partner in partners:
            pl.semaphore_signal(barrier, inc=1, device_id=partner, device_id_type=MESH)
        pl.semaphore_wait(barrier, len(partners))


class Wire:
    def __init__(self, send_sems, recv_sems):
        self.send_sems, self.recv_sems = send_sems, recv_sems
        self.used = 0
        self.sent = []

    def send(self, src, dst, target):
        copy = pltpu.make_async_remote_copy(
            src_ref=src,
            dst_ref=dst,
            send_sem=self.send_sems.at[self.used],
            recv_sem=self.recv_sems.at[self.used],
            device_id=target,
            device_id_type=MESH,
        )
        self.used += 1
        copy.start()
        self.sent.append(copy)
        return copy

    def finish(self):
        for copy in self.sent:
            copy.wait_send()


def gather_kernel(
    dims, k, v, w, go, pick, gpick, gowner,
    halo, glob, rnd, wall, gctx,
    kvm, kvp, kv2, kblk, vblk, sb0, sb1, sb2, sb3, edge,
    gcand, ga, gmine, gb, gpiece, wcol, ps, pr, ysum, lr, send_sems, recv_sems,
):
    me = Place(dims)
    Z, PN, Y, L = dims
    wire = Wire(send_sems, recv_sems)
    blocks = k.shape[0] // BLOCK
    half = go.shape[0] // 2
    piece = glob.shape[1]

    kblk[...] = k[...].reshape(blocks, BLOCK, HEAD_DIM)
    vblk[...] = v[...].reshape(blocks, BLOCK, HEAD_DIM)
    edge[0, 0] = kblk[blocks - 1]
    edge[0, 1] = vblk[blocks - 1]
    edge[1, 0] = kblk[0]
    edge[1, 1] = vblk[0]
    for j in range(2):
        at = gpick[j]
        for part, source in ((0, kblk), (1, vblk)):
            rows = source[at].reshape(BLOCK // piece, piece, HEAD_DIM)
            first = (j * 2 + part) * (BLOCK // piece)
            gcand[first : first + BLOCK // piece] = rows
    me.enter()

    w_z = [wire.send(w, wcol.at[me.z], me.at_z(j)) for j in range(1, Z)]
    edges = [
        wire.send(edge.at[0], halo.at[0], me.at_s(1)),
        wire.send(edge.at[1], halo.at[1], me.at_s(-1)),
    ]
    g_a = [
        wire.send(gcand.at[(me.p + j) % PN], ga.at[me.p], me.at_p(j)) for j in range(1, PN)
    ]
    k_up = wire.send(kblk, kvm.at[0], me.at_z(1))
    v_down = wire.send(vblk, kvp.at[1], me.at_z(-1))
    v_up = wire.send(vblk, kvm.at[1], me.at_z(1))
    k_down = wire.send(kblk, kvp.at[0], me.at_z(-1))

    arrivals = []

    def pack(at, keys, values, buffer):
        for requester in range(PN):
            for c in range(CAP):
                block = pick[(at * PN + requester) * CAP + c]
                buffer[requester, c, 0] = keys(block)
                buffer[requester, c, 1] = values(block)
        rnd[at, pl.ds(me.p, 1)] = buffer[pl.ds(me.p, 1)]
        for j in range(1, PN):
            arrivals.append(
                wire.send(buffer.at[(me.p + j) % PN], rnd.at[at, me.p], me.at_p(j))
            )

    wcol[pl.ds(me.z, 1)] = w[...][None]
    ga[pl.ds(me.p, 1)] = gcand[pl.ds(me.p, 1)]
    for copy in w_z:
        copy.wait_recv()
    wall[:, pl.ds(me.p, 1)] = wcol[...][:, None]
    w_p = [wire.send(wcol, wall.at[:, me.p], me.at_p(j)) for j in range(1, PN)]

    for copy in g_a:
        copy.wait_recv()
    half_pieces = PN // 2
    own_half = (me.p // half_pieces) % 2
    owner_p = jnp.where(own_half == 0, gowner[0], gowner[1])
    gmine[...] = ga[owner_p]
    g_b = [wire.send(gmine, gb.at[j], me.at_z(j)) for j in range(1, Z)]

    pack(0, lambda b: kblk[b], lambda b: vblk[b], sb0)

    for copy in w_p:
        copy.wait_recv()
    chunk_z = Z // Y
    width = L * HEAD_DIM
    y_sends = []
    for part in range(2):
        rows = go[part * half : (part + 1) * half]
        for j in list(range(1, Y)) + [0]:
            to = (me.y + j) % Y
            weight = wall[pl.ds(to * chunk_z, chunk_z)].reshape(width, HEAD_DIM)
            terms = lax.dot_general(
                rows, weight, (((1,), (1,)), ((), ())), preferred_element_type=f32
            ).astype(bf16)
            for head in range(L):
                ps[part, j, head] = terms[:, head * HEAD_DIM : (head + 1) * HEAD_DIM]
            if j:
                y_sends.append(wire.send(ps.at[part, j], pr.at[part, j - 1], me.at_y(j)))

    for copy in g_b:
        copy.wait_recv()
    owner_z = jnp.where(own_half == 0, gowner[2], gowner[3])
    gb[0] = gmine[...]
    gpiece[...] = gb[owner_z]
    glob[pl.ds(me.p, 1)] = gpiece[...][None]
    g_c = [wire.send(gpiece, glob.at[me.p], me.at_p(j)) for j in range(1, PN)]

    k_up.wait_recv()
    k_far = wire.send(kvm.at[0], kv2.at[0], me.at_z(1))
    v_down.wait_recv()
    v_far = wire.send(kvp.at[1], kv2.at[1], me.at_z(-1))

    def y_stage(part):
        for copy in y_sends[part * (Y - 1) : (part + 1) * (Y - 1)]:
            copy.wait_recv()
        for head in range(L):
            total = ps[part, 0, head].astype(f32)
            for j in range(1, Y):
                total = total + pr[part, j - 1, head].astype(f32)
            ysum[part, head] = total.astype(bf16)
        return [
            wire.send(ysum.at[part, (me.l + j) % L], lr.at[part, j - 1], me.at_l(j))
            for j in range(1, L)
        ]

    v_up.wait_recv()
    pack(1, lambda b: kvm[0, b], lambda b: kvm[1, b], sb1)
    k_down.wait_recv()
    pack(2, lambda b: kvp[0, b], lambda b: kvp[1, b], sb2)
    l_sends = [y_stage(0), y_stage(1)]
    k_far.wait_recv()
    v_far.wait_recv()
    pack(3, lambda b: kv2[0, b], lambda b: kv2[1, b], sb3)
    for part in range(2):
        for copy in l_sends[part]:
            copy.wait_recv()
        total = ysum[part, pl.ds(me.l, 1)][0].astype(f32)
        for j in range(1, L):
            total = total + lr[part, j - 1].astype(f32)
        gctx[part * half : (part + 1) * half] = total.astype(bf16)
    for copy in edges + g_c + arrivals:
        copy.wait_recv()
    wire.finish()


def attend_kernel(
    q, k, v, halo, glob, rnd, gctx, slot_of, entry_of,
    ctx, dq, sb, own, edge, gsum,
    fr,
):
    blocks = q.shape[0] // BLOCK
    entries = 3 * blocks

    def window(b, part, source):
        before = halo[0, part] if b == 0 else source[(b - 1) * BLOCK : b * BLOCK]
        after = halo[1, part] if b == blocks - 1 else source[(b + 1) * BLOCK : (b + 2) * BLOCK]
        return [before, source[b * BLOCK : (b + 1) * BLOCK], after]

    def dot(a, b, dims):
        return lax.dot_general(a, b, (dims, ((), ())), preferred_element_type=f32)

    nt, nn, tn = ((1,), (1,)), ((1,), (0,)), ((0,), (0,))
    gk = [glob[0], glob[2]]
    gv = [glob[1], glob[3]]
    acc = {}
    total = [jnp.zeros((2 * BLOCK, HEAD_DIM), f32) for _ in range(2)]

    def settle(at):
        for part in range(2):
            term = acc.pop((at, part))
            if at < 0:
                edge[0, part] = term.astype(bf16)
            elif at >= blocks:
                edge[1, part] = term.astype(bf16)
            else:
                own[part, at] = term

    fr[entries] = jnp.zeros(fr.shape[1:], bf16)
    for b in range(blocks):
        rows = slice(b * BLOCK, (b + 1) * BLOCK)
        slots = [slot_of[b * 3 + i] for i in range(3)]
        keys = jnp.concatenate(window(b, 0, k) + gk + [rnd[s, 0] for s in slots], axis=0)
        values = jnp.concatenate(window(b, 1, v) + gv + [rnd[s, 1] for s in slots], axis=0)
        qb, gb = q[rows], gctx[rows]
        scores = dot(qb, keys, nt) * SCALE
        top = jnp.max(scores, axis=-1, keepdims=True)
        raised = jnp.exp(scores - top)
        probs32 = raised / jnp.sum(raised, axis=-1, keepdims=True)
        probs = probs32.astype(bf16)
        context = dot(probs, values, nn).astype(bf16)
        ctx[rows] = context
        delta = jnp.sum(gb.astype(f32) * context.astype(f32), axis=-1, keepdims=True)
        gprobs = dot(gb, values, nt)
        gscores = (probs32 * (gprobs - delta)).astype(bf16)
        dq[rows] = (dot(gscores, keys, nn) * SCALE).astype(bf16)
        for part, term in (
            (0, dot(gscores, qb, tn) * SCALE),
            (1, dot(probs, gb, tn)),
        ):
            for i in range(3):
                at = (b - 1 + i, part)
                piece = term[i * BLOCK : (i + 1) * BLOCK]
                acc[at] = acc[at] + piece if at in acc else piece
            total[part] = total[part] + term[3 * BLOCK : 5 * BLOCK]
            for i in range(3):
                fr[b * 3 + i, part] = term[(5 + i) * BLOCK : (6 + i) * BLOCK].astype(bf16)
        settle(b - 1)
    settle(blocks - 1)
    settle(blocks)
    for j in range(2):
        for part in range(2):
            gsum[j * 2 + part] = total[part][j * BLOCK : (j + 1) * BLOCK].astype(bf16)
    for slot in range(sb.shape[0]):
        sb[slot] = fr[entry_of[slot]]


def scatter_kernel(
    dims, ctx, wall, sb, own, edge, gsum, pickx, ghit,
    out, dk, dv,
    halo, ar0, ar1, ar2, ar3, p1, p2, p3, fm, fp, rm, rp,
    ga, gmine, gb, gpiece, gall, cr, send_sems, recv_sems,
):
    me = Place(dims)
    Z, PN, Y, L = dims
    wire = Wire(send_sems, recv_sems)
    blocks = own.shape[1]
    me.enter()

    order = (3, 1, 2, 0)
    landing = {0: ar0, 1: ar1, 2: ar2, 3: ar3}
    arrivals = {}

    def spread(at):
        arrivals[at] = [
            wire.send(sb.at[at, (me.p + j) % PN], landing[at].at[me.p], me.at_p(j))
            for j in range(1, PN)
        ]

    spread(3)
    g_a = [
        wire.send(gsum.at[(me.p + j) % PN], ga.at[me.p], me.at_p(j)) for j in range(1, PN)
    ]
    cr[pl.ds(me.y, 1), pl.ds(me.l, 1)] = ctx[...][None, None]
    l_in = [
        wire.send(ctx, cr.at[me.y, me.l], me.at_l(j)) for j in range(1, L)
    ]
    y_in = [wire.send(ctx, cr.at[me.y, me.l], me.at_y(j)) for j in range(1, Y)]
    edges = [
        wire.send(edge.at[0], halo.at[1], me.at_s(-1)),
        wire.send(edge.at[1], halo.at[0], me.at_s(1)),
    ]
    for at in order[1:]:
        spread(at)

    def gather_sum(at):
        landed = landing[at]
        landed[pl.ds(me.p, 1)] = sb[at, pl.ds(me.p, 1)]
        for copy in arrivals[at]:
            copy.wait_recv()
        rows, cols = blocks * 16, PN * CAP * 16
        row = lax.broadcasted_iota(jnp.int32, (rows, cols), 0)
        col = lax.broadcasted_iota(jnp.int32, (rows, cols), 1)
        wanted = jnp.broadcast_to(pickx[at : at + 1], (rows, cols))
        here = (wanted == row // 16) & (row % 16 == col % 16)
        select = jnp.where(here, 1.0, 0.0).astype(bf16)
        sums = []
        for part in range(2):
            pieces = []
            for r in range(BLOCK // 16):
                data = landed[:, :, part, r * 16 : (r + 1) * 16].reshape(cols, HEAD_DIM)
                pieces.append(
                    jnp.dot(select, data, preferred_element_type=f32).reshape(
                        blocks, 16, HEAD_DIM
                    )
                )
            sums.append(jnp.concatenate(pieces, axis=1))
        return sums

    far = gather_sum(3)
    p2[0] = far[0].astype(bf16)
    p2[1] = far[1].astype(bf16)
    far_up = wire.send(p2.at[0], fm, me.at_z(1))
    far_down = wire.send(p2.at[1], fp, me.at_z(-1))

    for copy in g_a:
        copy.wait_recv()
    ga[pl.ds(me.p, 1)] = gsum[pl.ds(me.p, 1)]
    gmine[...] = jnp.sum(ga[...].astype(f32), axis=0).astype(bf16)
    g_b = [wire.send(gmine, gb.at[j - 1], me.at_z(j)) for j in range(1, Z)]

    down = gather_sum(1)
    p3[0] = down[0].astype(bf16)
    k_down = wire.send(p3.at[0], rp.at[0], me.at_z(-1))
    up = gather_sum(2)
    p1[1] = up[1].astype(bf16)
    v_up = wire.send(p1.at[1], rm.at[1], me.at_z(1))
    for j in range(1, L):
        l_in[j - 1].wait_recv()
        source = (me.l + L - j) % L
        for i in range(1, Y):
            y_in.append(wire.send(cr.at[me.y, source], cr.at[me.y, source], me.at_y(i)))
    far_up.wait_recv()
    p1[0] = (up[0] + fm[...].astype(f32)).astype(bf16)
    k_up = wire.send(p1.at[0], rm.at[0], me.at_z(1))
    far_down.wait_recv()
    p3[1] = (down[1] + fp[...].astype(f32)).astype(bf16)
    v_down = wire.send(p3.at[1], rp.at[1], me.at_z(-1))

    for copy in g_b:
        copy.wait_recv()
    gpiece[...] = (
        gmine[...].astype(f32) + jnp.sum(gb[...].astype(f32), axis=0)
    ).astype(bf16)
    gall[pl.ds(me.p, 1)] = gpiece[...][None]
    g_c = [wire.send(gpiece, gall.at[me.p], me.at_p(j)) for j in range(1, PN)]

    totals = gather_sum(0)
    for copy in y_in:
        copy.wait_recv()
    result = jnp.zeros(out.shape, f32)
    heads_z = Y * L // Z
    for y in range(Y):
        for l in range(L):
            head = y * L + l
            weight = wall[head * HEAD_DIM : (head + 1) * HEAD_DIM]
            result = result + jnp.dot(cr[y, l], weight, preferred_element_type=f32)
    out[...] = result.astype(bf16)

    for copy in edges + g_c:
        copy.wait_recv()
    k_down.wait_recv()
    v_up.wait_recv()
    k_up.wait_recv()
    v_down.wait_recv()
    everyone = gall[...].reshape(2, 2, BLOCK, HEAD_DIM).astype(f32)
    for part, target in ((0, dk), (1, dv)):
        total = totals[part] + own[part]
        total = total + (rm[part].astype(f32) + rp[part].astype(f32))
        for b in range(blocks):
            one = total[b]
            for j in range(2):
                hit = ghit[j] == b
                one = one + jnp.where(hit, everyone[j, part], 0.0)
            if b == 0:
                one = one + halo[0, part].astype(f32)
            if b == blocks - 1:
                one = one + halo[1, part].astype(f32)
            target[b * BLOCK : (b + 1) * BLOCK] = one.astype(bf16)
    wire.finish()


def plan(dims, pattern, blocks):
    me = Place(dims)
    Z, PN, Y, L = dims
    seqs = Z * PN
    head = lax.dynamic_slice_in_dim(pattern, me.dp, 1, 0)[0]
    shared = head[0, :2]
    entries = 3 * blocks
    mine = lax.dynamic_slice_in_dim(head, me.z * PN * blocks, PN * blocks, 0)
    wanted = mine[:, 2:].reshape(PN, entries)
    owner = wanted // blocks
    e = jnp.arange(entries, dtype=jnp.int32)
    same = owner[:, :, None] == owner[:, None, :]
    rank = jnp.sum((same & (e[None, :] < e[:, None])).astype(jnp.int32), axis=-1)
    rel = jnp.array([0, Z - 1, 1, 2], jnp.int32)
    places = (me.z + rel) % Z
    c = jnp.arange(CAP, dtype=jnp.int32)
    column = places * PN + me.p
    hit = (owner[None, :, None, :] == column[:, None, None, None]) & (
        rank[None, :, None, :] == c[None, None, :, None]
    )
    pick = jnp.sum(jnp.where(hit, wanted[None, :, None, :] % blocks + 1, 0), axis=-1) - 1
    my_owner = lax.dynamic_slice_in_dim(owner, me.p, 1, 0)[0]
    my_rank = lax.dynamic_slice_in_dim(rank, me.p, 1, 0)[0]
    back = (my_owner // PN - me.z) % Z
    order_of = jnp.where(back == 0, 0, jnp.where(back == 1, 2, jnp.where(back == 2, 3, 1)))
    slot_of = (order_of * PN + my_owner % PN) * CAP + my_rank
    slots = jnp.arange(4 * PN * CAP, dtype=jnp.int32)
    entry_of = entries - jnp.sum(
        jnp.where(slot_of[None, :] == slots[:, None], entries - e[None, :], 0), axis=-1
    )
    g_seq = shared // blocks
    g_owner = jnp.concatenate([g_seq % PN, (me.z - g_seq // PN) % Z])
    ghit = jnp.where(g_seq == me.seq, shared % blocks, -1)
    return pick, slot_of, entry_of, shared % blocks, g_owner, ghit


def vmem():
    return pl.BlockSpec(memory_space=pltpu.VMEM)


def smem():
    return pl.BlockSpec(memory_space=pltpu.SMEM)


def per_device(dims, queries, keys, values, out_weight, grad_out, pattern):
    Z, PN, Y, L = dims
    tokens = queries.shape[0]
    blocks = tokens // BLOCK
    rows = out_weight.shape[0]
    piece = 4 * BLOCK // PN
    block = (BLOCK, HEAD_DIM)
    pair = (2,) + block
    half = tokens // 2
    shape = jax.ShapeDtypeStruct
    pick, slot_of, entry_of, g_pick, g_owner, ghit = plan(dims, pattern, blocks)

    gather_sems = 3 + 2 + 7 + 4 + 7 * 4 + 7 + 3 + 6 + 7 + 2 + 6 + 8
    halo, glob, rnd, wall, gctx = pl.pallas_call(
        functools.partial(gather_kernel, dims),
        out_shape=(
            shape((2,) + pair, bf16),
            shape((PN, piece, HEAD_DIM), bf16),
            shape((4, PN, CAP) + pair, bf16),
            shape((Z, PN, rows, HEAD_DIM), bf16),
            shape((tokens, HEAD_DIM), bf16),
        ),
        in_specs=[vmem()] * 4 + [smem()] * 3,
        out_specs=(vmem(),) * 5,
        scratch_shapes=[
            pltpu.VMEM((2, blocks) + block, bf16),
            pltpu.VMEM((2, blocks) + block, bf16),
            pltpu.VMEM((2, blocks) + block, bf16),
            pltpu.VMEM((blocks,) + block, bf16),
            pltpu.VMEM((blocks,) + block, bf16),
            pltpu.VMEM((PN, CAP) + pair, bf16),
            pltpu.VMEM((PN, CAP) + pair, bf16),
            pltpu.VMEM((PN, CAP) + pair, bf16),
            pltpu.VMEM((PN, CAP) + pair, bf16),
            pltpu.VMEM((2,) + pair, bf16),
            pltpu.VMEM((PN, piece, HEAD_DIM), bf16),
            pltpu.VMEM((PN, piece, HEAD_DIM), bf16),
            pltpu.VMEM((piece, HEAD_DIM), bf16),
            pltpu.VMEM((Z, piece, HEAD_DIM), bf16),
            pltpu.VMEM((piece, HEAD_DIM), bf16),
            pltpu.VMEM((Z, rows, HEAD_DIM), bf16),
            pltpu.VMEM((2, Y, L, half, HEAD_DIM), bf16),
            pltpu.VMEM((2, Y - 1, L, half, HEAD_DIM), bf16),
            pltpu.VMEM((2, L, half, HEAD_DIM), bf16),
            pltpu.VMEM((2, L - 1, half, HEAD_DIM), bf16),
            pltpu.SemaphoreType.DMA((gather_sems,)),
            pltpu.SemaphoreType.DMA((gather_sems,)),
        ],
        compiler_params=pltpu.CompilerParams(
            collective_id=0, has_side_effects=True, vmem_limit_bytes=VMEM_LIMIT
        ),
    )(keys, values, out_weight, grad_out, jnp.maximum(pick, 0).reshape(-1), g_pick, g_owner)

    slots = 4 * PN * CAP
    ctx, dq, sb, own, edge, gsum = pl.pallas_call(
        attend_kernel,
        out_shape=(
            shape((tokens, HEAD_DIM), bf16),
            shape((tokens, HEAD_DIM), bf16),
            shape((slots,) + pair, bf16),
            shape((2, blocks) + block, f32),
            shape((2,) + pair, bf16),
            shape((4,) + block, bf16),
        ),
        in_specs=[vmem()] * 7 + [smem()] * 2,
        out_specs=(vmem(),) * 6,
        scratch_shapes=[pltpu.VMEM((3 * blocks + 1,) + pair, bf16)],
        compiler_params=pltpu.CompilerParams(vmem_limit_bytes=VMEM_LIMIT),
    )(
        queries, keys, values, halo, glob.reshape((4,) + block),
        rnd.reshape((slots,) + pair), gctx, slot_of, entry_of,
    )

    scatter_sems = 7 * 4 + 7 + 3 + 12 + 2 + 2 + 3 + 4 + 7 + 8
    landing = pltpu.VMEM((PN, CAP) + pair, bf16)
    half_sum = pltpu.VMEM((blocks,) + block, bf16)
    whole_sum = pltpu.VMEM((2, blocks) + block, bf16)
    out, dk, dv = pl.pallas_call(
        functools.partial(scatter_kernel, dims),
        out_shape=(shape((tokens, HEAD_DIM), bf16),) * 3,
        in_specs=[vmem()] * 7 + [smem()],
        out_specs=(vmem(),) * 3,
        scratch_shapes=[
            pltpu.VMEM((2,) + pair, bf16),
            landing, landing, landing, landing,
            whole_sum, whole_sum, whole_sum, half_sum, half_sum, whole_sum, whole_sum,
            pltpu.VMEM((PN, piece, HEAD_DIM), bf16),
            pltpu.VMEM((piece, HEAD_DIM), bf16),
            pltpu.VMEM((Z - 1, piece, HEAD_DIM), bf16),
            pltpu.VMEM((piece, HEAD_DIM), bf16),
            pltpu.VMEM((PN, piece, HEAD_DIM), bf16),
            pltpu.VMEM((Y, L, tokens, HEAD_DIM), bf16),
            pltpu.SemaphoreType.DMA((scatter_sems,)),
            pltpu.SemaphoreType.DMA((scatter_sems,)),
        ],
        compiler_params=pltpu.CompilerParams(
            collective_id=1, has_side_effects=True, vmem_limit_bytes=VMEM_LIMIT
        ),
    )(
        ctx, wall.reshape(-1, HEAD_DIM), sb.reshape((4, PN, CAP) + pair), own, edge,
        gsum.reshape(PN, piece, HEAD_DIM), jnp.repeat(pick.reshape(4, PN * CAP), 16, axis=1),
        ghit,
    )
    return out, dq, dk, dv


def solution(mesh, planes=8, lines=4):
    seq, dp = mesh.shape["seq"], mesh.shape["dp"]
    dims = (seq // planes, planes, dp // lines, lines)
    tile = P("seq", "dp")
    return jax.shard_map(
        functools.partial(per_device, dims),
        mesh=mesh,
        in_specs=(tile,) * 5 + (P(),),
        out_specs=(tile,) * 4,
        check_vma=False,
    )
```

```python
import functools

import jax
import jax.numpy as jnp
from jax import lax
from jax.experimental import pallas as pl
from jax.experimental.pallas import tpu as pltpu
from jax.sharding import PartitionSpec as P

HEAD_DIM = 128
BLOCK = 64
SCALE = HEAD_DIM**-0.5
CAP = 2
VMEM_LIMIT = 48 * 1024 * 1024
MESH = pl.DeviceIdType.MESH
f32 = jnp.float32
bf16 = jnp.bfloat16


class Place:
    def __init__(self, dims):
        self.Z, self.P, self.Y, self.L = dims
        seq, dp = lax.axis_index("seq"), lax.axis_index("dp")
        self.seq, self.dp = seq, dp
        self.z, self.p = seq // self.P, seq % self.P
        self.y, self.l = dp // self.L, dp % self.L

    def at_z(self, j):
        return {"seq": (self.z + j) % self.Z * self.P + self.p, "dp": self.dp}

    def at_p(self, j):
        return {"seq": self.z * self.P + (self.p + j) % self.P, "dp": self.dp}

    def at_y(self, j):
        return {"seq": self.seq, "dp": (self.y + j) % self.Y * self.L + self.l}

    def at_l(self, j):
        return {"seq": self.seq, "dp": self.y * self.L + (self.l + j) % self.L}

    def at_s(self, j):
        return {"seq": (self.seq + j) % (self.Z * self.P), "dp": self.dp}

    def enter(self, extra=()):
        partners = (
            [self.at_p(j) for j in range(1, self.P)]
            + [self.at_z(j) for j in range(1, self.Z)]
            + [self.at_y(j) for j in range(1, self.Y)]
            + [self.at_l(j) for j in range(1, self.L)]
            + [self.at_s(1), self.at_s(-1)]
        )
        partners += list(extra)
        barrier = pltpu.get_barrier_semaphore()
        for partner in partners:
            pl.semaphore_signal(barrier, inc=1, device_id=partner, device_id_type=MESH)
        pl.semaphore_wait(barrier, len(partners))


class Wire:
    def __init__(self, send_sems, recv_sems):
        self.send_sems, self.recv_sems = send_sems, recv_sems
        self.used = 0
        self.sent = []

    def send(self, src, dst, target):
        copy = pltpu.make_async_remote_copy(
            src_ref=src,
            dst_ref=dst,
            send_sem=self.send_sems.at[self.used],
            recv_sem=self.recv_sems.at[self.used],
            device_id=target,
            device_id_type=MESH,
        )
        self.used += 1
        copy.start()
        self.sent.append(copy)
        return copy

    def done(self, *copies):
        self.sent = [copy for copy in self.sent if not any(copy is c for c in copies)]

    def finish(self):
        for copy in self.sent:
            copy.wait_send()


def weight_route(me, dims, rows):
    seqs, heads = dims[0] * dims[1], dims[2] * dims[3]
    per_head = HEAD_DIM // rows
    shift = seqs // 2
    target = {
        "seq": (me.seq % per_head * heads + me.dp + shift) % seqs,
        "dp": me.seq // per_head,
    }
    tile = (me.seq + shift) % seqs
    source = {"seq": me.dp * per_head + tile // heads, "dp": tile % heads}
    return target, source


def gather_kernel(
    dims, k, v, w, go, pick, gpick, gowner,
    halo, glob, rnd, wh, gctx,
    km, vm, kp, vp, k2, v2, kblk, vblk, sb0, sb1, sb2, sb3, edge,
    gcand, ga, gmine, gb, gpiece, wmine, wcol, wall, gog, send_sems, recv_sems,
):
    me = Place(dims)
    Z, PN, Y, L = dims
    wire = Wire(send_sems, recv_sems)
    blocks = k.shape[0] // BLOCK
    piece = glob.shape[1]
    rows = w.shape[0]
    w_target, w_source = weight_route(me, dims, rows)

    kblk[...] = k[...].reshape(blocks, BLOCK, HEAD_DIM)
    vblk[...] = v[...].reshape(blocks, BLOCK, HEAD_DIM)
    edge[0, 0] = kblk[blocks - 1]
    edge[0, 1] = vblk[blocks - 1]
    edge[1, 0] = kblk[0]
    edge[1, 1] = vblk[0]
    for j in range(2):
        at = gpick[j]
        for part, source in ((0, kblk), (1, vblk)):
            first = (j * 2 + part) * (BLOCK // piece)
            gcand[first : first + BLOCK // piece] = source[at].reshape(
                BLOCK // piece, piece, HEAD_DIM
            )
    me.enter([w_source])

    w_in = wire.send(w, wmine, w_target)
    k_up = wire.send(kblk, km, me.at_z(1))
    k_down = wire.send(kblk, kp, me.at_z(-1))
    l_in = [wire.send(go, gog.at[me.y, me.l], me.at_l(j)) for j in range(1, L)]
    y_in = [wire.send(go, gog.at[me.y, me.l], me.at_y(j)) for j in range(1, Y)]
    g_a = [
        wire.send(gcand.at[(me.p + j) % PN], ga.at[me.p], me.at_p(j)) for j in range(1, PN)
    ]
    edges = [
        wire.send(edge.at[0], halo.at[0], me.at_s(1)),
        wire.send(edge.at[1], halo.at[1], me.at_s(-1)),
    ]
    gog[pl.ds(me.y, 1), pl.ds(me.l, 1)] = go[...][None, None]
    arrivals = []

    def pack(at, part, source, buffer):
        for requester in range(PN):
            for c in range(CAP):
                buffer[part, requester, c] = source(pick[(at * PN + requester) * CAP + c])
        rnd[at, part, pl.ds(me.p, 1)] = buffer[part, pl.ds(me.p, 1)]
        for j in range(1, PN):
            arrivals.append(
                wire.send(buffer.at[part, (me.p + j) % PN], rnd.at[at, part, me.p], me.at_p(j))
            )

    pack(0, 0, lambda b: kblk[b], sb0)
    pack(0, 1, lambda b: vblk[b], sb0)

    w_in.wait_recv()
    w_z = [wire.send(wmine, wcol.at[me.z], me.at_z(j)) for j in range(1, Z)]
    wcol[pl.ds(me.z, 1)] = wmine[...][None]

    ga[pl.ds(me.p, 1)] = gcand[pl.ds(me.p, 1)]
    for copy in g_a:
        copy.wait_recv()
    own_half = (me.p // (PN // 2)) % 2
    gmine[...] = ga[jnp.where(own_half == 0, gowner[0], gowner[1])]
    g_b = [wire.send(gmine, gb.at[j], me.at_z(j)) for j in range(1, Z)]

    for copy in w_z:
        copy.wait_recv()
    wall[pl.ds(me.p, 1)] = wcol[...][None]
    w_p = [wire.send(wcol, wall.at[me.p], me.at_p(j)) for j in range(1, PN)]

    gb[0] = gmine[...]
    for copy in g_b:
        copy.wait_recv()
    gpiece[...] = gb[jnp.where(own_half == 0, gowner[2], gowner[3])]
    glob[pl.ds(me.p, 1)] = gpiece[...][None]
    g_c = [wire.send(gpiece, glob.at[me.p], me.at_p(j)) for j in range(1, PN)]

    for j in range(1, L):
        l_in[j - 1].wait_recv()
        source = (me.l + L - j) % L
        for i in range(1, Y):
            y_in.append(wire.send(gog.at[me.y, source], gog.at[me.y, source], me.at_y(i)))

    k_up.wait_send()
    k_down.wait_send()
    wire.done(k_up, k_down)
    v_up = wire.send(vblk, vm, me.at_z(1))
    v_down = wire.send(vblk, vp, me.at_z(-1))

    low, high = pl.ds(0, blocks // 2), pl.ds(blocks // 2, blocks - blocks // 2)

    def forward(lower, upper, far):
        return [
            wire.send(lower.at[low], far.at[low], me.at_z(1)),
            wire.send(upper.at[high], far.at[high], me.at_z(-1)),
        ]

    k_up.wait_recv()
    k_down.wait_recv()
    k_far = forward(km, kp, k2)
    pack(1, 0, lambda b: km[b], sb1)
    pack(2, 0, lambda b: kp[b], sb2)
    v_up.wait_recv()
    v_down.wait_recv()
    v_far = forward(vm, vp, v2)
    for copy in k_far:
        copy.wait_recv()
    pack(1, 1, lambda b: vm[b], sb1)
    pack(2, 1, lambda b: vp[b], sb2)
    pack(3, 0, lambda b: k2[b], sb3)
    for copy in v_far:
        copy.wait_recv()
    pack(3, 1, lambda b: v2[b], sb3)

    for copy in w_p + y_in:
        copy.wait_recv()
    project(dims, rows, wall, gog, wh, gctx)
    for copy in edges + g_c + arrivals:
        copy.wait_recv()
    wire.finish()


def project(dims, rows, wall, gog, wh, gctx):
    Z, PN, Y, L = dims
    seqs, heads = Z * PN, Y * L
    total = jnp.zeros(gctx.shape, f32)
    for d in range(heads):
        tiles = []
        for i in range(HEAD_DIM // rows):
            slot = (i * heads + d + seqs // 2) % seqs
            tiles.append(wall[slot % PN, slot // PN])
        weight = jnp.concatenate(tiles, axis=0)
        wh[d] = weight
        total = total + lax.dot_general(
            gog[d // L, d % L], weight, (((1,), (1,)), ((), ())), preferred_element_type=f32
        )
    gctx[...] = total.astype(bf16)


def attend_kernel(
    q, k, v, halo, glob, rnd, gctx, slot_of, entry_of,
    ctx, dq, sb, own, edge, gsum,
    fr,
):
    blocks = q.shape[0] // BLOCK
    entries = 3 * blocks
    skip = rnd.shape[0] // 8

    def window(b, part, source):
        before = halo[0, part] if b == 0 else source[(b - 1) * BLOCK : b * BLOCK]
        after = halo[1, part] if b == blocks - 1 else source[(b + 1) * BLOCK : (b + 2) * BLOCK]
        return [before, source[b * BLOCK : (b + 1) * BLOCK], after]

    def dot(a, b, dims):
        return lax.dot_general(a, b, (dims, ((), ())), preferred_element_type=f32)

    nt, nn, tn = ((1,), (1,)), ((1,), (0,)), ((0,), (0,))
    gk = [glob[0], glob[2]]
    gv = [glob[1], glob[3]]
    acc = {}
    total = [jnp.zeros((2 * BLOCK, HEAD_DIM), f32) for _ in range(2)]

    def settle(at):
        for part in range(2):
            term = acc.pop((at, part))
            if at < 0:
                edge[0, part] = term.astype(bf16)
            elif at >= blocks:
                edge[1, part] = term.astype(bf16)
            else:
                own[part, at] = term

    fr[entries] = jnp.zeros(fr.shape[1:], bf16)
    for b in range(blocks):
        rows = slice(b * BLOCK, (b + 1) * BLOCK)
        slots = [slot_of[b * 3 + i] for i in range(3)]
        keys = jnp.concatenate(window(b, 0, k) + gk + [rnd[s] for s in slots], axis=0)
        values = jnp.concatenate(window(b, 1, v) + gv + [rnd[s + skip] for s in slots], axis=0)
        qb, gb = q[rows], gctx[rows]
        scores = dot(qb, keys, nt) * SCALE
        top = jnp.max(scores, axis=-1, keepdims=True)
        raised = jnp.exp(scores - top)
        probs32 = raised / jnp.sum(raised, axis=-1, keepdims=True)
        probs = probs32.astype(bf16)
        context = dot(probs, values, nn).astype(bf16)
        ctx[rows] = context
        delta = jnp.sum(gb.astype(f32) * context.astype(f32), axis=-1, keepdims=True)
        gprobs = dot(gb, values, nt)
        gscores = (probs32 * (gprobs - delta)).astype(bf16)
        dq[rows] = (dot(gscores, keys, nn) * SCALE).astype(bf16)
        for part, term in (
            (0, dot(gscores, qb, tn) * SCALE),
            (1, dot(probs, gb, tn)),
        ):
            for i in range(3):
                at = (b - 1 + i, part)
                piece = term[i * BLOCK : (i + 1) * BLOCK]
                acc[at] = acc[at] + piece if at in acc else piece
            total[part] = total[part] + term[3 * BLOCK : 5 * BLOCK]
            for i in range(3):
                fr[b * 3 + i, part] = term[(5 + i) * BLOCK : (6 + i) * BLOCK].astype(bf16)
        settle(b - 1)
    settle(blocks - 1)
    settle(blocks)
    for j in range(2):
        for part in range(2):
            gsum[j * 2 + part] = total[part][j * BLOCK : (j + 1) * BLOCK].astype(bf16)
    for at in range(4):
        for slot in range(skip):
            for part in range(2):
                sb[(at * 2 + part) * skip + slot] = fr[entry_of[at * skip + slot], part]


def scatter_kernel(
    dims, ctx, wh, sb, own, edge, gsum, pickx, ghit,
    out, dk, dv,
    halo, ar0, ar1, ar2, ar3, p1, p2, p3, fm, fp, rm, rp,
    ga, gmine, gb, gpiece, gall, ps, pr, ysum, lr, send_sems, recv_sems,
):
    me = Place(dims)
    Z, PN, Y, L = dims
    wire = Wire(send_sems, recv_sems)
    blocks = own.shape[1]
    half = ctx.shape[0] // 2
    me.enter()

    landing = {0: ar0, 1: ar1, 2: ar2, 3: ar3}
    arrivals = {}

    def spread(at, part):
        arrivals[at, part] = [
            wire.send(sb.at[at, part, (me.p + j) % PN], landing[at].at[part, me.p], me.at_p(j))
            for j in range(1, PN)
        ]

    def arrived(at, part):
        for copy in arrivals[at, part]:
            copy.wait_recv()

    def selection(at):
        rows, cols = blocks * 16, PN * CAP * 16
        row = lax.broadcasted_iota(jnp.int32, (rows, cols), 0)
        col = lax.broadcasted_iota(jnp.int32, (rows, cols), 1)
        wanted = jnp.broadcast_to(pickx[at : at + 1], (rows, cols))
        here = (wanted == row // 16) & (row % 16 == col % 16)
        return jnp.where(here, 1.0, 0.0).astype(bf16)

    def gather_sum(at, part, select):
        landed = landing[at]
        landed[part, pl.ds(me.p, 1)] = sb[at, part, pl.ds(me.p, 1)]
        pieces = []
        for r in range(BLOCK // 16):
            data = landed[part, :, :, r * 16 : (r + 1) * 16].reshape(-1, HEAD_DIM)
            terms = jnp.dot(select, data, preferred_element_type=f32)
            pieces.append(terms.reshape(blocks, 16, HEAD_DIM))
        return jnp.concatenate(pieces, axis=1)

    spread(3, 0)
    spread(3, 1)
    g_a = [
        wire.send(gsum.at[(me.p + j) % PN], ga.at[me.p], me.at_p(j)) for j in range(1, PN)
    ]
    edges = [
        wire.send(edge.at[0], halo.at[1], me.at_s(-1)),
        wire.send(edge.at[1], halo.at[0], me.at_s(1)),
    ]

    y_sends = []
    for part in range(2):
        rows = ctx[part * half : (part + 1) * half]
        for j in list(range(1, Y)) + [0]:
            to = (me.y + j) % Y
            for l in range(L):
                ps[part, j, l] = jnp.dot(
                    rows, wh[to * L + l], preferred_element_type=f32
                ).astype(bf16)
            if j:
                y_sends.append(wire.send(ps.at[part, j], pr.at[part, j - 1], me.at_y(j)))

    def y_stage(part):
        for copy in y_sends[part * (Y - 1) : (part + 1) * (Y - 1)]:
            copy.wait_recv()
        for l in range(L):
            total = ps[part, 0, l].astype(f32)
            for j in range(1, Y):
                total = total + pr[part, j - 1, l].astype(f32)
            ysum[part, l] = total.astype(bf16)
        return [
            wire.send(ysum.at[part, (me.l + j) % L], lr.at[part, j - 1], me.at_l(j))
            for j in range(1, L)
        ]

    select = selection(3)
    arrived(3, 0)
    p2[0] = gather_sum(3, 0, select).astype(bf16)
    far_up = wire.send(p2.at[0], fm, me.at_z(1))
    arrived(3, 1)
    spread(2, 1)
    spread(1, 0)
    p2[1] = gather_sum(3, 1, select).astype(bf16)
    far_down = wire.send(p2.at[1], fp, me.at_z(-1))

    for copy in g_a:
        copy.wait_recv()
    ga[pl.ds(me.p, 1)] = gsum[pl.ds(me.p, 1)]
    gmine[...] = jnp.sum(ga[...].astype(f32), axis=0).astype(bf16)
    g_b = [wire.send(gmine, gb.at[j - 1], me.at_z(j)) for j in range(1, Z)]

    select_up, select_down = selection(2), selection(1)
    arrived(2, 1)
    arrived(1, 0)
    spread(2, 0)
    spread(1, 1)
    p1[1] = gather_sum(2, 1, select_up).astype(bf16)
    v_up = wire.send(p1.at[1], rm.at[1], me.at_z(1))
    p3[0] = gather_sum(1, 0, select_down).astype(bf16)
    k_down = wire.send(p3.at[0], rp.at[0], me.at_z(-1))

    for copy in g_b:
        copy.wait_recv()
    gpiece[...] = (
        gmine[...].astype(f32) + jnp.sum(gb[...].astype(f32), axis=0)
    ).astype(bf16)
    gall[pl.ds(me.p, 1)] = gpiece[...][None]
    g_c = [wire.send(gpiece, gall.at[me.p], me.at_p(j)) for j in range(1, PN)]

    arrived(2, 0)
    arrived(1, 1)
    spread(0, 0)
    spread(0, 1)
    up = gather_sum(2, 0, select_up)
    down = gather_sum(1, 1, select_down)
    far_up.wait_recv()
    p1[0] = (up + fm[...].astype(f32)).astype(bf16)
    k_up = wire.send(p1.at[0], rm.at[0], me.at_z(1))
    far_down.wait_recv()
    p3[1] = (down + fp[...].astype(f32)).astype(bf16)
    v_down = wire.send(p3.at[1], rp.at[1], me.at_z(-1))
    l_sends = [y_stage(0)]

    select = selection(0)
    totals = []
    for part in range(2):
        arrived(0, part)
        totals.append(gather_sum(0, part, select) + own[part])
    l_sends.append(y_stage(1))
    for copy in edges + g_c:
        copy.wait_recv()
    everyone = gall[...].reshape(2, 2, BLOCK, HEAD_DIM).astype(f32)
    for part in range(2):
        ones = []
        for b in range(blocks):
            one = totals[part][b]
            for j in range(2):
                one = one + jnp.where(ghit[j] == b, everyone[j, part], 0.0)
            if b == 0:
                one = one + halo[0, part].astype(f32)
            if b == blocks - 1:
                one = one + halo[1, part].astype(f32)
            ones.append(one[None])
        totals[part] = jnp.concatenate(ones, axis=0)

    for part in range(2):
        for copy in l_sends[part]:
            copy.wait_recv()
        total = ysum[part, pl.ds(me.l, 1)][0].astype(f32)
        for j in range(1, L):
            total = total + lr[part, j - 1].astype(f32)
        out[part * half : (part + 1) * half] = total.astype(bf16)

    v_up.wait_recv()
    k_down.wait_recv()
    k_up.wait_recv()
    v_down.wait_recv()
    for part, target in ((0, dk), (1, dv)):
        total = totals[part] + (rm[part].astype(f32) + rp[part].astype(f32))
        target[...] = total.reshape(target.shape).astype(bf16)
    wire.finish()


def plan(dims, pattern, blocks):
    me = Place(dims)
    Z, PN, Y, L = dims
    seqs = Z * PN
    head = lax.dynamic_slice_in_dim(pattern, me.dp, 1, 0)[0]
    shared = head[0, :2]
    entries = 3 * blocks
    mine = lax.dynamic_slice_in_dim(head, me.z * PN * blocks, PN * blocks, 0)
    wanted = mine[:, 2:].reshape(PN, entries)
    owner = wanted // blocks
    e = jnp.arange(entries, dtype=jnp.int32)
    same = owner[:, :, None] == owner[:, None, :]
    rank = jnp.sum((same & (e[None, :] < e[:, None])).astype(jnp.int32), axis=-1)
    rel = jnp.array([0, Z - 1, 1, 2], jnp.int32)
    places = (me.z + rel) % Z
    c = jnp.arange(CAP, dtype=jnp.int32)
    column = places * PN + me.p
    hit = (owner[None, :, None, :] == column[:, None, None, None]) & (
        rank[None, :, None, :] == c[None, None, :, None]
    )
    pick = jnp.sum(jnp.where(hit, wanted[None, :, None, :] % blocks + 1, 0), axis=-1) - 1
    my_owner = lax.dynamic_slice_in_dim(owner, me.p, 1, 0)[0]
    my_rank = lax.dynamic_slice_in_dim(rank, me.p, 1, 0)[0]
    back = (my_owner // PN - me.z) % Z
    order_of = jnp.where(back == 0, 0, jnp.where(back == 1, 2, jnp.where(back == 2, 3, 1)))
    flat = (order_of * PN + my_owner % PN) * CAP + my_rank
    slots = jnp.arange(4 * PN * CAP, dtype=jnp.int32)
    entry_of = entries - jnp.sum(
        jnp.where(flat[None, :] == slots[:, None], entries - e[None, :], 0), axis=-1
    )
    slot_of = flat + order_of * (PN * CAP)
    g_seq = shared // blocks
    g_owner = jnp.concatenate([g_seq % PN, (me.z - g_seq // PN) % Z])
    ghit = jnp.where(g_seq == me.seq, shared % blocks, -1)
    return pick, slot_of, entry_of, shared % blocks, g_owner, ghit


def vmem():
    return pl.BlockSpec(memory_space=pltpu.VMEM)


def smem():
    return pl.BlockSpec(memory_space=pltpu.SMEM)


def per_device(dims, queries, keys, values, out_weight, grad_out, pattern):
    Z, PN, Y, L = dims
    tokens = queries.shape[0]
    blocks = tokens // BLOCK
    rows = out_weight.shape[0]
    piece = 4 * BLOCK // PN
    block = (BLOCK, HEAD_DIM)
    pair = (2,) + block
    half = tokens // 2
    shape = jax.ShapeDtypeStruct
    pick, slot_of, entry_of, g_pick, g_owner, ghit = plan(dims, pattern, blocks)

    gather_sems = 160
    halo, glob, rnd, wh, gctx = pl.pallas_call(
        functools.partial(gather_kernel, dims),
        out_shape=(
            shape((2,) + pair, bf16),
            shape((PN, piece, HEAD_DIM), bf16),
            shape((4, 2, PN, CAP) + block, bf16),
            shape((Y * L, HEAD_DIM, HEAD_DIM), bf16),
            shape((tokens, HEAD_DIM), bf16),
        ),
        in_specs=[vmem()] * 4 + [smem()] * 3,
        out_specs=(vmem(),) * 5,
        scratch_shapes=[
            *([pltpu.VMEM((blocks,) + block, bf16)] * 8),
            *([pltpu.VMEM((2, PN, CAP) + block, bf16)] * 4),
            pltpu.VMEM((2,) + pair, bf16),
            pltpu.VMEM((PN, piece, HEAD_DIM), bf16),
            pltpu.VMEM((PN, piece, HEAD_DIM), bf16),
            pltpu.VMEM((piece, HEAD_DIM), bf16),
            pltpu.VMEM((Z, piece, HEAD_DIM), bf16),
            pltpu.VMEM((piece, HEAD_DIM), bf16),
            pltpu.VMEM((rows, HEAD_DIM), bf16),
            pltpu.VMEM((Z, rows, HEAD_DIM), bf16),
            pltpu.VMEM((PN, Z, rows, HEAD_DIM), bf16),
            pltpu.VMEM((Y, L, tokens, HEAD_DIM), bf16),
            pltpu.SemaphoreType.DMA((gather_sems,)),
            pltpu.SemaphoreType.DMA((gather_sems,)),
        ],
        compiler_params=pltpu.CompilerParams(
            collective_id=0, has_side_effects=True, vmem_limit_bytes=VMEM_LIMIT
        ),
    )(keys, values, out_weight, grad_out, jnp.maximum(pick, 0).reshape(-1), g_pick, g_owner)

    slots = 4 * PN * CAP
    ctx, dq, sb, own, edge, gsum = pl.pallas_call(
        attend_kernel,
        out_shape=(
            shape((tokens, HEAD_DIM), bf16),
            shape((tokens, HEAD_DIM), bf16),
            shape((2 * slots,) + block, bf16),
            shape((2, blocks) + block, f32),
            shape((2,) + pair, bf16),
            shape((4,) + block, bf16),
        ),
        in_specs=[vmem()] * 7 + [smem()] * 2,
        out_specs=(vmem(),) * 6,
        scratch_shapes=[pltpu.VMEM((3 * blocks + 1,) + pair, bf16)],
        compiler_params=pltpu.CompilerParams(vmem_limit_bytes=VMEM_LIMIT),
    )(
        queries, keys, values, halo, glob.reshape((4,) + block),
        rnd.reshape((2 * slots,) + block), gctx, slot_of, entry_of,
    )

    scatter_sems = 160
    landing = pltpu.VMEM((2, PN, CAP) + block, bf16)
    half_sum = pltpu.VMEM((blocks,) + block, bf16)
    whole_sum = pltpu.VMEM((2, blocks) + block, bf16)
    out, dk, dv = pl.pallas_call(
        functools.partial(scatter_kernel, dims),
        out_shape=(shape((tokens, HEAD_DIM), bf16),) * 3,
        in_specs=[vmem()] * 7 + [smem()],
        out_specs=(vmem(),) * 3,
        scratch_shapes=[
            pltpu.VMEM((2,) + pair, bf16),
            landing, landing, landing, landing,
            whole_sum, whole_sum, whole_sum, half_sum, half_sum, whole_sum, whole_sum,
            pltpu.VMEM((PN, piece, HEAD_DIM), bf16),
            pltpu.VMEM((piece, HEAD_DIM), bf16),
            pltpu.VMEM((Z - 1, piece, HEAD_DIM), bf16),
            pltpu.VMEM((piece, HEAD_DIM), bf16),
            pltpu.VMEM((PN, piece, HEAD_DIM), bf16),
            pltpu.VMEM((2, Y, L, half, HEAD_DIM), bf16),
            pltpu.VMEM((2, max(Y - 1, 1), L, half, HEAD_DIM), bf16),
            pltpu.VMEM((2, L, half, HEAD_DIM), bf16),
            pltpu.VMEM((2, max(L - 1, 1), half, HEAD_DIM), bf16),
            pltpu.SemaphoreType.DMA((scatter_sems,)),
            pltpu.SemaphoreType.DMA((scatter_sems,)),
        ],
        compiler_params=pltpu.CompilerParams(
            collective_id=1, has_side_effects=True, vmem_limit_bytes=VMEM_LIMIT
        ),
    )(
        ctx, wh, sb.reshape((4, 2, PN, CAP) + block), own, edge,
        gsum.reshape(PN, piece, HEAD_DIM), jnp.repeat(pick.reshape(4, PN * CAP), 16, axis=1),
        ghit,
    )
    return out, dq, dk, dv


def solution(mesh, planes=8, lines=4):
    seq, dp = mesh.shape["seq"], mesh.shape["dp"]
    dims = (seq // planes, planes, dp // lines, lines)
    tile = P("seq", "dp")
    return jax.shard_map(
        functools.partial(per_device, dims),
        mesh=mesh,
        in_specs=(tile,) * 5 + (P(),),
        out_specs=(tile,) * 4,
        check_vma=False,
    )
```

```python
import functools

import jax
import jax.numpy as jnp
from jax import lax
from jax.experimental import pallas as pl
from jax.experimental.pallas import tpu as pltpu
from jax.sharding import PartitionSpec as P

HEAD_DIM = 128
BLOCK = 64
SCALE = HEAD_DIM**-0.5
CAP = 2
PICK, WANT, ENTRY = 0, 32, 64
LANES = 128
VMEM_LIMIT = 48 * 1024 * 1024
MESH = pl.DeviceIdType.MESH
f32 = jnp.float32
bf16 = jnp.bfloat16


class Place:
    def __init__(self, dims):
        self.Z, self.P, self.Y, self.L = dims
        seq, dp = lax.axis_index("seq"), lax.axis_index("dp")
        self.seq, self.dp = seq, dp
        self.z, self.p = seq // self.P, seq % self.P
        self.y, self.l = dp // self.L, dp % self.L

    def at_z(self, j):
        return {"seq": (self.z + j) % self.Z * self.P + self.p, "dp": self.dp}

    def at_p(self, j):
        return {"seq": self.z * self.P + (self.p + j) % self.P, "dp": self.dp}

    def at_y(self, j):
        return {"seq": self.seq, "dp": (self.y + j) % self.Y * self.L + self.l}

    def at_l(self, j):
        return {"seq": self.seq, "dp": self.y * self.L + (self.l + j) % self.L}

    def at_s(self, j):
        return {"seq": (self.seq + j) % (self.Z * self.P), "dp": self.dp}

    def signal(self):
        partners = (
            [self.at_p(j) for j in range(1, self.P)]
            + [self.at_z(j) for j in range(1, self.Z)]
            + [self.at_y(j) for j in range(1, self.Y)]
            + [self.at_l(j) for j in range(1, self.L)]
            + [self.at_s(1), self.at_s(-1)]
        )
        barrier = pltpu.get_barrier_semaphore()
        for partner in partners:
            pl.semaphore_signal(barrier, inc=1, device_id=partner, device_id_type=MESH)
        return len(partners)

    def wait(self, count):
        pl.semaphore_wait(pltpu.get_barrier_semaphore(), count)


class Wire:
    def __init__(self, send_sems, recv_sems):
        self.send_sems, self.recv_sems = send_sems, recv_sems
        self.used = 0
        self.sent = []

    def send(self, src, dst, target):
        copy = pltpu.make_async_remote_copy(
            src_ref=src,
            dst_ref=dst,
            send_sem=self.send_sems.at[self.used],
            recv_sem=self.recv_sems.at[self.used],
            device_id=target,
            device_id_type=MESH,
        )
        self.used += 1
        copy.start()
        self.sent.append(copy)
        return copy

    def finish(self):
        for copy in self.sent:
            copy.wait_send()


def kernel(
    dims, q, k, v, w, go, wanted, shared,
    out, dq, dk, dv,
    qv, kblk, vblk, wv, gov, ivec, idx, edge,
    km, vm, kp, vp, k2, v2, sb0, sb1, sb2, sb3, rnd, halo, glob,
    gcand, ga, gmine, gb, gpiece, wcol, wall, ps, pr, ysum, lr, gctx,
    kcat, vcat, probs32, fr, ctx, own, sb, eout, gsum,
    ehalo, ar0, ar1, ar2, ar3, selects, p1, p2, p3, fm, fp, rm, rp,
    sa, smine, sg, spiece, sall, cr,
    send_sems, recv_sems, local_sems,
):
    me = Place(dims)
    Z, PN, Y, L = dims
    wire = Wire(send_sems, recv_sems)
    blocks = k.shape[0]
    entries = 3 * blocks
    half = go.shape[0] // 2
    piece = glob.shape[1]
    pieces = BLOCK // piece
    skip = PN * CAP

    local = [
        pltpu.make_async_copy(src, dst, local_sems.at[i])
        for i, (src, dst) in enumerate(((k, kblk), (v, vblk), (w, wv), (go, gov), (q, qv)))
    ]
    for copy in local:
        copy.start()
    partners = me.signal()

    want = wanted[...]
    lane = lax.broadcasted_iota(jnp.int32, want.shape, 1)
    owner = lax.shift_right_arithmetic(want, blocks.bit_length() - 1)
    rank = jnp.zeros_like(want)
    for e in range(entries):
        at = WANT + e
        rank = rank + jnp.where((owner == owner[:, at : at + 1]) & (lane > at), 1, 0)
    rank = jnp.minimum(rank, CAP - 1)
    listed = (lane >= WANT) & (lane < WANT + entries)
    table = jnp.zeros_like(want)
    for i, rel in enumerate((0, Z - 1, 1, 2)):
        column = (me.z + rel) % Z * PN + me.p
        for c in range(CAP):
            hit = listed & (owner == column) & (rank == c)
            found = jnp.where(hit, (want & (blocks - 1)) + 1, 0)
            found = jnp.minimum(jnp.sum(found, axis=1, keepdims=True), blocks) - 1
            table = jnp.where(lane == PICK + i * CAP + c, found, table)
    back = (lax.shift_right_arithmetic(owner, PN.bit_length() - 1) - me.z) & (Z - 1)
    order_of = jnp.where(back == 0, 0, jnp.where(back == 1, 2, jnp.where(back == 2, 3, 1)))
    flat = (order_of * PN + (owner & (PN - 1))) * CAP + rank
    table = jnp.where(listed, flat, table)
    slot_entry = jnp.full_like(want, entries)
    for e in range(entries):
        at = WANT + e
        slot_entry = jnp.where(lane - ENTRY == flat[:, at : at + 1], e, slot_entry)
    ivec[...] = jnp.where(lane >= ENTRY, slot_entry, table)
    to_scalars = pltpu.make_async_copy(ivec, idx, local_sems.at[5])
    to_scalars.start()

    for copy in local:
        copy.wait()
    edge[0, 0] = kblk[blocks - 1]
    edge[0, 1] = vblk[blocks - 1]
    edge[1, 0] = kblk[0]
    edge[1, 1] = vblk[0]
    g_seq = [shared[j] // blocks for j in range(2)]
    g_block = [shared[j] % blocks for j in range(2)]
    for j in range(2):
        for part, source in ((0, kblk), (1, vblk)):
            first = (j * 2 + part) * pieces
            gcand[first : first + pieces] = source[g_block[j]].reshape(pieces, piece, HEAD_DIM)
    to_scalars.wait()
    me.wait(partners)

    w_z = [wire.send(w, wcol.at[me.z], me.at_z(j)) for j in range(1, Z)]
    k_up = wire.send(k, km, me.at_z(1))
    k_down = wire.send(k, kp, me.at_z(-1))
    v_up = wire.send(v, vm, me.at_z(1))
    v_down = wire.send(v, vp, me.at_z(-1))
    g_a = [
        wire.send(gcand.at[(me.p + j) % PN], ga.at[me.p], me.at_p(j)) for j in range(1, PN)
    ]
    edges = [
        wire.send(edge.at[0], halo.at[0], me.at_s(1)),
        wire.send(edge.at[1], halo.at[1], me.at_s(-1)),
    ]
    arrivals = []

    def pack(at, part, source, buffer):
        for requester in range(PN):
            for c in range(CAP):
                block = jnp.maximum(idx[requester, PICK + at * CAP + c], 0)
                buffer[part, requester, c] = source(block)
        rnd[pl.ds((at * 2 + part) * skip + me.p * CAP, CAP)] = buffer[part, pl.ds(me.p, 1)][0]
        for j in range(1, PN):
            arrivals.append(
                wire.send(
                    buffer.at[part, (me.p + j) % PN],
                    rnd.at[pl.ds((at * 2 + part) * skip + me.p * CAP, CAP)],
                    me.at_p(j),
                )
            )

    pack(0, 0, lambda b: kblk[b], sb0)
    pack(0, 1, lambda b: vblk[b], sb0)

    wcol[pl.ds(me.z, 1)] = wv[...][None]
    for copy in w_z:
        copy.wait_recv()
    wall[:, pl.ds(me.p, 1)] = wcol[...][:, None]
    w_p = [wire.send(wcol, wall.at[:, me.p], me.at_p(j)) for j in range(1, PN)]

    ga[pl.ds(me.p, 1)] = gcand[pl.ds(me.p, 1)]
    for copy in g_a:
        copy.wait_recv()
    own_half = (me.p // (PN // 2)) % 2
    gmine[...] = ga[jnp.where(own_half == 0, g_seq[0] % PN, g_seq[1] % PN)]
    g_b = [wire.send(gmine, gb.at[j], me.at_z(j)) for j in range(1, Z)]

    row = lax.broadcasted_iota(jnp.int32, (16, blocks * 16), 0)
    col = lax.broadcasted_iota(jnp.int32, (16, blocks * 16), 1)
    diagonal = col % 16 == row
    for at in range(4):
        for slot in range(skip):
            block = idx[slot // CAP, PICK + at * CAP + slot % CAP]
            hit = diagonal & (col // 16 == block)
            selects[at, slot * 16 : (slot + 1) * 16] = jnp.where(hit, 1.0, 0.0).astype(bf16)

    for copy in w_p:
        copy.wait_recv()
    chunk_z = Z // Y
    width = L * HEAD_DIM
    y_sends = []
    for part in range(2):
        rows = gov[part * half : (part + 1) * half]
        for j in list(range(1, Y)) + [0]:
            to = (me.y + j) % Y
            weight = wall[pl.ds(to * chunk_z, chunk_z)].reshape(width, HEAD_DIM)
            terms = lax.dot_general(
                rows, weight, (((1,), (1,)), ((), ())), preferred_element_type=f32
            ).astype(bf16)
            for head in range(L):
                ps[part, j, head] = terms[:, head * HEAD_DIM : (head + 1) * HEAD_DIM]
            if j:
                y_sends.append(wire.send(ps.at[part, j], pr.at[part, j - 1], me.at_y(j)))

    low, high = pl.ds(0, blocks // 2), pl.ds(blocks // 2, blocks - blocks // 2)

    def forward(lower, upper, far):
        return [
            wire.send(lower.at[low], far.at[low], me.at_z(1)),
            wire.send(upper.at[high], far.at[high], me.at_z(-1)),
        ]

    def y_stage(part):
        for copy in y_sends[part * (Y - 1) : (part + 1) * (Y - 1)]:
            copy.wait_recv()
        for head in range(L):
            total = ps[part, 0, head].astype(f32)
            for j in range(1, Y):
                total = total + pr[part, j - 1, head].astype(f32)
            ysum[part, head] = total.astype(bf16)
        return [
            wire.send(ysum.at[part, (me.l + j) % L], lr.at[part, j - 1], me.at_l(j))
            for j in range(1, L)
        ]

    k_up.wait_recv()
    k_down.wait_recv()
    k_far = forward(km, kp, k2)
    pack(1, 0, lambda b: km[b], sb1)
    pack(2, 0, lambda b: kp[b], sb2)
    v_up.wait_recv()
    v_down.wait_recv()
    v_far = forward(vm, vp, v2)
    pack(1, 1, lambda b: vm[b], sb1)
    pack(2, 1, lambda b: vp[b], sb2)
    gb[0] = gmine[...]
    for copy in g_b:
        copy.wait_recv()
    g_rel = [(me.z - g_seq[j] // PN + Z) % Z for j in range(2)]
    gpiece[...] = gb[jnp.where(own_half == 0, g_rel[0], g_rel[1])]
    glob[pl.ds(me.p, 1)] = gpiece[...][None]
    g_c = [wire.send(gpiece, glob.at[me.p], me.at_p(j)) for j in range(1, PN)]
    for copy in k_far:
        copy.wait_recv()
    pack(3, 0, lambda b: k2[b], sb3)
    l_sends = [y_stage(0)]
    for copy in v_far:
        copy.wait_recv()
    pack(3, 1, lambda b: v2[b], sb3)
    l_sends.append(y_stage(1))
    for copy in edges + g_c + arrivals:
        copy.wait_recv()

    def window(b, part, source):
        before = halo[0, part] if b == 0 else source[b - 1]
        after = halo[1, part] if b == blocks - 1 else source[b + 1]
        return [before, source[b], after]

    def dot(a, b, dims):
        return lax.dot_general(a, b, (dims, ((), ())), preferred_element_type=f32)

    nt, nn, tn = ((1,), (1,)), ((1,), (0,)), ((0,), (0,))
    everyone = glob[...].reshape(2, 2, BLOCK, HEAD_DIM)
    span = [slice(b * BLOCK, (b + 1) * BLOCK) for b in range(blocks)]
    for b in range(blocks):
        slots = []
        for i in range(3):
            flat_slot = idx[me.p, WANT + b * 3 + i]
            slots.append(flat_slot + flat_slot // skip * skip)
        keys = jnp.concatenate(
            window(b, 0, kblk) + [everyone[0, 0], everyone[1, 0]] + [rnd[s] for s in slots],
            axis=0,
        )
        values = jnp.concatenate(
            window(b, 1, vblk) + [everyone[0, 1], everyone[1, 1]] + [rnd[s + skip] for s in slots],
            axis=0,
        )
        kcat[b] = keys
        vcat[b] = values
        scores = dot(qv[span[b]], keys, nt) * SCALE
        raised = jnp.exp(scores - jnp.max(scores, axis=-1, keepdims=True))
        probs = raised / jnp.sum(raised, axis=-1, keepdims=True)
        probs32[b] = probs
        ctx[span[b]] = dot(probs.astype(bf16), values, nn).astype(bf16)

    l_in = [wire.send(ctx, cr.at[me.y, me.l], me.at_l(j)) for j in range(1, L)]
    y_in = [wire.send(ctx, cr.at[me.y, me.l], me.at_y(j)) for j in range(1, Y)]
    cr[pl.ds(me.y, 1), pl.ds(me.l, 1)] = ctx[...][None, None]
    for part in range(2):
        for copy in l_sends[part]:
            copy.wait_recv()
        total = ysum[part, pl.ds(me.l, 1)][0].astype(f32)
        for j in range(1, L):
            total = total + lr[part, j - 1].astype(f32)
        gctx[part * half : (part + 1) * half] = total.astype(bf16)

    acc = {}
    total = [jnp.zeros((2 * BLOCK, HEAD_DIM), f32) for _ in range(2)]

    def settle(at):
        for part in range(2):
            term = acc.pop((at, part))
            if at < 0:
                eout[0, part] = term.astype(bf16)
            elif at >= blocks:
                eout[1, part] = term.astype(bf16)
            else:
                own[part, at] = term

    fr[entries] = jnp.zeros(fr.shape[1:], bf16)
    for b in range(blocks):
        qb, gb_rows = qv[span[b]], gctx[span[b]]
        probs = probs32[b]
        keys, values = kcat[b], vcat[b]
        delta = jnp.sum(
            gb_rows.astype(f32) * ctx[span[b]].astype(f32), axis=-1, keepdims=True
        )
        gscores = (probs * (dot(gb_rows, values, nt) - delta)).astype(bf16)
        dq[span[b]] = (dot(gscores, keys, nn) * SCALE).astype(bf16)
        for part, term in (
            (0, dot(gscores, qb, tn) * SCALE),
            (1, dot(probs.astype(bf16), gb_rows, tn)),
        ):
            for i in range(3):
                at = (b - 1 + i, part)
                one = term[i * BLOCK : (i + 1) * BLOCK]
                acc[at] = acc[at] + one if at in acc else one
            total[part] = total[part] + term[3 * BLOCK : 5 * BLOCK]
            for i in range(3):
                fr[b * 3 + i, part] = term[(5 + i) * BLOCK : (6 + i) * BLOCK].astype(bf16)
        settle(b - 1)
    settle(blocks - 1)
    settle(blocks)

    landing = (ar0, ar1, ar2, ar3)
    returned = {}

    def spread(at, part):
        for slot in range(skip):
            entry = idx[me.p, ENTRY + at * skip + slot]
            sb[at, part, slot // CAP, slot % CAP] = fr[entry, part]
        landing[at][part, pl.ds(me.p, 1)] = sb[at, part, pl.ds(me.p, 1)]
        returned[at, part] = [
            wire.send(sb.at[at, part, (me.p + j) % PN], landing[at].at[part, me.p], me.at_p(j))
            for j in range(1, PN)
        ]

    spread(3, 0)
    spread(3, 1)
    for j in range(2):
        for part in range(2):
            first = (j * 2 + part) * pieces
            gsum[first : first + pieces] = (
                total[part][j * BLOCK : (j + 1) * BLOCK]
                .astype(bf16)
                .reshape(pieces, piece, HEAD_DIM)
            )
    s_a = [
        wire.send(gsum.at[(me.p + j) % PN], sa.at[me.p], me.at_p(j)) for j in range(1, PN)
    ]
    edges = [
        wire.send(eout.at[0], ehalo.at[1], me.at_s(-1)),
        wire.send(eout.at[1], ehalo.at[0], me.at_s(1)),
    ]
    for at, part in ((1, 0), (2, 1), (1, 1), (2, 0), (0, 0), (0, 1)):
        spread(at, part)

    def gather_sum(at, part):
        for copy in returned[at, part]:
            copy.wait_recv()
        sums = []
        for r in range(BLOCK // 16):
            data = landing[at][part, :, :, r * 16 : (r + 1) * 16].reshape(skip * 16, HEAD_DIM)
            sums.append(dot(selects[at], data, tn).reshape(blocks, 16, HEAD_DIM))
        return jnp.concatenate(sums, axis=1)

    p2[0] = gather_sum(3, 0).astype(bf16)
    far_up = wire.send(p2.at[0], fm, me.at_z(1))
    p2[1] = gather_sum(3, 1).astype(bf16)
    far_down = wire.send(p2.at[1], fp, me.at_z(-1))

    for copy in s_a:
        copy.wait_recv()
    sa[pl.ds(me.p, 1)] = gsum[pl.ds(me.p, 1)]
    smine[...] = jnp.sum(sa[...].astype(f32), axis=0).astype(bf16)
    s_b = [wire.send(smine, sg.at[j - 1], me.at_z(j)) for j in range(1, Z)]

    p3[0] = gather_sum(1, 0).astype(bf16)
    k_down = wire.send(p3.at[0], rp.at[0], me.at_z(-1))
    p1[1] = gather_sum(2, 1).astype(bf16)
    v_up = wire.send(p1.at[1], rm.at[1], me.at_z(1))
    for j in range(1, L):
        l_in[j - 1].wait_recv()
        source = (me.l + L - j) % L
        for i in range(1, Y):
            y_in.append(wire.send(cr.at[me.y, source], cr.at[me.y, source], me.at_y(i)))
    down = gather_sum(1, 1)
    up = gather_sum(2, 0)
    far_up.wait_recv()
    p1[0] = (up + fm[...].astype(f32)).astype(bf16)
    k_up = wire.send(p1.at[0], rm.at[0], me.at_z(1))
    far_down.wait_recv()
    p3[1] = (down + fp[...].astype(f32)).astype(bf16)
    v_down = wire.send(p3.at[1], rp.at[1], me.at_z(-1))

    for copy in s_b:
        copy.wait_recv()
    spiece[...] = (
        smine[...].astype(f32) + jnp.sum(sg[...].astype(f32), axis=0)
    ).astype(bf16)
    sall[pl.ds(me.p, 1)] = spiece[...][None]
    s_c = [wire.send(spiece, sall.at[me.p], me.at_p(j)) for j in range(1, PN)]

    totals = [gather_sum(0, part) + own[part] for part in range(2)]
    for copy in y_in:
        copy.wait_recv()
    per_head = HEAD_DIM // w.shape[0]
    result = jnp.zeros(out.shape, f32)
    for y in range(Y):
        for l in range(L):
            head = y * L + l
            tiles = range(head * per_head, (head + 1) * per_head)
            weight = jnp.concatenate([wall[t // PN, t % PN] for t in tiles], axis=0)
            result = result + jnp.dot(cr[y, l], weight, preferred_element_type=f32)
    out[...] = result.astype(bf16)

    for copy in edges + s_c:
        copy.wait_recv()
    everyone = sall[...].reshape(2, 2, BLOCK, HEAD_DIM).astype(f32)
    g_here = [jnp.where(g_seq[j] == me.seq, g_block[j], -1) for j in range(2)]
    for part in range(2):
        ones = []
        for b in range(blocks):
            one = totals[part][b]
            for j in range(2):
                one = one + jnp.where(g_here[j] == b, everyone[j, part], 0.0)
            if b == 0:
                one = one + ehalo[0, part].astype(f32)
            if b == blocks - 1:
                one = one + ehalo[1, part].astype(f32)
            ones.append(one[None])
        totals[part] = jnp.concatenate(ones, axis=0)
    for copy in (v_up, k_down, k_up, v_down):
        copy.wait_recv()
    for part, target in ((0, dk), (1, dv)):
        total = totals[part] + (rm[part].astype(f32) + rp[part].astype(f32))
        target[...] = total.reshape(target.shape).astype(bf16)
    wire.finish()


def per_device(dims, queries, keys, values, out_weight, grad_out, pattern):
    Z, PN, Y, L = dims
    me = Place(dims)
    tokens = queries.shape[0]
    blocks = tokens // BLOCK
    entries = 3 * blocks
    rows = out_weight.shape[0]
    piece = 4 * BLOCK // PN
    half = tokens // 2
    block = (BLOCK, HEAD_DIM)
    any_space = pl.BlockSpec(memory_space=pl.ANY)
    in_vmem = pl.BlockSpec(memory_space=pltpu.VMEM)
    shape = jax.ShapeDtypeStruct

    plane = lax.dynamic_slice(
        pattern, (me.dp, me.z * PN * blocks, 0), (1, PN * blocks, pattern.shape[2])
    )[0]
    wanted = jnp.pad(
        plane[:, 2:].reshape(PN, entries),
        ((0, 0), (WANT, LANES - WANT - entries)),
        constant_values=-1,
    )

    def buffer(*dims, dtype=bf16):
        return pltpu.VMEM(dims, dtype)

    keyed = buffer(blocks, *block)
    slots = buffer(2, PN, CAP, *block)
    pairs = buffer(2, 2, *block)
    whole = buffer(2, blocks, *block)
    small = buffer(piece, HEAD_DIM)
    spread_small = buffer(PN, piece, HEAD_DIM)
    out, dq, dk, dv = pl.pallas_call(
        functools.partial(kernel, dims),
        out_shape=(shape((tokens, HEAD_DIM), bf16),) * 4,
        in_specs=[any_space] * 5 + [in_vmem, pl.BlockSpec(memory_space=pltpu.SMEM)],
        out_specs=(in_vmem,) * 4,
        scratch_shapes=[
            buffer(tokens, HEAD_DIM), keyed, keyed, buffer(rows, HEAD_DIM),
            buffer(tokens, HEAD_DIM), buffer(PN, LANES, dtype=jnp.int32),
            pltpu.SMEM((PN, LANES), jnp.int32), pairs,
            keyed, keyed, keyed, keyed, keyed, keyed, slots, slots, slots, slots,
            buffer(8 * PN * CAP, *block), pairs, spread_small,
            spread_small, spread_small, small, buffer(Z, piece, HEAD_DIM), small,
            buffer(Z, rows, HEAD_DIM), buffer(Z, PN, rows, HEAD_DIM),
            buffer(2, Y, L, half, HEAD_DIM), buffer(2, max(Y - 1, 1), L, half, HEAD_DIM),
            buffer(2, L, half, HEAD_DIM), buffer(2, max(L - 1, 1), half, HEAD_DIM),
            buffer(tokens, HEAD_DIM),
            buffer(blocks, 8 * BLOCK, HEAD_DIM), buffer(blocks, 8 * BLOCK, HEAD_DIM),
            buffer(blocks, BLOCK, 8 * BLOCK, dtype=f32), buffer(entries + 1, 2, *block),
            buffer(tokens, HEAD_DIM), buffer(2, blocks, *block, dtype=f32),
            buffer(4, 2, PN, CAP, *block), pairs, spread_small,
            pairs, slots, slots, slots, slots,
            buffer(4, PN * CAP * 16, blocks * 16),
            whole, whole, whole, keyed, keyed, whole, whole,
            spread_small, small, buffer(Z - 1, piece, HEAD_DIM), small, spread_small,
            buffer(Y, L, tokens, HEAD_DIM),
            pltpu.SemaphoreType.DMA((256,)),
            pltpu.SemaphoreType.DMA((256,)),
            pltpu.SemaphoreType.DMA((6,)),
        ],
        compiler_params=pltpu.CompilerParams(
            collective_id=0, has_side_effects=True, vmem_limit_bytes=VMEM_LIMIT
        ),
    )(
        queries, keys.reshape((blocks,) + block), values.reshape((blocks,) + block),
        out_weight, grad_out, wanted, plane[0, :2],
    )
    return out, dq, dk, dv


def solution(mesh, planes=8, lines=4):
    seq, dp = mesh.shape["seq"], mesh.shape["dp"]
    dims = (seq // planes, planes, dp // lines, lines)
    tile = P("seq", "dp")
    return jax.shard_map(
        functools.partial(per_device, dims),
        mesh=mesh,
        in_specs=(tile,) * 5 + (P(),),
        out_specs=(tile,) * 4,
        check_vma=False,
    )
```

```python
import functools

import jax
import jax.numpy as jnp
from jax import lax
from jax.experimental import pallas as pl
from jax.experimental.pallas import tpu as pltpu
from jax.sharding import PartitionSpec as P

HEAD_DIM = 128
BLOCK = 64
SCALE = HEAD_DIM**-0.5
CAP = 2
PICK, WANT, ENTRY = 0, 32, 64
LANES = 128
VMEM_LIMIT = 64 * 1024 * 1024
MESH = pl.DeviceIdType.MESH
f32 = jnp.float32
bf16 = jnp.bfloat16


class Place:
    def __init__(self, dims):
        self.Z, self.P, self.Y, self.L = dims
        seq, dp = lax.axis_index("seq"), lax.axis_index("dp")
        self.seq, self.dp = seq, dp
        self.z, self.p = seq // self.P, seq % self.P
        self.y, self.l = dp // self.L, dp % self.L

    def at_z(self, j):
        return {"seq": (self.z + j) % self.Z * self.P + self.p, "dp": self.dp}

    def at_p(self, j):
        return {"seq": self.z * self.P + (self.p + j) % self.P, "dp": self.dp}

    def at_y(self, j):
        return {"seq": self.seq, "dp": (self.y + j) % self.Y * self.L + self.l}

    def at_l(self, j):
        return {"seq": self.seq, "dp": self.y * self.L + (self.l + j) % self.L}

    def at_s(self, j):
        return {"seq": (self.seq + j) % (self.Z * self.P), "dp": self.dp}

    def signal(self, extra=()):
        partners = (
            [self.at_p(j) for j in range(1, self.P)]
            + [self.at_z(j) for j in range(1, self.Z)]
            + [self.at_y(j) for j in range(1, self.Y)]
            + [self.at_l(j) for j in range(1, self.L)]
            + [self.at_s(1), self.at_s(-1)]
            + list(extra)
        )
        barrier = pltpu.get_barrier_semaphore()
        for partner in partners:
            pl.semaphore_signal(barrier, inc=1, device_id=partner, device_id_type=MESH)
        return len(partners)

    def wait(self, count):
        pl.semaphore_wait(pltpu.get_barrier_semaphore(), count)


class Wire:
    def __init__(self, send_sems, recv_sems):
        self.send_sems, self.recv_sems = send_sems, recv_sems
        self.used = 0
        self.sent = []

    def send(self, src, dst, target):
        copy = pltpu.make_async_remote_copy(
            src_ref=src,
            dst_ref=dst,
            send_sem=self.send_sems.at[self.used],
            recv_sem=self.recv_sems.at[self.used],
            device_id=target,
            device_id_type=MESH,
        )
        self.used += 1
        copy.start()
        self.sent.append(copy)
        return copy

    def finish(self):
        for copy in self.sent:
            copy.wait_send()


def weight_route(me, dims, rows):
    seqs, heads = dims[0] * dims[1], dims[2] * dims[3]
    per_head = HEAD_DIM // rows
    shift = seqs // 2
    target = {
        "seq": (me.seq % per_head * heads + me.dp + shift) % seqs,
        "dp": me.seq // per_head,
    }
    tile = (me.seq + shift) % seqs
    source = {"seq": me.dp * per_head + tile // heads, "dp": tile % heads}
    return target, source


def kernel(
    dims, q, k, v, w, go, wanted, shared,
    out, dq, dk, dv,
    qv, kblk, vblk, wv, gov, ivec, idx, edge,
    km, vm, kp, vp, k2, v2, sb0, sb1, sb2, sb3, rnd, halo, glob,
    gcand, ga, gmine, gb, gpiece, wcol, wall, wmine, wrcol, wrall, gog, gctx,
    kcat, vcat, probs32, fr, ctx, own, sb, eout, gsum,
    ehalo, ar0, ar1, ar2, ar3, selects, p1, p2, p3, fm, fp, rm, rp,
    sa, smine, sg, spiece, sall, cr,
    send_sems, recv_sems, local_sems,
):
    me = Place(dims)
    Z, PN, Y, L = dims
    wire = Wire(send_sems, recv_sems)
    blocks = k.shape[0]
    entries = 3 * blocks
    piece = glob.shape[1]
    pieces = BLOCK // piece
    skip = PN * CAP

    local = [
        pltpu.make_async_copy(src, dst, local_sems.at[i])
        for i, (src, dst) in enumerate(((k, kblk), (v, vblk), (w, wv), (go, gov), (q, qv)))
    ]
    for copy in local:
        copy.start()
    w_target, w_source = weight_route(me, dims, w.shape[0])
    partners = me.signal([w_source])

    want = wanted[...]
    lane = lax.broadcasted_iota(jnp.int32, want.shape, 1)
    owner = lax.shift_right_arithmetic(want, blocks.bit_length() - 1)
    rank = jnp.zeros_like(want)
    for e in range(entries):
        at = WANT + e
        rank = rank + jnp.where((owner == owner[:, at : at + 1]) & (lane > at), 1, 0)
    rank = jnp.minimum(rank, CAP - 1)
    listed = (lane >= WANT) & (lane < WANT + entries)
    table = jnp.zeros_like(want)
    for i, rel in enumerate((0, Z - 1, 1, 2)):
        column = (me.z + rel) % Z * PN + me.p
        for c in range(CAP):
            hit = listed & (owner == column) & (rank == c)
            found = jnp.where(hit, (want & (blocks - 1)) + 1, 0)
            found = jnp.minimum(jnp.sum(found, axis=1, keepdims=True), blocks) - 1
            table = jnp.where(lane == PICK + i * CAP + c, found, table)
    back = (lax.shift_right_arithmetic(owner, PN.bit_length() - 1) - me.z) & (Z - 1)
    order_of = jnp.where(back == 0, 0, jnp.where(back == 1, 2, jnp.where(back == 2, 3, 1)))
    flat = (order_of * PN + (owner & (PN - 1))) * CAP + rank
    table = jnp.where(listed, flat, table)
    slot_entry = jnp.full_like(want, entries)
    for e in range(entries):
        at = WANT + e
        slot_entry = jnp.where(lane - ENTRY == flat[:, at : at + 1], e, slot_entry)
    ivec[...] = jnp.where(lane >= ENTRY, slot_entry, table)
    to_scalars = pltpu.make_async_copy(ivec, idx, local_sems.at[5])
    to_scalars.start()

    for copy in local:
        copy.wait()
    edge[0, 0] = kblk[blocks - 1]
    edge[0, 1] = vblk[blocks - 1]
    edge[1, 0] = kblk[0]
    edge[1, 1] = vblk[0]
    g_seq = [shared[j] // blocks for j in range(2)]
    g_block = [shared[j] % blocks for j in range(2)]
    for j in range(2):
        for part, source in ((0, kblk), (1, vblk)):
            first = (j * 2 + part) * pieces
            gcand[first : first + pieces] = source[g_block[j]].reshape(pieces, piece, HEAD_DIM)
    to_scalars.wait()
    me.wait(partners)

    w_in = wire.send(w, wmine, w_target)
    w_z = [wire.send(w, wcol.at[me.z], me.at_z(j)) for j in range(1, Z)]
    g_a = [
        wire.send(gcand.at[(me.p + j) % PN], ga.at[me.p], me.at_p(j)) for j in range(1, PN)
    ]
    edges = [
        wire.send(edge.at[0], halo.at[0], me.at_s(1)),
        wire.send(edge.at[1], halo.at[1], me.at_s(-1)),
    ]
    k_up = wire.send(k, km, me.at_z(1))
    k_down = wire.send(k, kp, me.at_z(-1))
    v_up = wire.send(v, vm, me.at_z(1))
    v_down = wire.send(v, vp, me.at_z(-1))
    go_y = [wire.send(go, gog.at[me.y, me.l], me.at_y(j)) for j in range(1, Y)]
    arrivals = []

    def pack(at, part, source, buffer):
        for requester in range(PN):
            for c in range(CAP):
                block = jnp.maximum(idx[requester, PICK + at * CAP + c], 0)
                buffer[part, requester, c] = source(block)
        rnd[pl.ds((at * 2 + part) * skip + me.p * CAP, CAP)] = buffer[part, pl.ds(me.p, 1)][0]
        for j in range(1, PN):
            arrivals.append(
                wire.send(
                    buffer.at[part, (me.p + j) % PN],
                    rnd.at[pl.ds((at * 2 + part) * skip + me.p * CAP, CAP)],
                    me.at_p(j),
                )
            )

    pack(0, 0, lambda b: kblk[b], sb0)
    pack(0, 1, lambda b: vblk[b], sb0)

    go_l = [wire.send(go, gog.at[me.y, me.l], me.at_l(j)) for j in range(1, L)]
    gog[pl.ds(me.y, 1), pl.ds(me.l, 1)] = gov[...][None, None]
    wcol[pl.ds(me.z, 1)] = wv[...][None]
    w_in.wait_recv()
    wr_z = [wire.send(wmine, wrcol.at[me.z], me.at_z(j)) for j in range(1, Z)]
    wrcol[pl.ds(me.z, 1)] = wmine[...][None]

    ga[pl.ds(me.p, 1)] = gcand[pl.ds(me.p, 1)]
    for copy in g_a:
        copy.wait_recv()
    own_half = (me.p // (PN // 2)) % 2
    gmine[...] = ga[jnp.where(own_half == 0, g_seq[0] % PN, g_seq[1] % PN)]
    g_b = [wire.send(gmine, gb.at[j], me.at_z(j)) for j in range(1, Z)]

    row = lax.broadcasted_iota(jnp.int32, (16, blocks * 16), 0)
    col = lax.broadcasted_iota(jnp.int32, (16, blocks * 16), 1)
    diagonal = col % 16 == row
    for at in range(4):
        for slot in range(skip):
            block = idx[slot // CAP, PICK + at * CAP + slot % CAP]
            hit = diagonal & (col // 16 == block)
            selects[at, slot * 16 : (slot + 1) * 16] = jnp.where(hit, 1.0, 0.0).astype(bf16)

    low, high = pl.ds(0, blocks // 2), pl.ds(blocks // 2, blocks - blocks // 2)

    def forward(lower, upper, far):
        return [
            wire.send(lower.at[low], far.at[low], me.at_z(1)),
            wire.send(upper.at[high], far.at[high], me.at_z(-1)),
        ]

    k_up.wait_recv()
    k_down.wait_recv()
    k_far = forward(km, kp, k2)
    pack(1, 0, lambda b: km[b], sb1)
    pack(2, 0, lambda b: kp[b], sb2)
    for copy in wr_z:
        copy.wait_recv()
    wrall[pl.ds(me.p, 1)] = wrcol[...][None]
    wr_p = [wire.send(wrcol, wrall.at[me.p], me.at_p(j)) for j in range(1, PN)]
    v_up.wait_recv()
    v_down.wait_recv()
    v_far = forward(vm, vp, v2)
    pack(1, 1, lambda b: vm[b], sb1)
    pack(2, 1, lambda b: vp[b], sb2)
    for j in range(1, L):
        go_l[j - 1].wait_recv()
        source = (me.l + L - j) % L
        for i in range(1, Y):
            go_y.append(wire.send(gog.at[me.y, source], gog.at[me.y, source], me.at_y(i)))
    gb[0] = gmine[...]
    for copy in g_b:
        copy.wait_recv()
    g_rel = [(me.z - g_seq[j] // PN + Z) % Z for j in range(2)]
    gpiece[...] = gb[jnp.where(own_half == 0, g_rel[0], g_rel[1])]
    glob[pl.ds(me.p, 1)] = gpiece[...][None]
    g_c = [wire.send(gpiece, glob.at[me.p], me.at_p(j)) for j in range(1, PN)]
    for copy in k_far:
        copy.wait_recv()
    pack(3, 0, lambda b: k2[b], sb3)
    for copy in v_far:
        copy.wait_recv()
    pack(3, 1, lambda b: v2[b], sb3)
    for copy in w_z:
        copy.wait_recv()
    wall[:, pl.ds(me.p, 1)] = wcol[...][:, None]
    for copy in edges + g_c + arrivals:
        copy.wait_recv()

    def window(b, part, source):
        before = halo[0, part] if b == 0 else source[b - 1]
        after = halo[1, part] if b == blocks - 1 else source[b + 1]
        return [before, source[b], after]

    def dot(a, b, dims):
        return lax.dot_general(a, b, (dims, ((), ())), preferred_element_type=f32)

    nt, nn, tn = ((1,), (1,)), ((1,), (0,)), ((0,), (0,))
    everyone = glob[...].reshape(2, 2, BLOCK, HEAD_DIM)
    span = [slice(b * BLOCK, (b + 1) * BLOCK) for b in range(blocks)]
    for b in range(blocks):
        slots = []
        for i in range(3):
            flat_slot = idx[me.p, WANT + b * 3 + i]
            slots.append(flat_slot + flat_slot // skip * skip)
        keys = jnp.concatenate(
            window(b, 0, kblk) + [everyone[0, 0], everyone[1, 0]] + [rnd[s] for s in slots],
            axis=0,
        )
        values = jnp.concatenate(
            window(b, 1, vblk) + [everyone[0, 1], everyone[1, 1]] + [rnd[s + skip] for s in slots],
            axis=0,
        )
        kcat[b] = keys
        vcat[b] = values
        scores = dot(qv[span[b]], keys, nt) * SCALE
        raised = jnp.exp(scores - jnp.max(scores, axis=-1, keepdims=True))
        probs = raised / jnp.sum(raised, axis=-1, keepdims=True)
        probs32[b] = probs
        ctx[span[b]] = dot(probs.astype(bf16), values, nn).astype(bf16)

    l_in = [wire.send(ctx, cr.at[me.y, me.l], me.at_l(j)) for j in range(1, L)]
    y_in = [wire.send(ctx, cr.at[me.y, me.l], me.at_y(j)) for j in range(1, Y)]
    cr[pl.ds(me.y, 1), pl.ds(me.l, 1)] = ctx[...][None, None]
    w_p = [wire.send(wcol, wall.at[:, me.p], me.at_p(j)) for j in range(1, PN)]
    for copy in go_y + wr_p:
        copy.wait_recv()
    columns = []
    for d in range(Y * L):
        slots = [(i * Y * L + d + Z * PN // 2) % (Z * PN) for i in range(HEAD_DIM // w.shape[0])]
        columns.append(jnp.concatenate([wrall[t % PN, t // PN] for t in slots], axis=0))
    full = jnp.concatenate([gog[d // L, d % L] for d in range(Y * L)], axis=1)
    gctx[...] = dot(full, jnp.concatenate(columns, axis=1), nt).astype(bf16)

    acc = {}
    total = [jnp.zeros((2 * BLOCK, HEAD_DIM), f32) for _ in range(2)]

    def settle(at):
        for part in range(2):
            term = acc.pop((at, part))
            if at < 0:
                eout[0, part] = term.astype(bf16)
            elif at >= blocks:
                eout[1, part] = term.astype(bf16)
            else:
                own[part, at] = term

    fr[entries] = jnp.zeros(fr.shape[1:], bf16)
    for b in range(blocks):
        qb, gb_rows = qv[span[b]], gctx[span[b]]
        probs = probs32[b]
        keys, values = kcat[b], vcat[b]
        delta = jnp.sum(
            gb_rows.astype(f32) * ctx[span[b]].astype(f32), axis=-1, keepdims=True
        )
        gscores = (probs * (dot(gb_rows, values, nt) - delta)).astype(bf16)
        dq[span[b]] = (dot(gscores, keys, nn) * SCALE).astype(bf16)
        for part, term in (
            (0, dot(gscores, qb, tn) * SCALE),
            (1, dot(probs.astype(bf16), gb_rows, tn)),
        ):
            for i in range(3):
                at = (b - 1 + i, part)
                one = term[i * BLOCK : (i + 1) * BLOCK]
                acc[at] = acc[at] + one if at in acc else one
            total[part] = total[part] + term[3 * BLOCK : 5 * BLOCK]
            for i in range(3):
                fr[b * 3 + i, part] = term[(5 + i) * BLOCK : (6 + i) * BLOCK].astype(bf16)
        settle(b - 1)
    settle(blocks - 1)
    settle(blocks)

    landing = (ar0, ar1, ar2, ar3)
    returned = {}

    def spread(at, part):
        for slot in range(skip):
            entry = idx[me.p, ENTRY + at * skip + slot]
            sb[at, part, slot // CAP, slot % CAP] = fr[entry, part]
        landing[at][part, pl.ds(me.p, 1)] = sb[at, part, pl.ds(me.p, 1)]
        returned[at, part] = [
            wire.send(sb.at[at, part, (me.p + j) % PN], landing[at].at[part, me.p], me.at_p(j))
            for j in range(1, PN)
        ]

    spread(3, 0)
    spread(3, 1)
    for j in range(2):
        for part in range(2):
            first = (j * 2 + part) * pieces
            gsum[first : first + pieces] = (
                total[part][j * BLOCK : (j + 1) * BLOCK]
                .astype(bf16)
                .reshape(pieces, piece, HEAD_DIM)
            )
    s_a = [
        wire.send(gsum.at[(me.p + j) % PN], sa.at[me.p], me.at_p(j)) for j in range(1, PN)
    ]
    edges = [
        wire.send(eout.at[0], ehalo.at[1], me.at_s(-1)),
        wire.send(eout.at[1], ehalo.at[0], me.at_s(1)),
    ]
    for at, part in ((1, 0), (2, 1), (1, 1), (2, 0), (0, 0), (0, 1)):
        spread(at, part)

    def gather_sum(at, part):
        for copy in returned[at, part]:
            copy.wait_recv()
        sums = []
        for r in range(BLOCK // 16):
            data = landing[at][part, :, :, r * 16 : (r + 1) * 16].reshape(skip * 16, HEAD_DIM)
            sums.append(dot(selects[at], data, tn).reshape(blocks, 16, HEAD_DIM))
        return jnp.concatenate(sums, axis=1)

    p2[0] = gather_sum(3, 0).astype(bf16)
    far_up = wire.send(p2.at[0], fm, me.at_z(1))
    p2[1] = gather_sum(3, 1).astype(bf16)
    far_down = wire.send(p2.at[1], fp, me.at_z(-1))

    for copy in s_a:
        copy.wait_recv()
    sa[pl.ds(me.p, 1)] = gsum[pl.ds(me.p, 1)]
    smine[...] = jnp.sum(sa[...].astype(f32), axis=0).astype(bf16)
    s_b = [wire.send(smine, sg.at[j - 1], me.at_z(j)) for j in range(1, Z)]

    p3[0] = gather_sum(1, 0).astype(bf16)
    k_down = wire.send(p3.at[0], rp.at[0], me.at_z(-1))
    p1[1] = gather_sum(2, 1).astype(bf16)
    v_up = wire.send(p1.at[1], rm.at[1], me.at_z(1))
    for j in range(1, L):
        l_in[j - 1].wait_recv()
        source = (me.l + L - j) % L
        for i in range(1, Y):
            y_in.append(wire.send(cr.at[me.y, source], cr.at[me.y, source], me.at_y(i)))
    down = gather_sum(1, 1)
    up = gather_sum(2, 0)
    far_up.wait_recv()
    p1[0] = (up + fm[...].astype(f32)).astype(bf16)
    k_up = wire.send(p1.at[0], rm.at[0], me.at_z(1))
    far_down.wait_recv()
    p3[1] = (down + fp[...].astype(f32)).astype(bf16)
    v_down = wire.send(p3.at[1], rp.at[1], me.at_z(-1))

    for copy in s_b:
        copy.wait_recv()
    spiece[...] = (
        smine[...].astype(f32) + jnp.sum(sg[...].astype(f32), axis=0)
    ).astype(bf16)
    sall[pl.ds(me.p, 1)] = spiece[...][None]
    s_c = [wire.send(spiece, sall.at[me.p], me.at_p(j)) for j in range(1, PN)]

    totals = [gather_sum(0, part) + own[part] for part in range(2)]
    for copy in y_in + w_p:
        copy.wait_recv()
    full = jnp.concatenate([cr[d // L, d % L] for d in range(Y * L)], axis=1)
    out[...] = dot(full, wall[...].reshape(-1, HEAD_DIM), nn).astype(bf16)

    for copy in edges + s_c:
        copy.wait_recv()
    everyone = sall[...].reshape(2, 2, BLOCK, HEAD_DIM).astype(f32)
    g_here = [jnp.where(g_seq[j] == me.seq, g_block[j], -1) for j in range(2)]
    for part in range(2):
        ones = []
        for b in range(blocks):
            one = totals[part][b]
            for j in range(2):
                one = one + jnp.where(g_here[j] == b, everyone[j, part], 0.0)
            if b == 0:
                one = one + ehalo[0, part].astype(f32)
            if b == blocks - 1:
                one = one + ehalo[1, part].astype(f32)
            ones.append(one[None])
        totals[part] = jnp.concatenate(ones, axis=0)
    for copy in (v_up, k_down, k_up, v_down):
        copy.wait_recv()
    for part, target in ((0, dk), (1, dv)):
        total = totals[part] + (rm[part].astype(f32) + rp[part].astype(f32))
        target[...] = total.reshape(target.shape).astype(bf16)
    wire.finish()


def settle_kernel(*refs):
    for source, target in zip(refs[:4], refs[4:]):
        target[...] = source[...]


def per_device(dims, queries, keys, values, out_weight, grad_out, pattern):
    Z, PN, Y, L = dims
    me = Place(dims)
    tokens = queries.shape[0]
    blocks = tokens // BLOCK
    entries = 3 * blocks
    rows = out_weight.shape[0]
    piece = 4 * BLOCK // PN
    block = (BLOCK, HEAD_DIM)
    in_hbm = pl.BlockSpec(memory_space=pltpu.HBM)
    in_vmem = pl.BlockSpec(memory_space=pltpu.VMEM)
    shape = jax.ShapeDtypeStruct

    plane = lax.dynamic_slice(
        pattern, (me.dp, me.z * PN * blocks, 0), (1, PN * blocks, pattern.shape[2])
    )[0]
    wanted = jnp.pad(
        plane[:, 2:].reshape(PN, entries),
        ((0, 0), (WANT, LANES - WANT - entries)),
        constant_values=-1,
    )

    def buffer(*dims, dtype=bf16):
        return pltpu.VMEM(dims, dtype)

    keyed = buffer(blocks, *block)
    slots = buffer(2, PN, CAP, *block)
    pairs = buffer(2, 2, *block)
    whole = buffer(2, blocks, *block)
    small = buffer(piece, HEAD_DIM)
    spread_small = buffer(PN, piece, HEAD_DIM)
    out, dq, dk, dv = pl.pallas_call(
        functools.partial(kernel, dims),
        out_shape=(shape((tokens, HEAD_DIM), bf16),) * 4,
        in_specs=[in_hbm] * 5 + [in_vmem, pl.BlockSpec(memory_space=pltpu.SMEM)],
        out_specs=(in_vmem,) * 4,
        scratch_shapes=[
            buffer(tokens, HEAD_DIM), keyed, keyed, buffer(rows, HEAD_DIM),
            buffer(tokens, HEAD_DIM), buffer(PN, LANES, dtype=jnp.int32),
            pltpu.SMEM((PN, LANES), jnp.int32), pairs,
            keyed, keyed, keyed, keyed, keyed, keyed, slots, slots, slots, slots,
            buffer(8 * PN * CAP, *block), pairs, spread_small,
            spread_small, spread_small, small, buffer(Z, piece, HEAD_DIM), small,
            buffer(Z, rows, HEAD_DIM), buffer(Z, PN, rows, HEAD_DIM),
            buffer(rows, HEAD_DIM), buffer(Z, rows, HEAD_DIM), buffer(PN, Z, rows, HEAD_DIM),
            buffer(Y, L, tokens, HEAD_DIM),
            buffer(tokens, HEAD_DIM),
            buffer(blocks, 8 * BLOCK, HEAD_DIM), buffer(blocks, 8 * BLOCK, HEAD_DIM),
            buffer(blocks, BLOCK, 8 * BLOCK, dtype=f32), buffer(entries + 1, 2, *block),
            buffer(tokens, HEAD_DIM), buffer(2, blocks, *block, dtype=f32),
            buffer(4, 2, PN, CAP, *block), pairs, spread_small,
            pairs, slots, slots, slots, slots,
            buffer(4, PN * CAP * 16, blocks * 16),
            whole, whole, whole, keyed, keyed, whole, whole,
            spread_small, small, buffer(Z - 1, piece, HEAD_DIM), small, spread_small,
            buffer(Y, L, tokens, HEAD_DIM),
            pltpu.SemaphoreType.DMA((256,)),
            pltpu.SemaphoreType.DMA((256,)),
            pltpu.SemaphoreType.DMA((6,)),
        ],
        compiler_params=pltpu.CompilerParams(
            collective_id=0, has_side_effects=True, vmem_limit_bytes=VMEM_LIMIT
        ),
    )(
        queries, keys.reshape((blocks,) + block), values.reshape((blocks,) + block),
        out_weight, grad_out, wanted, plane[0, :2],
    )
    return pl.pallas_call(
        settle_kernel,
        out_shape=(shape((tokens, HEAD_DIM), bf16),) * 4,
        in_specs=[in_vmem] * 4,
        out_specs=(in_vmem,) * 4,
        compiler_params=pltpu.CompilerParams(vmem_limit_bytes=VMEM_LIMIT),
    )(out, dq, dk, dv)


def solution(mesh, planes=8, lines=4):
    seq, dp = mesh.shape["seq"], mesh.shape["dp"]
    dims = (seq // planes, planes, dp // lines, lines)
    tile = P("seq", "dp")
    return jax.shard_map(
        functools.partial(per_device, dims),
        mesh=mesh,
        in_specs=(tile,) * 5 + (P(),),
        out_specs=(tile,) * 4,
        check_vma=False,
    )
```

```python
import functools

import jax
import jax.numpy as jnp
from jax import lax
from jax.experimental import pallas as pl
from jax.experimental.pallas import tpu as pltpu
from jax.sharding import PartitionSpec as P

HEAD_DIM = 128
BLOCK = 64
SCALE = HEAD_DIM**-0.5
CAP = 2
PICK, WANT, ENTRY = 0, 32, 64
LANES = 128
VMEM_LIMIT = 64 * 1024 * 1024
MESH = pl.DeviceIdType.MESH
f32 = jnp.float32
bf16 = jnp.bfloat16


class Place:
    def __init__(self, dims):
        self.Z, self.P, self.Y, self.L = dims
        seq, dp = lax.axis_index("seq"), lax.axis_index("dp")
        self.seq, self.dp = seq, dp
        self.z, self.p = seq // self.P, seq % self.P
        self.y, self.l = dp // self.L, dp % self.L

    def at_z(self, j):
        return {"seq": (self.z + j) % self.Z * self.P + self.p, "dp": self.dp}

    def at_p(self, j):
        return {"seq": self.z * self.P + (self.p + j) % self.P, "dp": self.dp}

    def at_y(self, j):
        return {"seq": self.seq, "dp": (self.y + j) % self.Y * self.L + self.l}

    def at_l(self, j):
        return {"seq": self.seq, "dp": self.y * self.L + (self.l + j) % self.L}

    def at_s(self, j):
        return {"seq": (self.seq + j) % (self.Z * self.P), "dp": self.dp}

    def signal(self):
        partners = (
            [self.at_p(j) for j in range(1, self.P)]
            + [self.at_z(j) for j in range(1, self.Z)]
            + [self.at_y(j) for j in range(1, self.Y)]
            + [self.at_l(j) for j in range(1, self.L)]
            + [self.at_s(1), self.at_s(-1)]
        )
        barrier = pltpu.get_barrier_semaphore()
        for partner in partners:
            pl.semaphore_signal(barrier, inc=1, device_id=partner, device_id_type=MESH)
        return len(partners)

    def wait(self, count):
        pl.semaphore_wait(pltpu.get_barrier_semaphore(), count)


class Wire:
    def __init__(self, send_sems, recv_sems):
        self.send_sems, self.recv_sems = send_sems, recv_sems
        self.used = 0
        self.sent = []

    def send(self, src, dst, target):
        copy = pltpu.make_async_remote_copy(
            src_ref=src,
            dst_ref=dst,
            send_sem=self.send_sems.at[self.used],
            recv_sem=self.recv_sems.at[self.used],
            device_id=target,
            device_id_type=MESH,
        )
        self.used += 1
        copy.start()
        self.sent.append(copy)
        return copy

    def finish(self):
        for copy in self.sent:
            copy.wait_send()


def kernel(
    dims, q, k, v, w, go, wanted, shared,
    out, dq, dk, dv,
    qv, kblk, vblk, wv, gov, ivec, idx, edge,
    km, vm, kp, vp, k2, v2, sb0, sb1, sb2, sb3, rnd, halo, glob,
    gcand, ga, gmine, gb, gpiece, wcol, wall, ps, pr, ysum, lr, gctx,
    kcat, vcat, probs32, fr, ctx, own, sb, eout, gsum,
    ehalo, ar0, ar1, ar2, ar3, selects, p1, p2, p3, fm, fp, rm, rp,
    sa, smine, sg, spiece, sall, cr,
    send_sems, recv_sems, local_sems,
):
    me = Place(dims)
    Z, PN, Y, L = dims
    wire = Wire(send_sems, recv_sems)
    blocks = k.shape[0]
    entries = 3 * blocks
    half = go.shape[0] // 2
    piece = glob.shape[1]
    pieces = BLOCK // piece
    skip = PN * CAP

    local = [
        pltpu.make_async_copy(src, dst, local_sems.at[i])
        for i, (src, dst) in enumerate(((k, kblk), (v, vblk), (w, wv), (go, gov), (q, qv)))
    ]
    for copy in local:
        copy.start()
    partners = me.signal()

    want = wanted[...]
    lane = lax.broadcasted_iota(jnp.int32, want.shape, 1)
    owner = lax.shift_right_arithmetic(want, blocks.bit_length() - 1)
    rank = jnp.zeros_like(want)
    for e in range(entries):
        at = WANT + e
        rank = rank + jnp.where((owner == owner[:, at : at + 1]) & (lane > at), 1, 0)
    rank = jnp.minimum(rank, CAP - 1)
    listed = (lane >= WANT) & (lane < WANT + entries)
    table = jnp.zeros_like(want)
    for i, rel in enumerate((0, Z - 1, 1, 2)):
        column = (me.z + rel) % Z * PN + me.p
        for c in range(CAP):
            hit = listed & (owner == column) & (rank == c)
            found = jnp.where(hit, (want & (blocks - 1)) + 1, 0)
            found = jnp.minimum(jnp.sum(found, axis=1, keepdims=True), blocks) - 1
            table = jnp.where(lane == PICK + i * CAP + c, found, table)
    back = (lax.shift_right_arithmetic(owner, PN.bit_length() - 1) - me.z) & (Z - 1)
    order_of = jnp.where(back == 0, 0, jnp.where(back == 1, 2, jnp.where(back == 2, 3, 1)))
    flat = (order_of * PN + (owner & (PN - 1))) * CAP + rank
    table = jnp.where(listed, flat, table)
    slot_entry = jnp.full_like(want, entries)
    for e in range(entries):
        at = WANT + e
        slot_entry = jnp.where(lane - ENTRY == flat[:, at : at + 1], e, slot_entry)
    ivec[...] = jnp.where(lane >= ENTRY, slot_entry, table)
    to_scalars = pltpu.make_async_copy(ivec, idx, local_sems.at[5])
    to_scalars.start()

    for copy in local:
        copy.wait()
    edge[0, 0] = kblk[blocks - 1]
    edge[0, 1] = vblk[blocks - 1]
    edge[1, 0] = kblk[0]
    edge[1, 1] = vblk[0]
    g_seq = [shared[j] // blocks for j in range(2)]
    g_block = [shared[j] % blocks for j in range(2)]
    for j in range(2):
        for part, source in ((0, kblk), (1, vblk)):
            first = (j * 2 + part) * pieces
            gcand[first : first + pieces] = source[g_block[j]].reshape(pieces, piece, HEAD_DIM)
    to_scalars.wait()
    me.wait(partners)

    w_z = [wire.send(w, wcol.at[me.z], me.at_z(j)) for j in range(1, Z)]
    g_a = [
        wire.send(gcand.at[(me.p + j) % PN], ga.at[me.p], me.at_p(j)) for j in range(1, PN)
    ]
    edges = [
        wire.send(edge.at[0], halo.at[0], me.at_s(1)),
        wire.send(edge.at[1], halo.at[1], me.at_s(-1)),
    ]
    k_up = wire.send(k, km, me.at_z(1))
    k_down = wire.send(k, kp, me.at_z(-1))
    v_up = wire.send(v, vm, me.at_z(1))
    v_down = wire.send(v, vp, me.at_z(-1))
    arrivals = []

    def pack(at, part, source, buffer):
        for requester in range(PN):
            for c in range(CAP):
                block = jnp.maximum(idx[requester, PICK + at * CAP + c], 0)
                buffer[part, requester, c] = source(block)
        rnd[pl.ds((at * 2 + part) * skip + me.p * CAP, CAP)] = buffer[part, pl.ds(me.p, 1)][0]
        for j in range(1, PN):
            arrivals.append(
                wire.send(
                    buffer.at[part, (me.p + j) % PN],
                    rnd.at[pl.ds((at * 2 + part) * skip + me.p * CAP, CAP)],
                    me.at_p(j),
                )
            )


    wcol[pl.ds(me.z, 1)] = wv[...][None]
    for copy in w_z:
        copy.wait_recv()
    wall[:, pl.ds(me.p, 1)] = wcol[...][:, None]
    w_p = [wire.send(wcol, wall.at[:, me.p], me.at_p(j)) for j in range(1, PN)]

    pack(0, 0, lambda b: kblk[b], sb0)
    pack(0, 1, lambda b: vblk[b], sb0)

    ga[pl.ds(me.p, 1)] = gcand[pl.ds(me.p, 1)]
    for copy in g_a:
        copy.wait_recv()
    own_half = (me.p // (PN // 2)) % 2
    gmine[...] = ga[jnp.where(own_half == 0, g_seq[0] % PN, g_seq[1] % PN)]
    g_b = [wire.send(gmine, gb.at[j], me.at_z(j)) for j in range(1, Z)]

    row = lax.broadcasted_iota(jnp.int32, (16, blocks * 16), 0)
    col = lax.broadcasted_iota(jnp.int32, (16, blocks * 16), 1)
    diagonal = col % 16 == row
    for at in range(4):
        for slot in range(skip):
            block = idx[slot // CAP, PICK + at * CAP + slot % CAP]
            hit = diagonal & (col // 16 == block)
            selects[at, slot * 16 : (slot + 1) * 16] = jnp.where(hit, 1.0, 0.0).astype(bf16)

    for copy in w_p:
        copy.wait_recv()
    chunk_z = Z // Y
    width = L * HEAD_DIM
    y_sends = []
    for part in range(2):
        rows = gov[part * half : (part + 1) * half]
        for j in list(range(1, Y)) + [0]:
            to = (me.y + j) % Y
            weight = wall[pl.ds(to * chunk_z, chunk_z)].reshape(width, HEAD_DIM)
            terms = lax.dot_general(
                rows, weight, (((1,), (1,)), ((), ())), preferred_element_type=f32
            ).astype(bf16)
            for head in range(L):
                ps[part, j, head] = terms[:, head * HEAD_DIM : (head + 1) * HEAD_DIM]
            if j:
                y_sends.append(wire.send(ps.at[part, j], pr.at[part, j - 1], me.at_y(j)))

    low, high = pl.ds(0, blocks // 2), pl.ds(blocks // 2, blocks - blocks // 2)

    def forward(lower, upper, far):
        return [
            wire.send(lower.at[low], far.at[low], me.at_z(1)),
            wire.send(upper.at[high], far.at[high], me.at_z(-1)),
        ]

    def y_stage(part):
        for copy in y_sends[part * (Y - 1) : (part + 1) * (Y - 1)]:
            copy.wait_recv()
        for head in range(L):
            total = ps[part, 0, head].astype(f32)
            for j in range(1, Y):
                total = total + pr[part, j - 1, head].astype(f32)
            ysum[part, head] = total.astype(bf16)
        return [
            wire.send(ysum.at[part, (me.l + j) % L], lr.at[part, j - 1], me.at_l(j))
            for j in range(1, L)
        ]

    k_up.wait_recv()
    k_down.wait_recv()
    k_far = forward(km, kp, k2)
    pack(1, 0, lambda b: km[b], sb1)
    pack(2, 0, lambda b: kp[b], sb2)
    v_up.wait_recv()
    v_down.wait_recv()
    v_far = forward(vm, vp, v2)
    pack(1, 1, lambda b: vm[b], sb1)
    pack(2, 1, lambda b: vp[b], sb2)
    gb[0] = gmine[...]
    for copy in g_b:
        copy.wait_recv()
    g_rel = [(me.z - g_seq[j] // PN + Z) % Z for j in range(2)]
    gpiece[...] = gb[jnp.where(own_half == 0, g_rel[0], g_rel[1])]
    glob[pl.ds(me.p, 1)] = gpiece[...][None]
    g_c = [wire.send(gpiece, glob.at[me.p], me.at_p(j)) for j in range(1, PN)]
    for copy in k_far:
        copy.wait_recv()
    pack(3, 0, lambda b: k2[b], sb3)
    l_sends = [y_stage(0)]
    for copy in v_far:
        copy.wait_recv()
    pack(3, 1, lambda b: v2[b], sb3)
    l_sends.append(y_stage(1))
    for copy in edges + g_c + arrivals:
        copy.wait_recv()

    def window(b, part, source):
        before = halo[0, part] if b == 0 else source[b - 1]
        after = halo[1, part] if b == blocks - 1 else source[b + 1]
        return [before, source[b], after]

    def dot(a, b, dims):
        return lax.dot_general(a, b, (dims, ((), ())), preferred_element_type=f32)

    nt, nn, tn = ((1,), (1,)), ((1,), (0,)), ((0,), (0,))
    everyone = glob[...].reshape(2, 2, BLOCK, HEAD_DIM)
    span = [slice(b * BLOCK, (b + 1) * BLOCK) for b in range(blocks)]
    for b in range(blocks):
        slots = []
        for i in range(3):
            flat_slot = idx[me.p, WANT + b * 3 + i]
            slots.append(flat_slot + flat_slot // skip * skip)
        keys = jnp.concatenate(
            window(b, 0, kblk) + [everyone[0, 0], everyone[1, 0]] + [rnd[s] for s in slots],
            axis=0,
        )
        values = jnp.concatenate(
            window(b, 1, vblk) + [everyone[0, 1], everyone[1, 1]] + [rnd[s + skip] for s in slots],
            axis=0,
        )
        kcat[b] = keys
        vcat[b] = values
        scores = dot(qv[span[b]], keys, nt) * SCALE
        raised = jnp.exp(scores - jnp.max(scores, axis=-1, keepdims=True))
        probs = raised / jnp.sum(raised, axis=-1, keepdims=True)
        probs32[b] = probs
        ctx[span[b]] = dot(probs.astype(bf16), values, nn).astype(bf16)

    l_in = [wire.send(ctx, cr.at[me.y, me.l], me.at_l(j)) for j in range(1, L)]
    y_in = [wire.send(ctx, cr.at[me.y, me.l], me.at_y(j)) for j in range(1, Y)]
    cr[pl.ds(me.y, 1), pl.ds(me.l, 1)] = ctx[...][None, None]
    for part in range(2):
        for copy in l_sends[part]:
            copy.wait_recv()
        total = ysum[part, pl.ds(me.l, 1)][0].astype(f32)
        for j in range(1, L):
            total = total + lr[part, j - 1].astype(f32)
        gctx[part * half : (part + 1) * half] = total.astype(bf16)

    acc = {}
    total = [jnp.zeros((2 * BLOCK, HEAD_DIM), f32) for _ in range(2)]

    def settle(at):
        for part in range(2):
            term = acc.pop((at, part))
            if at < 0:
                eout[0, part] = term.astype(bf16)
            elif at >= blocks:
                eout[1, part] = term.astype(bf16)
            else:
                own[part, at] = term

    fr[entries] = jnp.zeros(fr.shape[1:], bf16)
    for b in range(blocks):
        qb, gb_rows = qv[span[b]], gctx[span[b]]
        probs = probs32[b]
        keys, values = kcat[b], vcat[b]
        delta = jnp.sum(
            gb_rows.astype(f32) * ctx[span[b]].astype(f32), axis=-1, keepdims=True
        )
        gscores = (probs * (dot(gb_rows, values, nt) - delta)).astype(bf16)
        dq[span[b]] = (dot(gscores, keys, nn) * SCALE).astype(bf16)
        for part, term in (
            (0, dot(gscores, qb, tn) * SCALE),
            (1, dot(probs.astype(bf16), gb_rows, tn)),
        ):
            for i in range(3):
                at = (b - 1 + i, part)
                one = term[i * BLOCK : (i + 1) * BLOCK]
                acc[at] = acc[at] + one if at in acc else one
            total[part] = total[part] + term[3 * BLOCK : 5 * BLOCK]
            for i in range(3):
                fr[b * 3 + i, part] = term[(5 + i) * BLOCK : (6 + i) * BLOCK].astype(bf16)
        settle(b - 1)
    settle(blocks - 1)
    settle(blocks)

    landing = (ar0, ar1, ar2, ar3)
    returned = {}

    def spread(at, part):
        for slot in range(skip):
            entry = idx[me.p, ENTRY + at * skip + slot]
            sb[at, part, slot // CAP, slot % CAP] = fr[entry, part]
        landing[at][part, pl.ds(me.p, 1)] = sb[at, part, pl.ds(me.p, 1)]
        returned[at, part] = [
            wire.send(sb.at[at, part, (me.p + j) % PN], landing[at].at[part, me.p], me.at_p(j))
            for j in range(1, PN)
        ]

    spread(3, 0)
    spread(3, 1)
    for j in range(2):
        for part in range(2):
            first = (j * 2 + part) * pieces
            gsum[first : first + pieces] = (
                total[part][j * BLOCK : (j + 1) * BLOCK]
                .astype(bf16)
                .reshape(pieces, piece, HEAD_DIM)
            )
    s_a = [
        wire.send(gsum.at[(me.p + j) % PN], sa.at[me.p], me.at_p(j)) for j in range(1, PN)
    ]
    edges = [
        wire.send(eout.at[0], ehalo.at[1], me.at_s(-1)),
        wire.send(eout.at[1], ehalo.at[0], me.at_s(1)),
    ]
    for at, part in ((1, 0), (2, 1), (1, 1), (2, 0), (0, 0), (0, 1)):
        spread(at, part)

    def gather_sum(at, part):
        for copy in returned[at, part]:
            copy.wait_recv()
        sums = []
        for r in range(BLOCK // 16):
            data = landing[at][part, :, :, r * 16 : (r + 1) * 16].reshape(skip * 16, HEAD_DIM)
            sums.append(dot(selects[at], data, tn).reshape(blocks, 16, HEAD_DIM))
        return jnp.concatenate(sums, axis=1)

    p2[0] = gather_sum(3, 0).astype(bf16)
    far_up = wire.send(p2.at[0], fm, me.at_z(1))
    p2[1] = gather_sum(3, 1).astype(bf16)
    far_down = wire.send(p2.at[1], fp, me.at_z(-1))

    for copy in s_a:
        copy.wait_recv()
    sa[pl.ds(me.p, 1)] = gsum[pl.ds(me.p, 1)]
    smine[...] = jnp.sum(sa[...].astype(f32), axis=0).astype(bf16)
    s_b = [wire.send(smine, sg.at[j - 1], me.at_z(j)) for j in range(1, Z)]

    p3[0] = gather_sum(1, 0).astype(bf16)
    k_down = wire.send(p3.at[0], rp.at[0], me.at_z(-1))
    p1[1] = gather_sum(2, 1).astype(bf16)
    v_up = wire.send(p1.at[1], rm.at[1], me.at_z(1))
    for j in range(1, L):
        l_in[j - 1].wait_recv()
        source = (me.l + L - j) % L
        for i in range(1, Y):
            y_in.append(wire.send(cr.at[me.y, source], cr.at[me.y, source], me.at_y(i)))
    down = gather_sum(1, 1)
    up = gather_sum(2, 0)
    far_up.wait_recv()
    p1[0] = (up + fm[...].astype(f32)).astype(bf16)
    k_up = wire.send(p1.at[0], rm.at[0], me.at_z(1))
    far_down.wait_recv()
    p3[1] = (down + fp[...].astype(f32)).astype(bf16)
    v_down = wire.send(p3.at[1], rp.at[1], me.at_z(-1))

    for copy in s_b:
        copy.wait_recv()
    spiece[...] = (
        smine[...].astype(f32) + jnp.sum(sg[...].astype(f32), axis=0)
    ).astype(bf16)
    sall[pl.ds(me.p, 1)] = spiece[...][None]
    s_c = [wire.send(spiece, sall.at[me.p], me.at_p(j)) for j in range(1, PN)]

    totals = [gather_sum(0, part) + own[part] for part in range(2)]
    for copy in y_in:
        copy.wait_recv()
    full = jnp.concatenate([cr[d // L, d % L] for d in range(Y * L)], axis=1)
    out[...] = dot(full, wall[...].reshape(-1, HEAD_DIM), nn).astype(bf16)

    for copy in edges + s_c:
        copy.wait_recv()
    everyone = sall[...].reshape(2, 2, BLOCK, HEAD_DIM).astype(f32)
    g_here = [jnp.where(g_seq[j] == me.seq, g_block[j], -1) for j in range(2)]
    for part in range(2):
        ones = []
        for b in range(blocks):
            one = totals[part][b]
            for j in range(2):
                one = one + jnp.where(g_here[j] == b, everyone[j, part], 0.0)
            if b == 0:
                one = one + ehalo[0, part].astype(f32)
            if b == blocks - 1:
                one = one + ehalo[1, part].astype(f32)
            ones.append(one[None])
        totals[part] = jnp.concatenate(ones, axis=0)
    for copy in (v_up, k_down, k_up, v_down):
        copy.wait_recv()
    for part, target in ((0, dk), (1, dv)):
        total = totals[part] + (rm[part].astype(f32) + rp[part].astype(f32))
        target[...] = total.reshape(target.shape).astype(bf16)
    wire.finish()


def settle_kernel(*refs):
    for source, target in zip(refs[:4], refs[4:]):
        target[...] = source[...]


def per_device(dims, queries, keys, values, out_weight, grad_out, pattern):
    Z, PN, Y, L = dims
    me = Place(dims)
    tokens = queries.shape[0]
    blocks = tokens // BLOCK
    entries = 3 * blocks
    rows = out_weight.shape[0]
    piece = 4 * BLOCK // PN
    half = tokens // 2
    block = (BLOCK, HEAD_DIM)
    in_hbm = pl.BlockSpec(memory_space=pltpu.HBM)
    in_vmem = pl.BlockSpec(memory_space=pltpu.VMEM)
    shape = jax.ShapeDtypeStruct

    plane = lax.dynamic_slice(
        pattern, (me.dp, me.z * PN * blocks, 0), (1, PN * blocks, pattern.shape[2])
    )[0]
    wanted = jnp.pad(
        plane[:, 2:].reshape(PN, entries),
        ((0, 0), (WANT, LANES - WANT - entries)),
        constant_values=-1,
    )

    def buffer(*dims, dtype=bf16):
        return pltpu.VMEM(dims, dtype)

    keyed = buffer(blocks, *block)
    slots = buffer(2, PN, CAP, *block)
    pairs = buffer(2, 2, *block)
    whole = buffer(2, blocks, *block)
    small = buffer(piece, HEAD_DIM)
    spread_small = buffer(PN, piece, HEAD_DIM)
    out, dq, dk, dv = pl.pallas_call(
        functools.partial(kernel, dims),
        out_shape=(shape((tokens, HEAD_DIM), bf16),) * 4,
        in_specs=[in_hbm] * 5 + [in_vmem, pl.BlockSpec(memory_space=pltpu.SMEM)],
        out_specs=(in_vmem,) * 4,
        scratch_shapes=[
            buffer(tokens, HEAD_DIM), keyed, keyed, buffer(rows, HEAD_DIM),
            buffer(tokens, HEAD_DIM), buffer(PN, LANES, dtype=jnp.int32),
            pltpu.SMEM((PN, LANES), jnp.int32), pairs,
            keyed, keyed, keyed, keyed, keyed, keyed, slots, slots, slots, slots,
            buffer(8 * PN * CAP, *block), pairs, spread_small,
            spread_small, spread_small, small, buffer(Z, piece, HEAD_DIM), small,
            buffer(Z, rows, HEAD_DIM), buffer(Z, PN, rows, HEAD_DIM),
            buffer(2, Y, L, half, HEAD_DIM), buffer(2, max(Y - 1, 1), L, half, HEAD_DIM),
            buffer(2, L, half, HEAD_DIM), buffer(2, max(L - 1, 1), half, HEAD_DIM),
            buffer(tokens, HEAD_DIM),
            buffer(blocks, 8 * BLOCK, HEAD_DIM), buffer(blocks, 8 * BLOCK, HEAD_DIM),
            buffer(blocks, BLOCK, 8 * BLOCK, dtype=f32), buffer(entries + 1, 2, *block),
            buffer(tokens, HEAD_DIM), buffer(2, blocks, *block, dtype=f32),
            buffer(4, 2, PN, CAP, *block), pairs, spread_small,
            pairs, slots, slots, slots, slots,
            buffer(4, PN * CAP * 16, blocks * 16),
            whole, whole, whole, keyed, keyed, whole, whole,
            spread_small, small, buffer(Z - 1, piece, HEAD_DIM), small, spread_small,
            buffer(Y, L, tokens, HEAD_DIM),
            pltpu.SemaphoreType.DMA((256,)),
            pltpu.SemaphoreType.DMA((256,)),
            pltpu.SemaphoreType.DMA((6,)),
        ],
        compiler_params=pltpu.CompilerParams(
            collective_id=0, has_side_effects=True, vmem_limit_bytes=VMEM_LIMIT
        ),
    )(
        queries, keys.reshape((blocks,) + block), values.reshape((blocks,) + block),
        out_weight, grad_out, wanted, plane[0, :2],
    )
    return pl.pallas_call(
        settle_kernel,
        out_shape=(shape((tokens, HEAD_DIM), bf16),) * 4,
        in_specs=[in_vmem] * 4,
        out_specs=(in_vmem,) * 4,
        compiler_params=pltpu.CompilerParams(vmem_limit_bytes=VMEM_LIMIT),
    )(out, dq, dk, dv)


def solution(mesh, planes=8, lines=4):
    seq, dp = mesh.shape["seq"], mesh.shape["dp"]
    dims = (seq // planes, planes, dp // lines, lines)
    tile = P("seq", "dp")
    return jax.shard_map(
        functools.partial(per_device, dims),
        mesh=mesh,
        in_specs=(tile,) * 5 + (P(),),
        out_specs=(tile,) * 4,
        check_vma=False,
    )
```

```python
import functools

import jax
import jax.numpy as jnp
from jax import lax
from jax.experimental import pallas as pl
from jax.experimental.pallas import tpu as pltpu
from jax.sharding import PartitionSpec as P

HEAD_DIM = 128
BLOCK = 64
SCALE = HEAD_DIM**-0.5
CAP = 2
QUARTERS = 4
PICK, WANT, ENTRY = 0, 32, 64
LANES = 128
VMEM_LIMIT = 64 * 1024 * 1024
MESH = pl.DeviceIdType.MESH
f32 = jnp.float32
bf16 = jnp.bfloat16


class Place:
    def __init__(self, dims):
        self.Z, self.P, self.Y, self.L = dims
        seq, dp = lax.axis_index("seq"), lax.axis_index("dp")
        self.seq, self.dp = seq, dp
        self.z, self.p = seq // self.P, seq % self.P
        self.y, self.l = dp // self.L, dp % self.L

    def at_z(self, j):
        return {"seq": (self.z + j) % self.Z * self.P + self.p, "dp": self.dp}

    def at_p(self, j):
        return {"seq": self.z * self.P + (self.p + j) % self.P, "dp": self.dp}

    def at_y(self, j):
        return {"seq": self.seq, "dp": (self.y + j) % self.Y * self.L + self.l}

    def at_l(self, j):
        return {"seq": self.seq, "dp": self.y * self.L + (self.l + j) % self.L}

    def at_s(self, j):
        return {"seq": (self.seq + j) % (self.Z * self.P), "dp": self.dp}

    def signal(self):
        partners = (
            [self.at_p(j) for j in range(1, self.P)]
            + [self.at_z(j) for j in range(1, self.Z)]
            + [self.at_y(j) for j in range(1, self.Y)]
            + [self.at_l(j) for j in range(1, self.L)]
            + [self.at_s(1), self.at_s(-1)]
        )
        barrier = pltpu.get_barrier_semaphore()
        for partner in partners:
            pl.semaphore_signal(barrier, inc=1, device_id=partner, device_id_type=MESH)
        return len(partners)

    def wait(self, count):
        pl.semaphore_wait(pltpu.get_barrier_semaphore(), count)


class Wire:
    def __init__(self, send_sems, recv_sems):
        self.send_sems, self.recv_sems = send_sems, recv_sems
        self.used = 0
        self.sent = []

    def send(self, src, dst, target):
        copy = pltpu.make_async_remote_copy(
            src_ref=src,
            dst_ref=dst,
            send_sem=self.send_sems.at[self.used],
            recv_sem=self.recv_sems.at[self.used],
            device_id=target,
            device_id_type=MESH,
        )
        self.used += 1
        copy.start()
        self.sent.append(copy)
        return copy

    def finish(self):
        for copy in self.sent:
            copy.wait_send()


def kernel(
    dims, q, k, v, w, go, wanted, shared,
    out, dq, dk, dv,
    qv, kblk, vblk, wv, gov, ivec, idx, edge,
    km, vm, kp, vp, k2, v2, sb0, sb1, sb2, sb3, rnd, halo, glob,
    gcand, ga, gmine, gb, gpiece, wcol, wall, ps, pr, ysum, lr, gctx,
    kcat, vcat, probs32, fr, ctx, own, sb, eout, gsum,
    ehalo, ar0, ar1, ar2, ar3, selects, p1, p2, p3, fm, fp, rm, rp,
    sa, smine, sg, spiece, sall, cr,
    send_sems, recv_sems, local_sems,
):
    me = Place(dims)
    Z, PN, Y, L = dims
    wire = Wire(send_sems, recv_sems)
    blocks = k.shape[0]
    entries = 3 * blocks
    half = go.shape[0] // QUARTERS
    piece = glob.shape[1]
    pieces = BLOCK // piece
    skip = PN * CAP

    local = [
        pltpu.make_async_copy(src, dst, local_sems.at[i])
        for i, (src, dst) in enumerate(((k, kblk), (v, vblk), (w, wv), (go, gov), (q, qv)))
    ]
    for copy in local:
        copy.start()
    partners = me.signal()

    want = wanted[...]
    lane = lax.broadcasted_iota(jnp.int32, want.shape, 1)
    owner = lax.shift_right_arithmetic(want, blocks.bit_length() - 1)
    rank = jnp.zeros_like(want)
    for e in range(entries):
        at = WANT + e
        rank = rank + jnp.where((owner == owner[:, at : at + 1]) & (lane > at), 1, 0)
    rank = jnp.minimum(rank, CAP - 1)
    listed = (lane >= WANT) & (lane < WANT + entries)
    table = jnp.zeros_like(want)
    for i, rel in enumerate((0, Z - 1, 1, 2)):
        column = (me.z + rel) % Z * PN + me.p
        for c in range(CAP):
            hit = listed & (owner == column) & (rank == c)
            found = jnp.where(hit, (want & (blocks - 1)) + 1, 0)
            found = jnp.minimum(jnp.sum(found, axis=1, keepdims=True), blocks) - 1
            table = jnp.where(lane == PICK + i * CAP + c, found, table)
    back = (lax.shift_right_arithmetic(owner, PN.bit_length() - 1) - me.z) & (Z - 1)
    order_of = jnp.where(back == 0, 0, jnp.where(back == 1, 2, jnp.where(back == 2, 3, 1)))
    flat = (order_of * PN + (owner & (PN - 1))) * CAP + rank
    table = jnp.where(listed, flat, table)
    slot_entry = jnp.full_like(want, entries)
    for e in range(entries):
        at = WANT + e
        slot_entry = jnp.where(lane - ENTRY == flat[:, at : at + 1], e, slot_entry)
    ivec[...] = jnp.where(lane >= ENTRY, slot_entry, table)
    to_scalars = pltpu.make_async_copy(ivec, idx, local_sems.at[5])
    to_scalars.start()

    for copy in local:
        copy.wait()
    edge[0, 0] = kblk[blocks - 1]
    edge[0, 1] = vblk[blocks - 1]
    edge[1, 0] = kblk[0]
    edge[1, 1] = vblk[0]
    g_seq = [shared[j] // blocks for j in range(2)]
    g_block = [shared[j] % blocks for j in range(2)]
    for j in range(2):
        for part, source in ((0, kblk), (1, vblk)):
            first = (j * 2 + part) * pieces
            gcand[first : first + pieces] = source[g_block[j]].reshape(pieces, piece, HEAD_DIM)
    to_scalars.wait()
    me.wait(partners)

    w_z = [wire.send(w, wcol.at[me.z], me.at_z(j)) for j in range(1, Z)]
    g_a = [
        wire.send(gcand.at[(me.p + j) % PN], ga.at[me.p], me.at_p(j)) for j in range(1, PN)
    ]
    edges = [
        wire.send(edge.at[0], halo.at[0], me.at_s(1)),
        wire.send(edge.at[1], halo.at[1], me.at_s(-1)),
    ]
    k_up = wire.send(k, km, me.at_z(1))
    k_down = wire.send(k, kp, me.at_z(-1))
    v_up = wire.send(v, vm, me.at_z(1))
    v_down = wire.send(v, vp, me.at_z(-1))
    arrivals = []

    def pack(at, part, source, buffer):
        for requester in range(PN):
            for c in range(CAP):
                block = jnp.maximum(idx[requester, PICK + at * CAP + c], 0)
                buffer[part, requester, c] = source(block)
        rnd[pl.ds((at * 2 + part) * skip + me.p * CAP, CAP)] = buffer[part, pl.ds(me.p, 1)][0]
        for j in range(1, PN):
            arrivals.append(
                wire.send(
                    buffer.at[part, (me.p + j) % PN],
                    rnd.at[pl.ds((at * 2 + part) * skip + me.p * CAP, CAP)],
                    me.at_p(j),
                )
            )


    wcol[pl.ds(me.z, 1)] = wv[...][None]
    for copy in w_z:
        copy.wait_recv()
    wall[:, pl.ds(me.p, 1)] = wcol[...][:, None]
    w_p = [wire.send(wcol, wall.at[:, me.p], me.at_p(j)) for j in range(1, PN)]

    pack(0, 0, lambda b: kblk[b], sb0)
    pack(0, 1, lambda b: vblk[b], sb0)

    ga[pl.ds(me.p, 1)] = gcand[pl.ds(me.p, 1)]
    for copy in g_a:
        copy.wait_recv()
    own_half = (me.p // (PN // 2)) % 2
    gmine[...] = ga[jnp.where(own_half == 0, g_seq[0] % PN, g_seq[1] % PN)]
    g_b = [wire.send(gmine, gb.at[j], me.at_z(j)) for j in range(1, Z)]

    row = lax.broadcasted_iota(jnp.int32, (16, blocks * 16), 0)
    col = lax.broadcasted_iota(jnp.int32, (16, blocks * 16), 1)
    diagonal = col % 16 == row
    for at in range(4):
        for slot in range(skip):
            block = idx[slot // CAP, PICK + at * CAP + slot % CAP]
            hit = diagonal & (col // 16 == block)
            selects[at, slot * 16 : (slot + 1) * 16] = jnp.where(hit, 1.0, 0.0).astype(bf16)

    for copy in w_p:
        copy.wait_recv()
    chunk_z = Z // Y
    width = L * HEAD_DIM
    y_sends = []
    for part in range(QUARTERS):
        rows = gov[part * half : (part + 1) * half]
        for j in list(range(1, Y)) + [0]:
            to = (me.y + j) % Y
            weight = wall[pl.ds(to * chunk_z, chunk_z)].reshape(width, HEAD_DIM)
            terms = lax.dot_general(
                rows, weight, (((1,), (1,)), ((), ())), preferred_element_type=f32
            ).astype(bf16)
            for head in range(L):
                ps[part, j, head] = terms[:, head * HEAD_DIM : (head + 1) * HEAD_DIM]
            if j:
                y_sends.append(wire.send(ps.at[part, j], pr.at[part, j - 1], me.at_y(j)))

    low, high = pl.ds(0, blocks // 2), pl.ds(blocks // 2, blocks - blocks // 2)

    def forward(lower, upper, far):
        return [
            wire.send(lower.at[low], far.at[low], me.at_z(1)),
            wire.send(upper.at[high], far.at[high], me.at_z(-1)),
        ]

    def y_stage(part):
        for copy in y_sends[part * (Y - 1) : (part + 1) * (Y - 1)]:
            copy.wait_recv()
        for head in range(L):
            total = ps[part, 0, head].astype(f32)
            for j in range(1, Y):
                total = total + pr[part, j - 1, head].astype(f32)
            ysum[part, head] = total.astype(bf16)
        return [
            wire.send(ysum.at[part, (me.l + j) % L], lr.at[part, j - 1], me.at_l(j))
            for j in range(1, L)
        ]

    k_up.wait_recv()
    k_down.wait_recv()
    k_far = forward(km, kp, k2)
    pack(1, 0, lambda b: km[b], sb1)
    pack(2, 0, lambda b: kp[b], sb2)
    v_up.wait_recv()
    v_down.wait_recv()
    v_far = forward(vm, vp, v2)
    pack(1, 1, lambda b: vm[b], sb1)
    pack(2, 1, lambda b: vp[b], sb2)
    gb[0] = gmine[...]
    for copy in g_b:
        copy.wait_recv()
    g_rel = [(me.z - g_seq[j] // PN + Z) % Z for j in range(2)]
    gpiece[...] = gb[jnp.where(own_half == 0, g_rel[0], g_rel[1])]
    glob[pl.ds(me.p, 1)] = gpiece[...][None]
    g_c = [wire.send(gpiece, glob.at[me.p], me.at_p(j)) for j in range(1, PN)]
    for copy in k_far:
        copy.wait_recv()
    pack(3, 0, lambda b: k2[b], sb3)
    l_sends = [y_stage(0), y_stage(1)]
    for copy in v_far:
        copy.wait_recv()
    pack(3, 1, lambda b: v2[b], sb3)
    l_sends += [y_stage(2), y_stage(3)]
    for copy in edges + g_c + arrivals:
        copy.wait_recv()

    def window(b, part, source):
        before = halo[0, part] if b == 0 else source[b - 1]
        after = halo[1, part] if b == blocks - 1 else source[b + 1]
        return [before, source[b], after]

    def dot(a, b, dims):
        return lax.dot_general(a, b, (dims, ((), ())), preferred_element_type=f32)

    nt, nn, tn = ((1,), (1,)), ((1,), (0,)), ((0,), (0,))
    everyone = glob[...].reshape(2, 2, BLOCK, HEAD_DIM)
    span = [slice(b * BLOCK, (b + 1) * BLOCK) for b in range(blocks)]
    for b in range(blocks):
        slots = []
        for i in range(3):
            flat_slot = idx[me.p, WANT + b * 3 + i]
            slots.append(flat_slot + flat_slot // skip * skip)
        keys = jnp.concatenate(
            window(b, 0, kblk) + [everyone[0, 0], everyone[1, 0]] + [rnd[s] for s in slots],
            axis=0,
        )
        values = jnp.concatenate(
            window(b, 1, vblk) + [everyone[0, 1], everyone[1, 1]] + [rnd[s + skip] for s in slots],
            axis=0,
        )
        kcat[b] = keys
        vcat[b] = values
        scores = dot(qv[span[b]], keys, nt) * SCALE
        raised = jnp.exp(scores - jnp.max(scores, axis=-1, keepdims=True))
        probs = raised / jnp.sum(raised, axis=-1, keepdims=True)
        probs32[b] = probs
        ctx[span[b]] = dot(probs.astype(bf16), values, nn).astype(bf16)

    l_in = [wire.send(ctx, cr.at[me.y, me.l], me.at_l(j)) for j in range(1, L)]
    y_in = [wire.send(ctx, cr.at[me.y, me.l], me.at_y(j)) for j in range(1, Y)]
    cr[pl.ds(me.y, 1), pl.ds(me.l, 1)] = ctx[...][None, None]
    for part in range(QUARTERS):
        for copy in l_sends[part]:
            copy.wait_recv()
        total = ysum[part, pl.ds(me.l, 1)][0].astype(f32)
        for j in range(1, L):
            total = total + lr[part, j - 1].astype(f32)
        gctx[part * half : (part + 1) * half] = total.astype(bf16)

    acc = {}
    total = [jnp.zeros((2 * BLOCK, HEAD_DIM), f32) for _ in range(2)]

    def settle(at):
        for part in range(2):
            term = acc.pop((at, part))
            if at < 0:
                eout[0, part] = term.astype(bf16)
            elif at >= blocks:
                eout[1, part] = term.astype(bf16)
            else:
                own[part, at] = term

    fr[entries] = jnp.zeros(fr.shape[1:], bf16)
    for b in range(blocks):
        qb, gb_rows = qv[span[b]], gctx[span[b]]
        probs = probs32[b]
        keys, values = kcat[b], vcat[b]
        delta = jnp.sum(
            gb_rows.astype(f32) * ctx[span[b]].astype(f32), axis=-1, keepdims=True
        )
        gscores = (probs * (dot(gb_rows, values, nt) - delta)).astype(bf16)
        dq[span[b]] = (dot(gscores, keys, nn) * SCALE).astype(bf16)
        for part, term in (
            (0, dot(gscores, qb, tn) * SCALE),
            (1, dot(probs.astype(bf16), gb_rows, tn)),
        ):
            for i in range(3):
                at = (b - 1 + i, part)
                one = term[i * BLOCK : (i + 1) * BLOCK]
                acc[at] = acc[at] + one if at in acc else one
            total[part] = total[part] + term[3 * BLOCK : 5 * BLOCK]
            for i in range(3):
                fr[b * 3 + i, part] = term[(5 + i) * BLOCK : (6 + i) * BLOCK].astype(bf16)
        settle(b - 1)
    settle(blocks - 1)
    settle(blocks)

    landing = (ar0, ar1, ar2, ar3)
    returned = {}

    def spread(at, part):
        for slot in range(skip):
            entry = idx[me.p, ENTRY + at * skip + slot]
            sb[at, part, slot // CAP, slot % CAP] = fr[entry, part]
        landing[at][part, pl.ds(me.p, 1)] = sb[at, part, pl.ds(me.p, 1)]
        returned[at, part] = [
            wire.send(sb.at[at, part, (me.p + j) % PN], landing[at].at[part, me.p], me.at_p(j))
            for j in range(1, PN)
        ]

    spread(3, 0)
    spread(3, 1)
    for j in range(2):
        for part in range(2):
            first = (j * 2 + part) * pieces
            gsum[first : first + pieces] = (
                total[part][j * BLOCK : (j + 1) * BLOCK]
                .astype(bf16)
                .reshape(pieces, piece, HEAD_DIM)
            )
    s_a = [
        wire.send(gsum.at[(me.p + j) % PN], sa.at[me.p], me.at_p(j)) for j in range(1, PN)
    ]
    edges = [
        wire.send(eout.at[0], ehalo.at[1], me.at_s(-1)),
        wire.send(eout.at[1], ehalo.at[0], me.at_s(1)),
    ]
    for at, part in ((1, 0), (2, 1), (1, 1), (2, 0), (0, 0), (0, 1)):
        spread(at, part)

    def gather_sum(at, part):
        for copy in returned[at, part]:
            copy.wait_recv()
        sums = []
        for r in range(BLOCK // 16):
            data = landing[at][part, :, :, r * 16 : (r + 1) * 16].reshape(skip * 16, HEAD_DIM)
            sums.append(dot(selects[at], data, tn).reshape(blocks, 16, HEAD_DIM))
        return jnp.concatenate(sums, axis=1)

    p2[0] = gather_sum(3, 0).astype(bf16)
    far_up = wire.send(p2.at[0], fm, me.at_z(1))
    p2[1] = gather_sum(3, 1).astype(bf16)
    far_down = wire.send(p2.at[1], fp, me.at_z(-1))

    for copy in s_a:
        copy.wait_recv()
    sa[pl.ds(me.p, 1)] = gsum[pl.ds(me.p, 1)]
    smine[...] = jnp.sum(sa[...].astype(f32), axis=0).astype(bf16)
    s_b = [wire.send(smine, sg.at[j - 1], me.at_z(j)) for j in range(1, Z)]

    p3[0] = gather_sum(1, 0).astype(bf16)
    k_down = wire.send(p3.at[0], rp.at[0], me.at_z(-1))
    p1[1] = gather_sum(2, 1).astype(bf16)
    v_up = wire.send(p1.at[1], rm.at[1], me.at_z(1))
    for j in range(1, L):
        l_in[j - 1].wait_recv()
        source = (me.l + L - j) % L
        for i in range(1, Y):
            y_in.append(wire.send(cr.at[me.y, source], cr.at[me.y, source], me.at_y(i)))
    down = gather_sum(1, 1)
    up = gather_sum(2, 0)
    far_up.wait_recv()
    p1[0] = (up + fm[...].astype(f32)).astype(bf16)
    k_up = wire.send(p1.at[0], rm.at[0], me.at_z(1))
    far_down.wait_recv()
    p3[1] = (down + fp[...].astype(f32)).astype(bf16)
    v_down = wire.send(p3.at[1], rp.at[1], me.at_z(-1))

    for copy in s_b:
        copy.wait_recv()
    spiece[...] = (
        smine[...].astype(f32) + jnp.sum(sg[...].astype(f32), axis=0)
    ).astype(bf16)
    sall[pl.ds(me.p, 1)] = spiece[...][None]
    s_c = [wire.send(spiece, sall.at[me.p], me.at_p(j)) for j in range(1, PN)]

    totals = [gather_sum(0, part) + own[part] for part in range(2)]
    for copy in y_in:
        copy.wait_recv()
    full = jnp.concatenate([cr[d // L, d % L] for d in range(Y * L)], axis=1)
    out[...] = dot(full, wall[...].reshape(-1, HEAD_DIM), nn).astype(bf16)

    for copy in edges + s_c:
        copy.wait_recv()
    everyone = sall[...].reshape(2, 2, BLOCK, HEAD_DIM).astype(f32)
    g_here = [jnp.where(g_seq[j] == me.seq, g_block[j], -1) for j in range(2)]
    for part in range(2):
        ones = []
        for b in range(blocks):
            one = totals[part][b]
            for j in range(2):
                one = one + jnp.where(g_here[j] == b, everyone[j, part], 0.0)
            if b == 0:
                one = one + ehalo[0, part].astype(f32)
            if b == blocks - 1:
                one = one + ehalo[1, part].astype(f32)
            ones.append(one[None])
        totals[part] = jnp.concatenate(ones, axis=0)
    for copy in (v_up, k_down, k_up, v_down):
        copy.wait_recv()
    for part, target in ((0, dk), (1, dv)):
        total = totals[part] + (rm[part].astype(f32) + rp[part].astype(f32))
        target[...] = total.reshape(target.shape).astype(bf16)
    wire.finish()


def settle_kernel(*refs):
    for source, target in zip(refs[:4], refs[4:]):
        target[...] = source[...]


def per_device(dims, queries, keys, values, out_weight, grad_out, pattern):
    Z, PN, Y, L = dims
    me = Place(dims)
    tokens = queries.shape[0]
    blocks = tokens // BLOCK
    entries = 3 * blocks
    rows = out_weight.shape[0]
    piece = 4 * BLOCK // PN
    half = tokens // QUARTERS
    block = (BLOCK, HEAD_DIM)
    in_hbm = pl.BlockSpec(memory_space=pltpu.HBM)
    in_vmem = pl.BlockSpec(memory_space=pltpu.VMEM)
    shape = jax.ShapeDtypeStruct

    plane = lax.dynamic_slice(
        pattern, (me.dp, me.z * PN * blocks, 0), (1, PN * blocks, pattern.shape[2])
    )[0]
    wanted = jnp.pad(
        plane[:, 2:].reshape(PN, entries),
        ((0, 0), (WANT, LANES - WANT - entries)),
        constant_values=-1,
    )

    def buffer(*dims, dtype=bf16):
        return pltpu.VMEM(dims, dtype)

    keyed = buffer(blocks, *block)
    slots = buffer(2, PN, CAP, *block)
    pairs = buffer(2, 2, *block)
    whole = buffer(2, blocks, *block)
    small = buffer(piece, HEAD_DIM)
    spread_small = buffer(PN, piece, HEAD_DIM)
    out, dq, dk, dv = pl.pallas_call(
        functools.partial(kernel, dims),
        out_shape=(shape((tokens, HEAD_DIM), bf16),) * 4,
        in_specs=[in_hbm] * 5 + [in_vmem, pl.BlockSpec(memory_space=pltpu.SMEM)],
        out_specs=(in_vmem,) * 4,
        scratch_shapes=[
            buffer(tokens, HEAD_DIM), keyed, keyed, buffer(rows, HEAD_DIM),
            buffer(tokens, HEAD_DIM), buffer(PN, LANES, dtype=jnp.int32),
            pltpu.SMEM((PN, LANES), jnp.int32), pairs,
            keyed, keyed, keyed, keyed, keyed, keyed, slots, slots, slots, slots,
            buffer(8 * PN * CAP, *block), pairs, spread_small,
            spread_small, spread_small, small, buffer(Z, piece, HEAD_DIM), small,
            buffer(Z, rows, HEAD_DIM), buffer(Z, PN, rows, HEAD_DIM),
            buffer(QUARTERS, Y, L, half, HEAD_DIM), buffer(QUARTERS, max(Y - 1, 1), L, half, HEAD_DIM),
            buffer(QUARTERS, L, half, HEAD_DIM), buffer(QUARTERS, max(L - 1, 1), half, HEAD_DIM),
            buffer(tokens, HEAD_DIM),
            buffer(blocks, 8 * BLOCK, HEAD_DIM), buffer(blocks, 8 * BLOCK, HEAD_DIM),
            buffer(blocks, BLOCK, 8 * BLOCK, dtype=f32), buffer(entries + 1, 2, *block),
            buffer(tokens, HEAD_DIM), buffer(2, blocks, *block, dtype=f32),
            buffer(4, 2, PN, CAP, *block), pairs, spread_small,
            pairs, slots, slots, slots, slots,
            buffer(4, PN * CAP * 16, blocks * 16),
            whole, whole, whole, keyed, keyed, whole, whole,
            spread_small, small, buffer(Z - 1, piece, HEAD_DIM), small, spread_small,
            buffer(Y, L, tokens, HEAD_DIM),
            pltpu.SemaphoreType.DMA((256,)),
            pltpu.SemaphoreType.DMA((256,)),
            pltpu.SemaphoreType.DMA((6,)),
        ],
        compiler_params=pltpu.CompilerParams(
            collective_id=0, has_side_effects=True, vmem_limit_bytes=VMEM_LIMIT
        ),
    )(
        queries, keys.reshape((blocks,) + block), values.reshape((blocks,) + block),
        out_weight, grad_out, wanted, plane[0, :2],
    )
    return pl.pallas_call(
        settle_kernel,
        out_shape=(shape((tokens, HEAD_DIM), bf16),) * 4,
        in_specs=[in_vmem] * 4,
        out_specs=(in_vmem,) * 4,
        compiler_params=pltpu.CompilerParams(vmem_limit_bytes=VMEM_LIMIT),
    )(out, dq, dk, dv)


def solution(mesh, planes=8, lines=4):
    seq, dp = mesh.shape["seq"], mesh.shape["dp"]
    dims = (seq // planes, planes, dp // lines, lines)
    tile = P("seq", "dp")
    return jax.shard_map(
        functools.partial(per_device, dims),
        mesh=mesh,
        in_specs=(tile,) * 5 + (P(),),
        out_specs=(tile,) * 4,
        check_vma=False,
    )
```

```python
import functools

import jax
import jax.numpy as jnp
from jax import lax
from jax.experimental import pallas as pl
from jax.experimental.pallas import tpu as pltpu
from jax.sharding import PartitionSpec as P

HEAD_DIM = 128
BLOCK = 64
SCALE = HEAD_DIM**-0.5
CAP = 2
PICK, WANT, ENTRY = 0, 32, 64
LANES = 128
VMEM_LIMIT = 64 * 1024 * 1024
MESH = pl.DeviceIdType.MESH
f32 = jnp.float32
bf16 = jnp.bfloat16


class Place:
    def __init__(self, dims):
        self.Z, self.P, self.Y, self.L = dims
        seq, dp = lax.axis_index("seq"), lax.axis_index("dp")
        self.seq, self.dp = seq, dp
        self.z, self.p = seq // self.P, seq % self.P
        self.y, self.l = dp // self.L, dp % self.L

    def at_z(self, j):
        return {"seq": (self.z + j) % self.Z * self.P + self.p, "dp": self.dp}

    def at_p(self, j):
        return {"seq": self.z * self.P + (self.p + j) % self.P, "dp": self.dp}

    def at_y(self, j):
        return {"seq": self.seq, "dp": (self.y + j) % self.Y * self.L + self.l}

    def at_l(self, j):
        return {"seq": self.seq, "dp": self.y * self.L + (self.l + j) % self.L}

    def at_s(self, j):
        return {"seq": (self.seq + j) % (self.Z * self.P), "dp": self.dp}

    def signal(self):
        partners = (
            [self.at_p(j) for j in range(1, self.P)]
            + [self.at_z(j) for j in range(1, self.Z)]
            + [self.at_y(j) for j in range(1, self.Y)]
            + [self.at_l(j) for j in range(1, self.L)]
            + [self.at_s(1), self.at_s(-1)]
        )
        barrier = pltpu.get_barrier_semaphore()
        for partner in partners:
            pl.semaphore_signal(barrier, inc=1, device_id=partner, device_id_type=MESH)
        return len(partners)

    def wait(self, count):
        pl.semaphore_wait(pltpu.get_barrier_semaphore(), count)


class Wire:
    def __init__(self, send_sems, recv_sems):
        self.send_sems, self.recv_sems = send_sems, recv_sems
        self.used = 0
        self.sent = []

    def send(self, src, dst, target):
        copy = pltpu.make_async_remote_copy(
            src_ref=src,
            dst_ref=dst,
            send_sem=self.send_sems.at[self.used],
            recv_sem=self.recv_sems.at[self.used],
            device_id=target,
            device_id_type=MESH,
        )
        self.used += 1
        copy.start()
        self.sent.append(copy)
        return copy

    def finish(self):
        for copy in self.sent:
            copy.wait_send()


def kernel(
    dims, q, k, v, w, go, wanted, shared,
    out, dq, dk, dv,
    qv, kblk, vblk, wv, gov, ivec, idx, edge,
    km, vm, kp, vp, k2, v2, sb0, sb1, sb2, sb3, rnd, halo, glob,
    gcand, ga, gmine, gb, gpiece, wcol, wall, ps, pr, ysum, lr, gctx,
    kcat, vcat, probs32, fr, ctx, own, sb, eout, gsum,
    ehalo, ar0, ar1, ar2, ar3, selects, p1, p2, p3, fm, fp, rm, rp,
    sa, smine, sg, spiece, sall, cr,
    send_sems, recv_sems, local_sems,
):
    me = Place(dims)
    Z, PN, Y, L = dims
    wire = Wire(send_sems, recv_sems)
    blocks = k.shape[0]
    entries = 3 * blocks
    half = go.shape[0] // 2
    piece = glob.shape[1]
    pieces = BLOCK // piece
    skip = PN * CAP

    local = [
        pltpu.make_async_copy(src, dst, local_sems.at[i])
        for i, (src, dst) in enumerate(((k, kblk), (v, vblk), (w, wv), (go, gov), (q, qv)))
    ]
    for copy in local:
        copy.start()
    partners = me.signal()

    want = wanted[...]
    lane = lax.broadcasted_iota(jnp.int32, want.shape, 1)
    owner = lax.shift_right_arithmetic(want, blocks.bit_length() - 1)
    rank = jnp.zeros_like(want)
    for e in range(entries):
        at = WANT + e
        rank = rank + jnp.where((owner == owner[:, at : at + 1]) & (lane > at), 1, 0)
    rank = jnp.minimum(rank, CAP - 1)
    listed = (lane >= WANT) & (lane < WANT + entries)
    table = jnp.zeros_like(want)
    for i, rel in enumerate((0, Z - 1, 1, 2)):
        column = (me.z + rel) % Z * PN + me.p
        for c in range(CAP):
            hit = listed & (owner == column) & (rank == c)
            found = jnp.where(hit, (want & (blocks - 1)) + 1, 0)
            found = jnp.minimum(jnp.sum(found, axis=1, keepdims=True), blocks) - 1
            table = jnp.where(lane == PICK + i * CAP + c, found, table)
    back = (lax.shift_right_arithmetic(owner, PN.bit_length() - 1) - me.z) & (Z - 1)
    order_of = jnp.where(back == 0, 0, jnp.where(back == 1, 2, jnp.where(back == 2, 3, 1)))
    flat = (order_of * PN + (owner & (PN - 1))) * CAP + rank
    table = jnp.where(listed, flat, table)
    slot_entry = jnp.full_like(want, entries)
    for e in range(entries):
        at = WANT + e
        slot_entry = jnp.where(lane - ENTRY == flat[:, at : at + 1], e, slot_entry)
    ivec[...] = jnp.where(lane >= ENTRY, slot_entry, table)
    to_scalars = pltpu.make_async_copy(ivec, idx, local_sems.at[5])
    to_scalars.start()

    for copy in local:
        copy.wait()
    edge[0, 0] = kblk[blocks - 1]
    edge[0, 1] = vblk[blocks - 1]
    edge[1, 0] = kblk[0]
    edge[1, 1] = vblk[0]
    g_seq = [shared[j] // blocks for j in range(2)]
    g_block = [shared[j] % blocks for j in range(2)]
    for j in range(2):
        for part, source in ((0, kblk), (1, vblk)):
            first = (j * 2 + part) * pieces
            gcand[first : first + pieces] = source[g_block[j]].reshape(pieces, piece, HEAD_DIM)
    to_scalars.wait()
    me.wait(partners)

    w_z = [wire.send(w, wcol.at[me.z], me.at_z(j)) for j in range(1, Z)]
    w_p = [wire.send(w, wall.at[me.z, me.p], me.at_p(j)) for j in range(1, PN)]
    g_a = [
        wire.send(gcand.at[(me.p + j) % PN], ga.at[me.p], me.at_p(j)) for j in range(1, PN)
    ]
    edges = [
        wire.send(edge.at[0], halo.at[0], me.at_s(1)),
        wire.send(edge.at[1], halo.at[1], me.at_s(-1)),
    ]
    k_up = wire.send(k, km, me.at_z(1))
    k_down = wire.send(k, kp, me.at_z(-1))
    v_up = wire.send(v, vm, me.at_z(1))
    v_down = wire.send(v, vp, me.at_z(-1))
    arrivals = []

    def pack(at, part, source, buffer):
        for requester in range(PN):
            for c in range(CAP):
                block = jnp.maximum(idx[requester, PICK + at * CAP + c], 0)
                buffer[part, requester, c] = source(block)
        rnd[pl.ds((at * 2 + part) * skip + me.p * CAP, CAP)] = buffer[part, pl.ds(me.p, 1)][0]
        for j in range(1, PN):
            arrivals.append(
                wire.send(
                    buffer.at[part, (me.p + j) % PN],
                    rnd.at[pl.ds((at * 2 + part) * skip + me.p * CAP, CAP)],
                    me.at_p(j),
                )
            )


    wcol[pl.ds(me.z, 1)] = wv[...][None]
    for j in (1, Z - 1, *range(2, Z - 1)):
        w_z[j - 1].wait_recv()
        source = (me.z + Z - j) % Z
        w_p += [
            wire.send(wcol.at[source], wall.at[source, me.p], me.at_p(i)) for i in range(1, PN)
        ]
    wall[:, pl.ds(me.p, 1)] = wcol[...][:, None]

    pack(0, 0, lambda b: kblk[b], sb0)
    pack(0, 1, lambda b: vblk[b], sb0)

    ga[pl.ds(me.p, 1)] = gcand[pl.ds(me.p, 1)]
    for copy in g_a:
        copy.wait_recv()
    own_half = (me.p // (PN // 2)) % 2
    gmine[...] = ga[jnp.where(own_half == 0, g_seq[0] % PN, g_seq[1] % PN)]
    g_b = [wire.send(gmine, gb.at[j], me.at_z(j)) for j in range(1, Z)]

    row = lax.broadcasted_iota(jnp.int32, (16, blocks * 16), 0)
    col = lax.broadcasted_iota(jnp.int32, (16, blocks * 16), 1)
    diagonal = col % 16 == row
    for at in range(4):
        for slot in range(skip):
            block = idx[slot // CAP, PICK + at * CAP + slot % CAP]
            hit = diagonal & (col // 16 == block)
            selects[at, slot * 16 : (slot + 1) * 16] = jnp.where(hit, 1.0, 0.0).astype(bf16)

    for copy in w_p:
        copy.wait_recv()
    chunk_z = Z // Y
    width = L * HEAD_DIM
    y_sends = []
    y_order = sorted(range(Y), key=lambda j: -min(j, Y - j))
    for part in range(2):
        rows = gov[part * half : (part + 1) * half]
        for j in y_order:
            to = (me.y + j) % Y
            weight = wall[pl.ds(to * chunk_z, chunk_z)].reshape(width, HEAD_DIM)
            terms = lax.dot_general(
                rows, weight, (((1,), (1,)), ((), ())), preferred_element_type=f32
            ).astype(bf16)
            for head in range(L):
                ps[part, j, head] = terms[:, head * HEAD_DIM : (head + 1) * HEAD_DIM]
            if j:
                y_sends.append(wire.send(ps.at[part, j], pr.at[part, j - 1], me.at_y(j)))

    low, high = pl.ds(0, blocks // 2), pl.ds(blocks // 2, blocks - blocks // 2)

    def forward(lower, upper, far):
        return [
            wire.send(lower.at[low], far.at[low], me.at_z(1)),
            wire.send(upper.at[high], far.at[high], me.at_z(-1)),
        ]

    def y_stage(part):
        for copy in y_sends[part * (Y - 1) : (part + 1) * (Y - 1)]:
            copy.wait_recv()
        for head in range(L):
            total = ps[part, 0, head].astype(f32)
            for j in range(1, Y):
                total = total + pr[part, j - 1, head].astype(f32)
            ysum[part, head] = total.astype(bf16)
        return [
            wire.send(ysum.at[part, (me.l + j) % L], lr.at[part, j - 1], me.at_l(j))
            for j in range(1, L)
        ]

    k_up.wait_recv()
    k_down.wait_recv()
    k_far = forward(km, kp, k2)
    pack(1, 0, lambda b: km[b], sb1)
    pack(2, 0, lambda b: kp[b], sb2)
    v_up.wait_recv()
    v_down.wait_recv()
    v_far = forward(vm, vp, v2)
    pack(1, 1, lambda b: vm[b], sb1)
    pack(2, 1, lambda b: vp[b], sb2)
    gb[0] = gmine[...]
    for copy in g_b:
        copy.wait_recv()
    g_rel = [(me.z - g_seq[j] // PN + Z) % Z for j in range(2)]
    gpiece[...] = gb[jnp.where(own_half == 0, g_rel[0], g_rel[1])]
    glob[pl.ds(me.p, 1)] = gpiece[...][None]
    g_c = [wire.send(gpiece, glob.at[me.p], me.at_p(j)) for j in range(1, PN)]
    for copy in k_far:
        copy.wait_recv()
    pack(3, 0, lambda b: k2[b], sb3)
    l_sends = [y_stage(0)]
    for copy in v_far:
        copy.wait_recv()
    pack(3, 1, lambda b: v2[b], sb3)
    l_sends.append(y_stage(1))
    for copy in edges + g_c + arrivals:
        copy.wait_recv()

    def window(b, part, source):
        before = halo[0, part] if b == 0 else source[b - 1]
        after = halo[1, part] if b == blocks - 1 else source[b + 1]
        return [before, source[b], after]

    def dot(a, b, dims):
        return lax.dot_general(a, b, (dims, ((), ())), preferred_element_type=f32)

    nt, nn, tn = ((1,), (1,)), ((1,), (0,)), ((0,), (0,))
    everyone = glob[...].reshape(2, 2, BLOCK, HEAD_DIM)
    span = [slice(b * BLOCK, (b + 1) * BLOCK) for b in range(blocks)]
    for b in range(blocks):
        slots = []
        for i in range(3):
            flat_slot = idx[me.p, WANT + b * 3 + i]
            slots.append(flat_slot + flat_slot // skip * skip)
        keys = jnp.concatenate(
            window(b, 0, kblk) + [everyone[0, 0], everyone[1, 0]] + [rnd[s] for s in slots],
            axis=0,
        )
        values = jnp.concatenate(
            window(b, 1, vblk) + [everyone[0, 1], everyone[1, 1]] + [rnd[s + skip] for s in slots],
            axis=0,
        )
        kcat[b] = keys
        vcat[b] = values
        scores = dot(qv[span[b]], keys, nt) * SCALE
        raised = jnp.exp(scores - jnp.max(scores, axis=-1, keepdims=True))
        probs = raised / jnp.sum(raised, axis=-1, keepdims=True)
        probs32[b] = probs
        ctx[span[b]] = dot(probs.astype(bf16), values, nn).astype(bf16)

    l_in = [wire.send(ctx, cr.at[me.y, me.l], me.at_l(j)) for j in range(1, L)]
    y_in = [wire.send(ctx, cr.at[me.y, me.l], me.at_y(j)) for j in range(1, Y)]
    cr[pl.ds(me.y, 1), pl.ds(me.l, 1)] = ctx[...][None, None]
    for part in range(2):
        for copy in l_sends[part]:
            copy.wait_recv()
        total = ysum[part, pl.ds(me.l, 1)][0].astype(f32)
        for j in range(1, L):
            total = total + lr[part, j - 1].astype(f32)
        gctx[part * half : (part + 1) * half] = total.astype(bf16)

    acc = {}
    total = [jnp.zeros((2 * BLOCK, HEAD_DIM), f32) for _ in range(2)]

    def settle(at):
        for part in range(2):
            term = acc.pop((at, part))
            if at < 0:
                eout[0, part] = term.astype(bf16)
            elif at >= blocks:
                eout[1, part] = term.astype(bf16)
            else:
                own[part, at] = term

    fr[entries] = jnp.zeros(fr.shape[1:], bf16)
    for b in range(blocks):
        qb, gb_rows = qv[span[b]], gctx[span[b]]
        probs = probs32[b]
        keys, values = kcat[b], vcat[b]
        delta = jnp.sum(
            gb_rows.astype(f32) * ctx[span[b]].astype(f32), axis=-1, keepdims=True
        )
        gscores = (probs * (dot(gb_rows, values, nt) - delta)).astype(bf16)
        dq[span[b]] = (dot(gscores, keys, nn) * SCALE).astype(bf16)
        for part, term in (
            (0, dot(gscores, qb, tn) * SCALE),
            (1, dot(probs.astype(bf16), gb_rows, tn)),
        ):
            for i in range(3):
                at = (b - 1 + i, part)
                one = term[i * BLOCK : (i + 1) * BLOCK]
                acc[at] = acc[at] + one if at in acc else one
            total[part] = total[part] + term[3 * BLOCK : 5 * BLOCK]
            for i in range(3):
                fr[b * 3 + i, part] = term[(5 + i) * BLOCK : (6 + i) * BLOCK].astype(bf16)
        settle(b - 1)
    settle(blocks - 1)
    settle(blocks)

    landing = (ar0, ar1, ar2, ar3)
    returned = {}

    def spread(at, part):
        for slot in range(skip):
            entry = idx[me.p, ENTRY + at * skip + slot]
            sb[at, part, slot // CAP, slot % CAP] = fr[entry, part]
        landing[at][part, pl.ds(me.p, 1)] = sb[at, part, pl.ds(me.p, 1)]
        returned[at, part] = [
            wire.send(sb.at[at, part, (me.p + j) % PN], landing[at].at[part, me.p], me.at_p(j))
            for j in range(1, PN)
        ]

    spread(3, 0)
    spread(3, 1)
    for j in range(2):
        for part in range(2):
            first = (j * 2 + part) * pieces
            gsum[first : first + pieces] = (
                total[part][j * BLOCK : (j + 1) * BLOCK]
                .astype(bf16)
                .reshape(pieces, piece, HEAD_DIM)
            )
    s_a = [
        wire.send(gsum.at[(me.p + j) % PN], sa.at[me.p], me.at_p(j)) for j in range(1, PN)
    ]
    edges = [
        wire.send(eout.at[0], ehalo.at[1], me.at_s(-1)),
        wire.send(eout.at[1], ehalo.at[0], me.at_s(1)),
    ]
    for at, part in ((1, 0), (2, 1), (1, 1), (2, 0), (0, 0), (0, 1)):
        spread(at, part)

    def gather_sum(at, part):
        for copy in returned[at, part]:
            copy.wait_recv()
        sums = []
        for r in range(BLOCK // 16):
            data = landing[at][part, :, :, r * 16 : (r + 1) * 16].reshape(skip * 16, HEAD_DIM)
            sums.append(dot(selects[at], data, tn).reshape(blocks, 16, HEAD_DIM))
        return jnp.concatenate(sums, axis=1)

    p2[0] = gather_sum(3, 0).astype(bf16)
    far_up = wire.send(p2.at[0], fm, me.at_z(1))
    p2[1] = gather_sum(3, 1).astype(bf16)
    far_down = wire.send(p2.at[1], fp, me.at_z(-1))

    for copy in s_a:
        copy.wait_recv()
    sa[pl.ds(me.p, 1)] = gsum[pl.ds(me.p, 1)]
    smine[...] = jnp.sum(sa[...].astype(f32), axis=0).astype(bf16)
    s_b = [wire.send(smine, sg.at[j - 1], me.at_z(j)) for j in range(1, Z)]

    p3[0] = gather_sum(1, 0).astype(bf16)
    k_down = wire.send(p3.at[0], rp.at[0], me.at_z(-1))
    p1[1] = gather_sum(2, 1).astype(bf16)
    v_up = wire.send(p1.at[1], rm.at[1], me.at_z(1))
    for j in range(1, L):
        l_in[j - 1].wait_recv()
        source = (me.l + L - j) % L
        for i in range(1, Y):
            y_in.append(wire.send(cr.at[me.y, source], cr.at[me.y, source], me.at_y(i)))
    down = gather_sum(1, 1)
    up = gather_sum(2, 0)
    far_up.wait_recv()
    p1[0] = (up + fm[...].astype(f32)).astype(bf16)
    k_up = wire.send(p1.at[0], rm.at[0], me.at_z(1))
    far_down.wait_recv()
    p3[1] = (down + fp[...].astype(f32)).astype(bf16)
    v_down = wire.send(p3.at[1], rp.at[1], me.at_z(-1))

    for copy in s_b:
        copy.wait_recv()
    spiece[...] = (
        smine[...].astype(f32) + jnp.sum(sg[...].astype(f32), axis=0)
    ).astype(bf16)
    sall[pl.ds(me.p, 1)] = spiece[...][None]
    s_c = [wire.send(spiece, sall.at[me.p], me.at_p(j)) for j in range(1, PN)]

    totals = [gather_sum(0, part) + own[part] for part in range(2)]
    for copy in y_in:
        copy.wait_recv()
    full = jnp.concatenate([cr[d // L, d % L] for d in range(Y * L)], axis=1)
    out[...] = dot(full, wall[...].reshape(-1, HEAD_DIM), nn).astype(bf16)

    for copy in edges + s_c:
        copy.wait_recv()
    everyone = sall[...].reshape(2, 2, BLOCK, HEAD_DIM).astype(f32)
    g_here = [jnp.where(g_seq[j] == me.seq, g_block[j], -1) for j in range(2)]
    for part in range(2):
        ones = []
        for b in range(blocks):
            one = totals[part][b]
            for j in range(2):
                one = one + jnp.where(g_here[j] == b, everyone[j, part], 0.0)
            if b == 0:
                one = one + ehalo[0, part].astype(f32)
            if b == blocks - 1:
                one = one + ehalo[1, part].astype(f32)
            ones.append(one[None])
        totals[part] = jnp.concatenate(ones, axis=0)
    for copy in (v_up, k_down, k_up, v_down):
        copy.wait_recv()
    for part, target in ((0, dk), (1, dv)):
        total = totals[part] + (rm[part].astype(f32) + rp[part].astype(f32))
        target[...] = total.reshape(target.shape).astype(bf16)
    wire.finish()


def settle_kernel(*refs):
    for source, target in zip(refs[:4], refs[4:]):
        target[...] = source[...]


def per_device(dims, queries, keys, values, out_weight, grad_out, pattern):
    Z, PN, Y, L = dims
    me = Place(dims)
    tokens = queries.shape[0]
    blocks = tokens // BLOCK
    entries = 3 * blocks
    rows = out_weight.shape[0]
    piece = 4 * BLOCK // PN
    half = tokens // 2
    block = (BLOCK, HEAD_DIM)
    in_hbm = pl.BlockSpec(memory_space=pltpu.HBM)
    in_vmem = pl.BlockSpec(memory_space=pltpu.VMEM)
    shape = jax.ShapeDtypeStruct

    plane = lax.dynamic_slice(
        pattern, (me.dp, me.z * PN * blocks, 0), (1, PN * blocks, pattern.shape[2])
    )[0]
    wanted = jnp.pad(
        plane[:, 2:].reshape(PN, entries),
        ((0, 0), (WANT, LANES - WANT - entries)),
        constant_values=-1,
    )

    def buffer(*dims, dtype=bf16):
        return pltpu.VMEM(dims, dtype)

    keyed = buffer(blocks, *block)
    slots = buffer(2, PN, CAP, *block)
    pairs = buffer(2, 2, *block)
    whole = buffer(2, blocks, *block)
    small = buffer(piece, HEAD_DIM)
    spread_small = buffer(PN, piece, HEAD_DIM)
    out, dq, dk, dv = pl.pallas_call(
        functools.partial(kernel, dims),
        out_shape=(shape((tokens, HEAD_DIM), bf16),) * 4,
        in_specs=[in_hbm] * 5 + [in_vmem, pl.BlockSpec(memory_space=pltpu.SMEM)],
        out_specs=(in_vmem,) * 4,
        scratch_shapes=[
            buffer(tokens, HEAD_DIM), keyed, keyed, buffer(rows, HEAD_DIM),
            buffer(tokens, HEAD_DIM), buffer(PN, LANES, dtype=jnp.int32),
            pltpu.SMEM((PN, LANES), jnp.int32), pairs,
            keyed, keyed, keyed, keyed, keyed, keyed, slots, slots, slots, slots,
            buffer(8 * PN * CAP, *block), pairs, spread_small,
            spread_small, spread_small, small, buffer(Z, piece, HEAD_DIM), small,
            buffer(Z, rows, HEAD_DIM), buffer(Z, PN, rows, HEAD_DIM),
            buffer(2, Y, L, half, HEAD_DIM), buffer(2, max(Y - 1, 1), L, half, HEAD_DIM),
            buffer(2, L, half, HEAD_DIM), buffer(2, max(L - 1, 1), half, HEAD_DIM),
            buffer(tokens, HEAD_DIM),
            buffer(blocks, 8 * BLOCK, HEAD_DIM), buffer(blocks, 8 * BLOCK, HEAD_DIM),
            buffer(blocks, BLOCK, 8 * BLOCK, dtype=f32), buffer(entries + 1, 2, *block),
            buffer(tokens, HEAD_DIM), buffer(2, blocks, *block, dtype=f32),
            buffer(4, 2, PN, CAP, *block), pairs, spread_small,
            pairs, slots, slots, slots, slots,
            buffer(4, PN * CAP * 16, blocks * 16),
            whole, whole, whole, keyed, keyed, whole, whole,
            spread_small, small, buffer(Z - 1, piece, HEAD_DIM), small, spread_small,
            buffer(Y, L, tokens, HEAD_DIM),
            pltpu.SemaphoreType.DMA((256,)),
            pltpu.SemaphoreType.DMA((256,)),
            pltpu.SemaphoreType.DMA((6,)),
        ],
        compiler_params=pltpu.CompilerParams(
            collective_id=0, has_side_effects=True, vmem_limit_bytes=VMEM_LIMIT
        ),
    )(
        queries, keys.reshape((blocks,) + block), values.reshape((blocks,) + block),
        out_weight, grad_out, wanted, plane[0, :2],
    )
    return pl.pallas_call(
        settle_kernel,
        out_shape=(shape((tokens, HEAD_DIM), bf16),) * 4,
        in_specs=[in_vmem] * 4,
        out_specs=(in_vmem,) * 4,
        compiler_params=pltpu.CompilerParams(vmem_limit_bytes=VMEM_LIMIT),
    )(out, dq, dk, dv)


def solution(mesh, planes=8, lines=4):
    seq, dp = mesh.shape["seq"], mesh.shape["dp"]
    dims = (seq // planes, planes, dp // lines, lines)
    tile = P("seq", "dp")
    return jax.shard_map(
        functools.partial(per_device, dims),
        mesh=mesh,
        in_specs=(tile,) * 5 + (P(),),
        out_specs=(tile,) * 4,
        check_vma=False,
    )
```

```python
import functools

import jax
import jax.numpy as jnp
from jax import lax
from jax.experimental import pallas as pl
from jax.experimental.pallas import tpu as pltpu
from jax.sharding import PartitionSpec as P

HEAD_DIM = 128
BLOCK = 64
SCALE = HEAD_DIM**-0.5
CAP = 2
PICK, WANT, ENTRY = 0, 32, 64
LANES = 128
VMEM_LIMIT = 64 * 1024 * 1024
MESH = pl.DeviceIdType.MESH
f32 = jnp.float32
bf16 = jnp.bfloat16


class Place:
    def __init__(self, dims):
        self.Z, self.P, self.Y, self.L = dims
        seq, dp = lax.axis_index("seq"), lax.axis_index("dp")
        self.seq, self.dp = seq, dp
        self.z, self.p = seq // self.P, seq % self.P
        self.y, self.l = dp // self.L, dp % self.L

    def at_z(self, j):
        return {"seq": (self.z + j) % self.Z * self.P + self.p, "dp": self.dp}

    def at_p(self, j):
        return {"seq": self.z * self.P + (self.p + j) % self.P, "dp": self.dp}

    def at_y(self, j):
        return {"seq": self.seq, "dp": (self.y + j) % self.Y * self.L + self.l}

    def at_l(self, j):
        return {"seq": self.seq, "dp": self.y * self.L + (self.l + j) % self.L}

    def at_s(self, j):
        return {"seq": (self.seq + j) % (self.Z * self.P), "dp": self.dp}

    def signal(self):
        partners = (
            [self.at_p(j) for j in range(1, self.P)]
            + [self.at_z(j) for j in range(1, self.Z)]
            + [self.at_y(j) for j in range(1, self.Y)]
            + [self.at_l(j) for j in range(1, self.L)]
            + [self.at_s(1), self.at_s(-1)]
        )
        barrier = pltpu.get_barrier_semaphore()
        for partner in partners:
            pl.semaphore_signal(barrier, inc=1, device_id=partner, device_id_type=MESH)
        return len(partners)

    def wait(self, count):
        pl.semaphore_wait(pltpu.get_barrier_semaphore(), count)


class Wire:
    def __init__(self, send_sems, recv_sems):
        self.send_sems, self.recv_sems = send_sems, recv_sems
        self.used = 0
        self.sent = []

    def send(self, src, dst, target):
        copy = pltpu.make_async_remote_copy(
            src_ref=src,
            dst_ref=dst,
            send_sem=self.send_sems.at[self.used],
            recv_sem=self.recv_sems.at[self.used],
            device_id=target,
            device_id_type=MESH,
        )
        self.used += 1
        copy.start()
        self.sent.append(copy)
        return copy

    def finish(self):
        for copy in self.sent:
            copy.wait_send()


def kernel(
    dims, q, k, v, w, go, wanted, shared,
    out, dq, dk, dv,
    qv, kblk, vblk, wv, gov, ivec, idx, edge,
    km, vm, kp, vp, k2, v2, sb0, sb1, sb2, sb3, rnd, halo, glob,
    gcand, ga, gmine, gb, gpiece, wcol, wall, ps, pr, ysum, lr, gctx,
    kcat, vcat, probs32, fr, ctx, own, sb, eout, gsum,
    ehalo, ar0, ar1, ar2, ar3, selects, p1, p2, p3, fm, fp, rm, rp,
    sa, smine, sg, spiece, sall, cr,
    send_sems, recv_sems, local_sems,
):
    me = Place(dims)
    Z, PN, Y, L = dims
    wire = Wire(send_sems, recv_sems)
    blocks = k.shape[0]
    entries = 3 * blocks
    half = go.shape[0] // 2
    piece = glob.shape[1]
    pieces = BLOCK // piece
    skip = PN * CAP

    local = [
        pltpu.make_async_copy(src, dst, local_sems.at[i])
        for i, (src, dst) in enumerate(((k, kblk), (v, vblk), (w, wv), (go, gov), (q, qv)))
    ]
    for copy in local:
        copy.start()
    partners = me.signal()

    want = wanted[...]
    lane = lax.broadcasted_iota(jnp.int32, want.shape, 1)
    owner = lax.shift_right_arithmetic(want, blocks.bit_length() - 1)
    rank = jnp.zeros_like(want)
    for e in range(entries):
        at = WANT + e
        rank = rank + jnp.where((owner == owner[:, at : at + 1]) & (lane > at), 1, 0)
    rank = jnp.minimum(rank, CAP - 1)
    listed = (lane >= WANT) & (lane < WANT + entries)
    table = jnp.zeros_like(want)
    for i, rel in enumerate((0, Z - 1, 1, 2)):
        column = (me.z + rel) % Z * PN + me.p
        for c in range(CAP):
            hit = listed & (owner == column) & (rank == c)
            found = jnp.where(hit, (want & (blocks - 1)) + 1, 0)
            found = jnp.minimum(jnp.sum(found, axis=1, keepdims=True), blocks) - 1
            table = jnp.where(lane == PICK + i * CAP + c, found, table)
    back = (lax.shift_right_arithmetic(owner, PN.bit_length() - 1) - me.z) & (Z - 1)
    order_of = jnp.where(back == 0, 0, jnp.where(back == 1, 2, jnp.where(back == 2, 3, 1)))
    flat = (order_of * PN + (owner & (PN - 1))) * CAP + rank
    table = jnp.where(listed, flat, table)
    slot_entry = jnp.full_like(want, entries)
    for e in range(entries):
        at = WANT + e
        slot_entry = jnp.where(lane - ENTRY == flat[:, at : at + 1], e, slot_entry)
    ivec[...] = jnp.where(lane >= ENTRY, slot_entry, table)
    to_scalars = pltpu.make_async_copy(ivec, idx, local_sems.at[5])
    to_scalars.start()

    for copy in local:
        copy.wait()
    edge[0, 0] = kblk[blocks - 1]
    edge[0, 1] = vblk[blocks - 1]
    edge[1, 0] = kblk[0]
    edge[1, 1] = vblk[0]
    g_seq = [shared[j] // blocks for j in range(2)]
    g_block = [shared[j] % blocks for j in range(2)]
    for j in range(2):
        for part, source in ((0, kblk), (1, vblk)):
            first = (j * 2 + part) * pieces
            gcand[first : first + pieces] = source[g_block[j]].reshape(pieces, piece, HEAD_DIM)
    to_scalars.wait()
    me.wait(partners)

    w_z = [wire.send(w, wcol.at[me.z], me.at_z(j)) for j in range(1, Z)]
    g_a = [
        wire.send(gcand.at[(me.p + j) % PN], ga.at[me.p], me.at_p(j)) for j in range(1, PN)
    ]
    edges = [
        wire.send(edge.at[0], halo.at[0], me.at_s(1)),
        wire.send(edge.at[1], halo.at[1], me.at_s(-1)),
    ]
    k_up = wire.send(k, km, me.at_z(1))
    k_down = wire.send(k, kp, me.at_z(-1))
    v_up = wire.send(v, vm, me.at_z(1))
    v_down = wire.send(v, vp, me.at_z(-1))
    arrivals = []

    def pack(at, part, source, buffer):
        for requester in range(PN):
            for c in range(CAP):
                block = jnp.maximum(idx[requester, PICK + at * CAP + c], 0)
                buffer[part, requester, c] = source(block)
        rnd[pl.ds((at * 2 + part) * skip + me.p * CAP, CAP)] = buffer[part, pl.ds(me.p, 1)][0]
        for j in range(1, PN):
            arrivals.append(
                wire.send(
                    buffer.at[part, (me.p + j) % PN],
                    rnd.at[pl.ds((at * 2 + part) * skip + me.p * CAP, CAP)],
                    me.at_p(j),
                )
            )


    wcol[pl.ds(me.z, 1)] = wv[...][None]
    for copy in w_z:
        copy.wait_recv()
    wall[:, pl.ds(me.p, 1)] = wcol[...][:, None]
    w_p = [wire.send(wcol, wall.at[:, me.p], me.at_p(j)) for j in range(1, PN)]

    pack(0, 0, lambda b: kblk[b], sb0)
    pack(0, 1, lambda b: vblk[b], sb0)

    ga[pl.ds(me.p, 1)] = gcand[pl.ds(me.p, 1)]
    for copy in g_a:
        copy.wait_recv()
    own_half = (me.p // (PN // 2)) % 2
    gmine[...] = ga[jnp.where(own_half == 0, g_seq[0] % PN, g_seq[1] % PN)]
    g_b = [wire.send(gmine, gb.at[j], me.at_z(j)) for j in range(1, Z)]

    row = lax.broadcasted_iota(jnp.int32, (16, blocks * 16), 0)
    col = lax.broadcasted_iota(jnp.int32, (16, blocks * 16), 1)
    diagonal = col % 16 == row
    for at in range(4):
        for slot in range(skip):
            block = idx[slot // CAP, PICK + at * CAP + slot % CAP]
            hit = diagonal & (col // 16 == block)
            selects[at, slot * 16 : (slot + 1) * 16] = jnp.where(hit, 1.0, 0.0).astype(bf16)

    for copy in w_p:
        copy.wait_recv()
    chunk_z = Z // Y
    width = L * HEAD_DIM
    y_sends = []
    for part in range(2):
        rows = gov[part * half : (part + 1) * half]
        for j in list(range(1, Y)) + [0]:
            to = (me.y + j) % Y
            weight = wall[pl.ds(to * chunk_z, chunk_z)].reshape(width, HEAD_DIM)
            terms = lax.dot_general(
                rows, weight, (((1,), (1,)), ((), ())), preferred_element_type=f32
            ).astype(bf16)
            for head in range(L):
                ps[part, j, head] = terms[:, head * HEAD_DIM : (head + 1) * HEAD_DIM]
            if j:
                y_sends.append(wire.send(ps.at[part, j], pr.at[part, j - 1], me.at_y(j)))

    low, high = pl.ds(0, blocks // 2), pl.ds(blocks // 2, blocks - blocks // 2)

    def forward(lower, upper, far):
        return [
            wire.send(lower.at[low], far.at[low], me.at_z(1)),
            wire.send(upper.at[high], far.at[high], me.at_z(-1)),
        ]

    def y_stage(part):
        for copy in y_sends[part * (Y - 1) : (part + 1) * (Y - 1)]:
            copy.wait_recv()
        for head in range(L):
            total = ps[part, 0, head].astype(f32)
            for j in range(1, Y):
                total = total + pr[part, j - 1, head].astype(f32)
            ysum[part, head] = total.astype(bf16)
        return [
            wire.send(ysum.at[part, (me.l + j) % L], lr.at[part, j - 1], me.at_l(j))
            for j in range(1, L)
        ]

    k_up.wait_recv()
    k_down.wait_recv()
    k_far = forward(km, kp, k2)
    pack(1, 0, lambda b: km[b], sb1)
    pack(2, 0, lambda b: kp[b], sb2)
    v_up.wait_recv()
    v_down.wait_recv()
    v_far = forward(vm, vp, v2)
    pack(1, 1, lambda b: vm[b], sb1)
    pack(2, 1, lambda b: vp[b], sb2)
    gb[0] = gmine[...]
    for copy in g_b:
        copy.wait_recv()
    g_rel = [(me.z - g_seq[j] // PN + Z) % Z for j in range(2)]
    gpiece[...] = gb[jnp.where(own_half == 0, g_rel[0], g_rel[1])]
    glob[pl.ds(me.p, 1)] = gpiece[...][None]
    g_c = [wire.send(gpiece, glob.at[me.p], me.at_p(j)) for j in range(1, PN)]
    for copy in k_far:
        copy.wait_recv()
    pack(3, 0, lambda b: k2[b], sb3)
    l_sends = [y_stage(0)]
    for copy in v_far:
        copy.wait_recv()
    pack(3, 1, lambda b: v2[b], sb3)
    l_sends.append(y_stage(1))
    for copy in edges + g_c + arrivals:
        copy.wait_recv()

    def window(b, part, source):
        before = halo[0, part] if b == 0 else source[b - 1]
        after = halo[1, part] if b == blocks - 1 else source[b + 1]
        return [before, source[b], after]

    def dot(a, b, dims):
        return lax.dot_general(a, b, (dims, ((), ())), preferred_element_type=f32)

    nt, nn, tn = ((1,), (1,)), ((1,), (0,)), ((0,), (0,))
    everyone = glob[...].reshape(2, 2, BLOCK, HEAD_DIM)
    span = [slice(b * BLOCK, (b + 1) * BLOCK) for b in range(blocks)]
    for b in range(blocks):
        slots = []
        for i in range(3):
            flat_slot = idx[me.p, WANT + b * 3 + i]
            slots.append(flat_slot + flat_slot // skip * skip)
        keys = jnp.concatenate(
            window(b, 0, kblk) + [everyone[0, 0], everyone[1, 0]] + [rnd[s] for s in slots],
            axis=0,
        )
        values = jnp.concatenate(
            window(b, 1, vblk) + [everyone[0, 1], everyone[1, 1]] + [rnd[s + skip] for s in slots],
            axis=0,
        )
        kcat[b] = keys
        vcat[b] = values
        scores = dot(qv[span[b]], keys, nt) * SCALE
        raised = jnp.exp(scores - jnp.max(scores, axis=-1, keepdims=True))
        probs = raised / jnp.sum(raised, axis=-1, keepdims=True)
        probs32[b] = probs
        ctx[span[b]] = dot(probs.astype(bf16), values, nn).astype(bf16)

    l_in = [wire.send(ctx, cr.at[me.y, me.l], me.at_l(j)) for j in range(1, L)]
    y_in = [wire.send(ctx, cr.at[me.y, me.l], me.at_y(j)) for j in range(1, Y)]
    cr[pl.ds(me.y, 1), pl.ds(me.l, 1)] = ctx[...][None, None]
    for part in range(2):
        for copy in l_sends[part]:
            copy.wait_recv()
        total = ysum[part, pl.ds(me.l, 1)][0].astype(f32)
        for j in range(1, L):
            total = total + lr[part, j - 1].astype(f32)
        gctx[part * half : (part + 1) * half] = total.astype(bf16)

    acc = {}
    total = [jnp.zeros((2 * BLOCK, HEAD_DIM), f32) for _ in range(2)]

    def settle(at, part):
        term = acc.pop((at, part))
        if at < 0:
            eout[0, part] = term.astype(bf16)
        elif at >= blocks:
            eout[1, part] = term.astype(bf16)
        else:
            own[part, at] = term

    def add_terms(b, part, term):
        for i in range(3):
            at = (b - 1 + i, part)
            one = term[i * BLOCK : (i + 1) * BLOCK]
            acc[at] = acc[at] + one if at in acc else one
        total[part] = total[part] + term[3 * BLOCK : 5 * BLOCK]
        for i in range(3):
            fr[b * 3 + i, part] = term[(5 + i) * BLOCK : (6 + i) * BLOCK].astype(bf16)
        settle(b - 1, part)
        if b == blocks - 1:
            settle(b, part)
            settle(b + 1, part)

    landing = (ar0, ar1, ar2, ar3)
    returned = {}

    def spread(at, part):
        for slot in range(skip):
            entry = idx[me.p, ENTRY + at * skip + slot]
            sb[at, part, slot // CAP, slot % CAP] = fr[entry, part]
        landing[at][part, pl.ds(me.p, 1)] = sb[at, part, pl.ds(me.p, 1)]
        returned[at, part] = [
            wire.send(sb.at[at, part, (me.p + j) % PN], landing[at].at[part, me.p], me.at_p(j))
            for j in range(1, PN)
        ]

    fr[entries] = jnp.zeros(fr.shape[1:], bf16)
    for b in range(blocks):
        add_terms(b, 1, dot(probs32[b].astype(bf16), gctx[span[b]], tn))
    spread(3, 1)
    for b in range(blocks):
        qb, gb_rows = qv[span[b]], gctx[span[b]]
        keys = kcat[b]
        delta = jnp.sum(
            gb_rows.astype(f32) * ctx[span[b]].astype(f32), axis=-1, keepdims=True
        )
        gscores = (probs32[b] * (dot(gb_rows, vcat[b], nt) - delta)).astype(bf16)
        dq[span[b]] = (dot(gscores, keys, nn) * SCALE).astype(bf16)
        add_terms(b, 0, dot(gscores, qb, tn) * SCALE)

    spread(3, 0)
    for j in range(2):
        for part in range(2):
            first = (j * 2 + part) * pieces
            gsum[first : first + pieces] = (
                total[part][j * BLOCK : (j + 1) * BLOCK]
                .astype(bf16)
                .reshape(pieces, piece, HEAD_DIM)
            )
    s_a = [
        wire.send(gsum.at[(me.p + j) % PN], sa.at[me.p], me.at_p(j)) for j in range(1, PN)
    ]
    edges = [
        wire.send(eout.at[0], ehalo.at[1], me.at_s(-1)),
        wire.send(eout.at[1], ehalo.at[0], me.at_s(1)),
    ]
    for at, part in ((1, 0), (2, 1), (1, 1), (2, 0), (0, 0), (0, 1)):
        spread(at, part)

    def gather_sum(at, part):
        for copy in returned[at, part]:
            copy.wait_recv()
        sums = []
        for r in range(BLOCK // 16):
            data = landing[at][part, :, :, r * 16 : (r + 1) * 16].reshape(skip * 16, HEAD_DIM)
            sums.append(dot(selects[at], data, tn).reshape(blocks, 16, HEAD_DIM))
        return jnp.concatenate(sums, axis=1)

    p2[1] = gather_sum(3, 1).astype(bf16)
    far_down = wire.send(p2.at[1], fp, me.at_z(-1))
    p2[0] = gather_sum(3, 0).astype(bf16)
    far_up = wire.send(p2.at[0], fm, me.at_z(1))

    for copy in s_a:
        copy.wait_recv()
    sa[pl.ds(me.p, 1)] = gsum[pl.ds(me.p, 1)]
    smine[...] = jnp.sum(sa[...].astype(f32), axis=0).astype(bf16)
    s_b = [wire.send(smine, sg.at[j - 1], me.at_z(j)) for j in range(1, Z)]

    p3[0] = gather_sum(1, 0).astype(bf16)
    k_down = wire.send(p3.at[0], rp.at[0], me.at_z(-1))
    p1[1] = gather_sum(2, 1).astype(bf16)
    v_up = wire.send(p1.at[1], rm.at[1], me.at_z(1))
    for j in range(1, L):
        l_in[j - 1].wait_recv()
        source = (me.l + L - j) % L
        for i in range(1, Y):
            y_in.append(wire.send(cr.at[me.y, source], cr.at[me.y, source], me.at_y(i)))
    down = gather_sum(1, 1)
    up = gather_sum(2, 0)
    far_up.wait_recv()
    p1[0] = (up + fm[...].astype(f32)).astype(bf16)
    k_up = wire.send(p1.at[0], rm.at[0], me.at_z(1))
    far_down.wait_recv()
    p3[1] = (down + fp[...].astype(f32)).astype(bf16)
    v_down = wire.send(p3.at[1], rp.at[1], me.at_z(-1))

    for copy in s_b:
        copy.wait_recv()
    spiece[...] = (
        smine[...].astype(f32) + jnp.sum(sg[...].astype(f32), axis=0)
    ).astype(bf16)
    sall[pl.ds(me.p, 1)] = spiece[...][None]
    s_c = [wire.send(spiece, sall.at[me.p], me.at_p(j)) for j in range(1, PN)]

    totals = [gather_sum(0, part) + own[part] for part in range(2)]
    for copy in y_in:
        copy.wait_recv()
    full = jnp.concatenate([cr[d // L, d % L] for d in range(Y * L)], axis=1)
    out[...] = dot(full, wall[...].reshape(-1, HEAD_DIM), nn).astype(bf16)

    for copy in edges + s_c:
        copy.wait_recv()
    everyone = sall[...].reshape(2, 2, BLOCK, HEAD_DIM).astype(f32)
    g_here = [jnp.where(g_seq[j] == me.seq, g_block[j], -1) for j in range(2)]
    for part in range(2):
        ones = []
        for b in range(blocks):
            one = totals[part][b]
            for j in range(2):
                one = one + jnp.where(g_here[j] == b, everyone[j, part], 0.0)
            if b == 0:
                one = one + ehalo[0, part].astype(f32)
            if b == blocks - 1:
                one = one + ehalo[1, part].astype(f32)
            ones.append(one[None])
        totals[part] = jnp.concatenate(ones, axis=0)
    for copy in (v_up, k_down, k_up, v_down):
        copy.wait_recv()
    for part, target in ((0, dk), (1, dv)):
        total = totals[part] + (rm[part].astype(f32) + rp[part].astype(f32))
        target[...] = total.reshape(target.shape).astype(bf16)
    wire.finish()


def settle_kernel(*refs):
    for source, target in zip(refs[:4], refs[4:]):
        target[...] = source[...]


def per_device(dims, queries, keys, values, out_weight, grad_out, pattern):
    Z, PN, Y, L = dims
    me = Place(dims)
    tokens = queries.shape[0]
    blocks = tokens // BLOCK
    entries = 3 * blocks
    rows = out_weight.shape[0]
    piece = 4 * BLOCK // PN
    half = tokens // 2
    block = (BLOCK, HEAD_DIM)
    in_hbm = pl.BlockSpec(memory_space=pltpu.HBM)
    in_vmem = pl.BlockSpec(memory_space=pltpu.VMEM)
    shape = jax.ShapeDtypeStruct

    plane = lax.dynamic_slice(
        pattern, (me.dp, me.z * PN * blocks, 0), (1, PN * blocks, pattern.shape[2])
    )[0]
    wanted = jnp.pad(
        plane[:, 2:].reshape(PN, entries),
        ((0, 0), (WANT, LANES - WANT - entries)),
        constant_values=-1,
    )

    def buffer(*dims, dtype=bf16):
        return pltpu.VMEM(dims, dtype)

    keyed = buffer(blocks, *block)
    slots = buffer(2, PN, CAP, *block)
    pairs = buffer(2, 2, *block)
    whole = buffer(2, blocks, *block)
    small = buffer(piece, HEAD_DIM)
    spread_small = buffer(PN, piece, HEAD_DIM)
    out, dq, dk, dv = pl.pallas_call(
        functools.partial(kernel, dims),
        out_shape=(shape((tokens, HEAD_DIM), bf16),) * 4,
        in_specs=[in_hbm] * 5 + [in_vmem, pl.BlockSpec(memory_space=pltpu.SMEM)],
        out_specs=(in_vmem,) * 4,
        scratch_shapes=[
            buffer(tokens, HEAD_DIM), keyed, keyed, buffer(rows, HEAD_DIM),
            buffer(tokens, HEAD_DIM), buffer(PN, LANES, dtype=jnp.int32),
            pltpu.SMEM((PN, LANES), jnp.int32), pairs,
            keyed, keyed, keyed, keyed, keyed, keyed, slots, slots, slots, slots,
            buffer(8 * PN * CAP, *block), pairs, spread_small,
            spread_small, spread_small, small, buffer(Z, piece, HEAD_DIM), small,
            buffer(Z, rows, HEAD_DIM), buffer(Z, PN, rows, HEAD_DIM),
            buffer(2, Y, L, half, HEAD_DIM), buffer(2, max(Y - 1, 1), L, half, HEAD_DIM),
            buffer(2, L, half, HEAD_DIM), buffer(2, max(L - 1, 1), half, HEAD_DIM),
            buffer(tokens, HEAD_DIM),
            buffer(blocks, 8 * BLOCK, HEAD_DIM), buffer(blocks, 8 * BLOCK, HEAD_DIM),
            buffer(blocks, BLOCK, 8 * BLOCK, dtype=f32), buffer(entries + 1, 2, *block),
            buffer(tokens, HEAD_DIM), buffer(2, blocks, *block, dtype=f32),
            buffer(4, 2, PN, CAP, *block), pairs, spread_small,
            pairs, slots, slots, slots, slots,
            buffer(4, PN * CAP * 16, blocks * 16),
            whole, whole, whole, keyed, keyed, whole, whole,
            spread_small, small, buffer(Z - 1, piece, HEAD_DIM), small, spread_small,
            buffer(Y, L, tokens, HEAD_DIM),
            pltpu.SemaphoreType.DMA((256,)),
            pltpu.SemaphoreType.DMA((256,)),
            pltpu.SemaphoreType.DMA((6,)),
        ],
        compiler_params=pltpu.CompilerParams(
            collective_id=0, has_side_effects=True, vmem_limit_bytes=VMEM_LIMIT
        ),
    )(
        queries, keys.reshape((blocks,) + block), values.reshape((blocks,) + block),
        out_weight, grad_out, wanted, plane[0, :2],
    )
    return pl.pallas_call(
        settle_kernel,
        out_shape=(shape((tokens, HEAD_DIM), bf16),) * 4,
        in_specs=[in_vmem] * 4,
        out_specs=(in_vmem,) * 4,
        compiler_params=pltpu.CompilerParams(vmem_limit_bytes=VMEM_LIMIT),
    )(out, dq, dk, dv)


def solution(mesh, planes=8, lines=4):
    seq, dp = mesh.shape["seq"], mesh.shape["dp"]
    dims = (seq // planes, planes, dp // lines, lines)
    tile = P("seq", "dp")
    return jax.shard_map(
        functools.partial(per_device, dims),
        mesh=mesh,
        in_specs=(tile,) * 5 + (P(),),
        out_specs=(tile,) * 4,
        check_vma=False,
    )
```
